32 devices in a mesh: img: 4 (over z), ha: 8 (over y, x, core).
Axes of the slice: x: 2, y: 2, z: 4, core: 2. Of those that a mesh axis runs over, the one named last changes fastest.
Arguments:
- maps_wide: float32 [4, 64, 96, 512], P('img', 'ha'), may hold values from -12 to 12
- maps_tall: float32 [4, 96, 64, 512], P('img', 'ha'), may hold values from -12 to 12
- upstream_wide: float32 [4, 64, 96, 512], P('img', 'ha'), may hold values from -6 to 6
- upstream_tall: float32 [4, 96, 64, 512], P('img', 'ha'), may hold values from -6 to 6
- near_weight: float32 [1, 3, 3, 128, 128], P(None, None, None, None, 'ha'), may hold values from -0.1875 to 0.1875
- near_moment: float32 [1, 3, 3, 128, 128], P(None, None, None, None, 'ha'), may hold values from -640 to 640
- near_average: float32 [1, 3, 3, 128, 128], P(None, None, None, None, 'ha'), may hold values from -0.1875 to 0.1875
- inward_weight: float32 [1, 3, 3, 384, 128], P(None, None, None, None, 'ha'), may hold values from -0.109375 to 0.109375
- inward_moment: float32 [1, 3, 3, 384, 128], P(None, None, None, None, 'ha'), may hold values from -640 to 640
- inward_average: float32 [1, 3, 3, 384, 128], P(None, None, None, None, 'ha'), may hold values from -0.109375 to 0.109375
- outward_weight: float32 [1, 3, 3, 128, 384], P(None, None, None, None, 'ha'), may hold values from -0.1875 to 0.1875
- outward_moment: float32 [1, 3, 3, 128, 384], P(None, None, None, None, 'ha'), may hold values from -640 to 640
- outward_average: float32 [1, 3, 3, 128, 384], P(None, None, None, None, 'ha'), may hold values from -0.1875 to 0.1875
- squeeze_weight: float32 [1, 384, 192], P(None, None, 'ha'), may hold values from -0.3125 to 0.3125
- squeeze_moment: float32 [1, 384, 192], P(None, None, 'ha'), may hold values from -640 to 640
- squeeze_average: float32 [1, 384, 192], P(None, None, 'ha'), may hold values from -0.3125 to 0.3125
- fourier_weight: float32 [1, 384, 384], P(None, None, 'ha'), may hold values from -0.3125 to 0.3125
- fourier_moment: float32 [1, 384, 384], P(None, None, 'ha'), may hold values from -640 to 640
- fourier_average: float32 [1, 384, 384], P(None, None, 'ha'), may hold values from -0.3125 to 0.3125
- expand_weight: float32 [1, 192, 384], P(None, None, 'ha'), may hold values from -0.4375 to 0.4375
- expand_moment: float32 [1, 192, 384], P(None, None, 'ha'), may hold values from -640 to 640
- expand_average: float32 [1, 192, 384], P(None, None, 'ha'), may hold values from -0.4375 to 0.4375
- norm_weight: float32 [1, 2, 1088], P(None, None, 'ha'), may hold values from -1.35 to 1.5
- norm_moment: float32 [1, 2, 1088], P(None, None, 'ha'), may hold values from -640 to 640
- norm_average: float32 [1, 2, 1088], P(None, None, 'ha'), may hold values from -1.35 to 1.5
Outputs:
- block_wide: float32 [4, 64, 96, 512], P('img', 'ha')
- block_tall: float32 [4, 96, 64, 512], P('img', 'ha')
- back_wide: float32 [4, 64, 96, 512], P('img', 'ha')
- back_tall: float32 [4, 96, 64, 512], P('img', 'ha')
- rerun_wide: float32 [4, 64, 96, 512], P('img', 'ha')
- rerun_tall: float32 [4, 96, 64, 512], P('img', 'ha')
- near_updated: float32 [1, 3, 3, 128, 128], P(None, None, None, None, 'ha')
- near_velocity: float32 [1, 3, 3, 128, 128], P(None, None, None, None, 'ha')
- near_smoothed: float32 [1, 3, 3, 128, 128], P(None, None, None, None, 'ha')
- near_half: bfloat16 [1, 3, 3, 128, 128], P(None, None, None, None, 'ha')
- inward_updated: float32 [1, 3, 3, 384, 128], P(None, None, None, None, 'ha')
- inward_velocity: float32 [1, 3, 3, 384, 128], P(None, None, None, None, 'ha')
- inward_smoothed: float32 [1, 3, 3, 384, 128], P(None, None, None, None, 'ha')
- inward_half: bfloat16 [1, 3, 3, 384, 128], P(None, None, None, None, 'ha')
- outward_updated: float32 [1, 3, 3, 128, 384], P(None, None, None, None, 'ha')
- outward_velocity: float32 [1, 3, 3, 128, 384], P(None, None, None, None, 'ha')
- outward_smoothed: float32 [1, 3, 3, 128, 384], P(None, None, None, None, 'ha')
- outward_half: bfloat16 [1, 3, 3, 128, 384], P(None, None, None, None, 'ha')
- squeeze_updated: float32 [1, 384, 192], P(None, None, 'ha')
- squeeze_velocity: float32 [1, 384, 192], P(None, None, 'ha')
- squeeze_smoothed: float32 [1, 384, 192], P(None, None, 'ha')
- squeeze_half: bfloat16 [1, 384, 192], P(None, None, 'ha')
- fourier_updated: float32 [1, 384, 384], P(None, None, 'ha')
- fourier_velocity: float32 [1, 384, 384], P(None, None, 'ha')
- fourier_smoothed: float32 [1, 384, 384], P(None, None, 'ha')
- fourier_half: bfloat16 [1, 384, 384], P(None, None, 'ha')
- expand_updated: float32 [1, 192, 384], P(None, None, 'ha')
- expand_velocity: float32 [1, 192, 384], P(None, None, 'ha')
- expand_smoothed: float32 [1, 192, 384], P(None, None, 'ha')
- expand_half: bfloat16 [1, 192, 384], P(None, None, 'ha')
- norm_updated: float32 [1, 2, 1088], P(None, None, 'ha')
- norm_velocity: float32 [1, 2, 1088], P(None, None, 'ha')
- norm_smoothed: float32 [1, 2, 1088], P(None, None, 'ha')
- norm_half: bfloat16 [1, 2, 1088], P(None, None, 'ha')
The draws below stay inside these ranges and needn't reach their ends.
All inputs are finite; a program needn't handle non-finite values.
Results may differ from the reference program's by a relative error of at most 0.001.
Values sent between devices are 32-bit elements; how exact they have to be, the bound alone decides.
A program may use at most 192 MiB of HBM per device.

```python
import jax
import jax.numpy as jnp
from jax import lax

CL = 128
CG = 384
CH = 192
NP = 1088
IMGS = 4
H_WIDE = 64
W_WIDE = 96
H_TALL = 96
W_TALL = 64
LAYERS = 1
STEP = 6


def rising_scale(images, height, growth):
    image_part = jnp.arange(images, dtype=jnp.float32)[:, None] / (images - 1)
    row_part = jnp.arange(height, dtype=jnp.float32)[None, :] / (height - 1)
    return growth ** (0.5 * (image_part + row_part))


def gain_bias_table(key, gain_low, gain_high, bias_scale):
    gain_key, bias_key = jax.random.split(key)
    gains = jax.random.uniform(gain_key, (LAYERS, 1, NP), jnp.float32, gain_low, gain_high)
    biases = bias_scale * jax.random.truncated_normal(bias_key, -3.0, 3.0, (LAYERS, 1, NP), jnp.float32)
    return jnp.concatenate([gains, biases], 1)


def draw_maps_wide(key, part):
    key = jax.random.fold_in(key, 3)
    noise_key = jax.random.fold_in(key, 0)
    full_shape = (IMGS, H_WIDE, W_WIDE, CL + CG)
    values = jax.random.truncated_normal(noise_key, -4.0, 4.0, full_shape, jnp.float32)
    profile = rising_scale(IMGS, H_WIDE, 3.0)
    return values * profile[:, :, None, None]


def draw_maps_tall(key, part):
    key = jax.random.fold_in(key, 4)
    noise_key = jax.random.fold_in(key, 0)
    full_shape = (IMGS, H_TALL, W_TALL, CL + CG)
    values = jax.random.truncated_normal(noise_key, -4.0, 4.0, full_shape, jnp.float32)
    profile = rising_scale(IMGS, H_TALL, 3.0)
    return values * profile[:, :, None, None]


def draw_norm_weight(key, part):
    key = jax.random.fold_in(key, 5)
    return gain_bias_table(key, 0.7, 1.3, 0.3)


def draw_norm_average(key, part):
    key = jax.random.fold_in(key, 7)
    return gain_bias_table(key, 0.7, 1.3, 0.3)


def level_of(rng, dims, cuts, smallest, largest):
    level = 1.0
    for axis_at, parts in cuts:
        heights = jax.random.uniform(jax.random.fold_in(jax.random.fold_in(rng, 6), axis_at), (parts,), jnp.float32, smallest / len(cuts), largest / len(cuts))
        level = level * jnp.repeat(jnp.exp(heights), dims[axis_at] // parts).reshape((-1,) + (1,) * (len(dims) - 1 - axis_at))
    return level


def centred(stream_key, dims, spread, bound, pieces=(), kind=jnp.bfloat16):
    drawn = jax.random.normal(stream_key, dims, jnp.float32) * spread
    if len(pieces) > 0:
        drawn = level_of(stream_key, dims, pieces, -0.22, 0.18) * drawn
    return jnp.clip(drawn, min=-bound, max=bound).astype(kind)


def setup_inputs(seed: int = 0) -> dict:
    seeds = jax.random.split(jax.random.key(seed), 26)
    return {
        "maps_wide": draw_maps_wide(jax.random.fold_in(seeds[25], 71), 0),
        "maps_tall": draw_maps_tall(jax.random.fold_in(seeds[25], 71), 0),
        "upstream_wide": centred(seeds[2], (IMGS, H_WIDE, W_WIDE, CL + CG), 1.0, 6.0, ((0, 4), (1, 8)), jnp.float32),
        "upstream_tall": centred(seeds[3], (IMGS, H_TALL, W_TALL, CL + CG), 1.0, 6.0, ((0, 4), (1, 8)), jnp.float32),
        "near_weight": centred(seeds[4], (LAYERS, 3, 3, CL, CL), (9 * CL) ** -0.5, 0.1875, ((4, 8),), jnp.float32),
        "near_moment": centred(seeds[5], (LAYERS, 3, 3, CL, CL), (0.5 * (IMGS * (H_WIDE * W_WIDE + H_TALL * W_TALL)) ** 0.5), 640.0, ((4, 8),), jnp.float32),
        "near_average": centred(seeds[6], (LAYERS, 3, 3, CL, CL), (9 * CL) ** -0.5, 0.1875, ((4, 8),), jnp.float32),
        "inward_weight": centred(seeds[7], (LAYERS, 3, 3, CG, CL), (9 * CG) ** -0.5, 0.109375, ((4, 8),), jnp.float32),
        "inward_moment": centred(seeds[8], (LAYERS, 3, 3, CG, CL), (0.5 * (IMGS * (H_WIDE * W_WIDE + H_TALL * W_TALL)) ** 0.5), 640.0, ((4, 8),), jnp.float32),
        "inward_average": centred(seeds[9], (LAYERS, 3, 3, CG, CL), (9 * CG) ** -0.5, 0.109375, ((4, 8),), jnp.float32),
        "outward_weight": centred(seeds[10], (LAYERS, 3, 3, CL, CG), (9 * CL) ** -0.5, 0.1875, ((4, 8),), jnp.float32),
        "outward_moment": centred(seeds[11], (LAYERS, 3, 3, CL, CG), (0.5 * (IMGS * (H_WIDE * W_WIDE + H_TALL * W_TALL)) ** 0.5), 640.0, ((4, 8),), jnp.float32),
        "outward_average": centred(seeds[12], (LAYERS, 3, 3, CL, CG), (9 * CL) ** -0.5, 0.1875, ((4, 8),), jnp.float32),
        "squeeze_weight": centred(seeds[13], (LAYERS, CG, CH), CG ** -0.5, 0.3125, ((2, 8),), jnp.float32),
        "squeeze_moment": centred(seeds[14], (LAYERS, CG, CH), (0.5 * (IMGS * (H_WIDE * W_WIDE + H_TALL * W_TALL)) ** 0.5), 640.0, ((2, 8),), jnp.float32),
        "squeeze_average": centred(seeds[15], (LAYERS, CG, CH), CG ** -0.5, 0.3125, ((2, 8),), jnp.float32),
        "fourier_weight": centred(seeds[16], (LAYERS, CG, CG), CG ** -0.5, 0.3125, ((2, 8),), jnp.float32),
        "fourier_moment": centred(seeds[17], (LAYERS, CG, CG), (0.5 * (IMGS * (H_WIDE * W_WIDE + H_TALL * W_TALL)) ** 0.5), 640.0, ((2, 8),), jnp.float32),
        "fourier_average": centred(seeds[18], (LAYERS, CG, CG), CG ** -0.5, 0.3125, ((2, 8),), jnp.float32),
        "expand_weight": centred(seeds[19], (LAYERS, CH, CG), CH ** -0.5, 0.4375, ((2, 8),), jnp.float32),
        "expand_moment": centred(seeds[20], (LAYERS, CH, CG), (0.5 * (IMGS * (H_WIDE * W_WIDE + H_TALL * W_TALL)) ** 0.5), 640.0, ((2, 8),), jnp.float32),
        "expand_average": centred(seeds[21], (LAYERS, CH, CG), CH ** -0.5, 0.4375, ((2, 8),), jnp.float32),
        "norm_weight": draw_norm_weight(jax.random.fold_in(seeds[25], 71), 0),
        "norm_moment": centred(seeds[23], (LAYERS, 2, NP), (0.5 * (IMGS * (H_WIDE * W_WIDE + H_TALL * W_TALL)) ** 0.5), 640.0, ((2, 8),), jnp.float32),
        "norm_average": draw_norm_average(jax.random.fold_in(seeds[25], 71), 0),
    }


@jax.custom_vjp
def low(v):
    return lax.optimization_barrier(v.astype(jnp.bfloat16)).astype(jnp.float32)

@jax.custom_vjp
def low_back(v):
    return v

def low_keep(v):
    return (low(v), None)

def low_pass(kept, grad):
    return (grad,)

def back_keep(v):
    return (v, None)

def back_low(kept, grad):
    return (low(grad),)
low.defvjp(low_keep, low_pass)
low_back.defvjp(back_keep, back_low)
epsilon = 1e-05
learn_rate = 3e-05
momentum = 0.5
highest = lax.Precision.HIGHEST

def conv_same(current, kernel):
    return lax.conv_general_dilated(current, kernel, (1, 1), ((1, 1), (1, 1)), dimension_numbers=('NHWC', 'HWIO', 'NHWC'), precision=highest)

def batch_norm(current, gain_vec, offset):
    center = lax.optimization_barrier(jnp.mean(current, (0, 1, 2)))
    variance = lax.optimization_barrier(jnp.mean(current * current, (0, 1, 2))) - center * center
    return (current - center) * lax.rsqrt(variance + epsilon) * gain_vec + offset

def ffc_layer(current, near_kernel, inward_kernel, outward_kernel, squeeze_matrix, fourier_matrix, expand_matrix, norm_table):
    local_width = near_kernel.shape[2]
    half_width = squeeze_matrix.shape[1]
    total_width = current.shape[3]
    height = current.shape[1]
    width = current.shape[2]
    local_in = current[..., :local_width]
    global_in = current[..., local_width:]
    pre_local = conv_same(local_in, near_kernel) + conv_same(global_in, inward_kernel)
    cross = conv_same(local_in, outward_kernel)
    squeezed = jnp.einsum('nhwc,cd->nhwd', global_in, squeeze_matrix, precision=highest)
    stop_in = total_width + half_width
    active = jax.nn.silu(batch_norm(squeezed, norm_table[0, total_width:stop_in], norm_table[1, total_width:stop_in]))
    spectrum = jnp.fft.rfft2(active, axes=(1, 2), norm='ortho')
    stacked = jnp.concatenate([jnp.real(spectrum), jnp.imag(spectrum)], -1)
    mixed = jnp.einsum('nhkc,cd->nhkd', stacked, fourier_matrix, precision=highest)
    excited = jax.nn.silu(batch_norm(mixed, norm_table[0, stop_in:], norm_table[1, stop_in:]))
    restored = jnp.fft.irfft2(lax.complex(excited[..., :half_width], excited[..., half_width:]), s=(height, width), axes=(1, 2), norm='ortho')
    pre_global = cross + jnp.einsum('nhwc,cd->nhwd', active + restored, expand_matrix, precision=highest)
    joined = jnp.concatenate([pre_local, pre_global], -1)
    return jax.nn.silu(batch_norm(joined, norm_table[0, :total_width], norm_table[1, :total_width]))

def ffc_block(map_batch, weights):
    current = map_batch
    for layer_index in range(LAYERS):
        current = jax.checkpoint(ffc_layer)(current, *[piece[layer_index] for piece in weights])
    return map_batch + current

def reference(maps_wide, maps_tall, upstream_wide, upstream_tall, near_weight, near_moment, near_average, inward_weight, inward_moment, inward_average, outward_weight, outward_moment, outward_average, squeeze_weight, squeeze_moment, squeeze_average, fourier_weight, fourier_moment, fourier_average, expand_weight, expand_moment, expand_average, norm_weight, norm_moment, norm_average):
    weights = (near_weight, inward_weight, outward_weight, squeeze_weight, fourier_weight, expand_weight, norm_weight)
    moments = (near_moment, inward_moment, outward_moment, squeeze_moment, fourier_moment, expand_moment, norm_moment)
    averages = (near_average, inward_average, outward_average, squeeze_average, fourier_average, expand_average, norm_average)

    def both_buckets(wide_in, tall_in, params):
        return (ffc_block(wide_in, params), ffc_block(tall_in, params))
    (block_wide, block_tall), pullback = jax.vjp(both_buckets, maps_wide, maps_tall, weights)
    back_wide, back_tall, grads = pullback((upstream_wide, upstream_tall))
    decay = min(0.5, (1.0 + STEP) / (10.0 + STEP))
    velocity = tuple((momentum * old_moment + gradient for old_moment, gradient in zip(moments, grads)))
    updated = tuple((weight_old - learn_rate * (gradient + momentum * moving) for weight_old, gradient, moving in zip(weights, grads, velocity)))
    smoothed = tuple((decay * average + (1.0 - decay) * weight_new for average, weight_new in zip(averages, updated)))
    halves = tuple((weight_new.astype(jnp.bfloat16) for weight_new in updated))
    rerun_wide = ffc_block(maps_wide, updated)
    rerun_tall = ffc_block(maps_tall, updated)
    return (block_wide, block_tall, back_wide, back_tall, rerun_wide, rerun_tall, updated[0], velocity[0], smoothed[0], halves[0], updated[1], velocity[1], smoothed[1], halves[1], updated[2], velocity[2], smoothed[2], halves[2], updated[3], velocity[3], smoothed[3], halves[3], updated[4], velocity[4], smoothed[4], halves[4], updated[5], velocity[5], smoothed[5], halves[5], updated[6], velocity[6], smoothed[6], halves[6])
```

```python
import functools
import math

import jax
import jax.numpy as jnp
import numpy as np
from jax import lax
from jax.experimental import pallas as pl
from jax.experimental.pallas import tpu as pltpu
from jax.sharding import PartitionSpec as P

STEP = 6

epsilon = 1e-05
learn_rate = 3e-05
momentum = 0.5

f32 = jnp.float32
bf16 = jnp.bfloat16
MESH = pl.DeviceIdType.MESH
VMEM_LIMIT = 60 * 1024 * 1024

NN = (((1,), (0,)), ((), ()))
NT = (((1,), (1,)), ((), ()))
TN = (((0,), (0,)), ((), ()))


def dg(left, right, dims):
    return lax.dot_general(left, right, dims, preferred_element_type=f32)


def split(value):
    high = value.astype(bf16)
    return high, (value - high.astype(f32)).astype(bf16)


def dot3(left, right, dims):
    lh, ll = left
    rh, rl = right
    return dg(lh, rh, dims) + dg(ll, rh, dims) + dg(lh, rl, dims)


def sigmoid(v):
    return 1.0 / (1.0 + jnp.exp(-v))


def pad_to(n, m):
    return -(-n // m) * m


def chunks(count, step, body, carry):
    def run(i, carry):
        return body(pl.multiple_of(i * step, 8), carry)

    return lax.fori_loop(0, count // step, run, carry)


class Bucket:
    def __init__(self, rows, width, group):
        self.R, self.W, self.A = rows, width, group
        self.H = rows * group
        self.N = rows * width
        self.nb = -(-(width // 2) // group)
        self.Cp = pad_to(self.nb * rows, 8)
        self.Q = (self.nb + 1) * self.H
        self.MB = max(r * width for r in range(1, rows + 1) if rows % r == 0 and r * width <= 384)


def hi_lo(table):
    table = np.asarray(table, np.float64)
    high = table.astype(np.float32).astype(jnp.bfloat16)
    low = (table - high.astype(np.float64)).astype(np.float32).astype(jnp.bfloat16)
    return np.stack([high, low])


def tables_of(bk):
    A, nb, W, H, R = bk.A, bk.nb, bk.W, bk.H, bk.R
    row = np.zeros((2, nb, A, W))
    w = np.arange(W)
    for b in range(nb):
        for d in range(A):
            j = d * nb + b
            if j == 0:
                row[0, b, d] = 1.0
                row[1, b, d] = np.cos(math.pi * w)
            elif 2 * j < W:
                row[0, b, d] = np.cos(2 * math.pi * (j * w % W) / W)
                row[1, b, d] = -np.sin(2 * math.pi * (j * w % W) / W)
    row = row.reshape(2 * nb * A, W) / math.sqrt(W)
    k = np.arange(H)[:, None]
    h = np.array([s * R + r for r in range(R) for s in range(A)])[None, :]
    phase = 2 * math.pi * (k * h % H) / H
    cos, sin = np.cos(phase) / math.sqrt(H), np.sin(phase) / math.sqrt(H)
    none = np.zeros_like(cos)
    plain = np.block([[cos, sin], [-sin, cos]])
    packed = np.block([[cos, none], [-sin, none], [none, cos], [none, -sin]])
    other = np.concatenate([plain, np.zeros_like(plain)], 0)
    first = np.stack([hi_lo(packed), hi_lo(other)])
    return (
        hi_lo(row),
        hi_lo(row.T),
        hi_lo(plain),
        hi_lo(plain.T),
        first,
        np.swapaxes(first, 2, 3),
    )


class Names:
    def __getattr__(self, name):
        return name


n = Names()
TABLES = (n.row, n.rowT, n.col, n.colT, n.col0, n.col0T)
SPECTRA = (n.sendA, n.recvA, n.sendB, n.recvB)


def for_both(*names):
    return [name + str(q) for q in (0, 1) for name in names]


class View:
    def __init__(self, refs, q):
        self.refs, self.q = refs, q

    def __getattr__(self, name):
        return getattr(self.refs, name + str(self.q))


class Fields:
    pass


def take(names, refs):
    out = Fields()
    for name, ref in zip(names, refs):
        setattr(out, name, ref)
    return out


class Comm:
    def __init__(self, A, B):
        self.A, self.B = A, B
        self.a = lax.axis_index("ha")
        self.z = lax.axis_index("img")
        self.pending = []

    def enter(self):
        bar = pltpu.get_barrier_semaphore()
        for d in range(1, self.A):
            pl.semaphore_signal(
                bar, inc=1, device_id=(self.z, lax.rem(self.a + d, self.A)), device_id_type=MESH
            )
        for d in range(1, self.B):
            pl.semaphore_signal(
                bar, inc=1, device_id=(lax.rem(self.z + d, self.B), self.a), device_id_type=MESH
            )

    def entered(self):
        pl.semaphore_wait(pltpu.get_barrier_semaphore(), self.A + self.B - 2)

    def send(self, src, dst, ssem, rsem, ha=None, img=None):
        copy = pltpu.make_async_remote_copy(
            src,
            dst,
            ssem,
            rsem,
            device_id=(self.z if img is None else img, self.a if ha is None else ha),
            device_id_type=MESH,
        )
        copy.start()
        self.pending.append(copy)
        return copy

    def sent(self, copies):
        for copy in copies:
            copy.wait_send()
            self.pending = [other for other in self.pending if other is not copy]

    def finish(self):
        for copy in self.pending:
            copy.wait_send()

    def sum_start(self, f, k, q, sums):
        i = 2 * k + q
        for part in (0, 1):
            value = jnp.sum(sums[part], 0, keepdims=True)
            for t in range(-(-value.shape[1] // 128)):
                piece = value[:, 128 * t : 128 * (t + 1)]
                f.sum_src[i, 4 * part + t : 4 * part + t + 1, : piece.shape[1]] = piece
        f.sum_a[i, self.a] = f.sum_src[i]
        return [
            self.send(
                f.sum_src.at[i],
                f.sum_a.at[i, self.a],
                f.sum_as.at[i, d],
                f.sum_ar.at[i, d],
                ha=lax.rem(self.a + d, self.A),
            )
            for d in range(1, self.A)
        ]

    def sum_cross(self, f, k, q, copies):
        i = 2 * k + q
        for copy in copies:
            copy.wait_recv()
        total = f.sum_a[i, 0]
        for d in range(1, self.A):
            total = total + f.sum_a[i, d]
        f.sum_z[i, self.z] = total
        return [
            self.send(
                f.sum_z.at[i, self.z],
                f.sum_z.at[i, self.z],
                f.sum_zs.at[i, d],
                f.sum_zr.at[i, d],
                img=lax.rem(self.z + d, self.B),
            )
            for d in range(1, self.B)
        ]

    def sum_end(self, f, k, q, copies):
        i = 2 * k + q
        for copy in copies:
            copy.wait_recv()
        total = f.sum_z[i, 0]
        for d in range(1, self.B):
            total = total + f.sum_z[i, d]
        f.sum_out[i] = total

    def swap_start(self, src, dst, ssem, rsem, rows):
        copies = []
        for d in range(1, self.A):
            t = lax.rem(self.a + d, self.A)
            copies.append(
                self.send(
                    src.at[:, pl.ds(pl.multiple_of(t * rows, 8), rows)],
                    dst.at[:, pl.ds(pl.multiple_of(self.a * rows, 8), rows)],
                    ssem.at[d],
                    rsem.at[d],
                    ha=t,
                )
            )
        mine = pl.ds(pl.multiple_of(self.a * rows, 8), rows)
        dst[:, mine, :] = src[:, mine, :]
        return copies

    def swap_end(self, copies):
        for copy in copies:
            copy.wait_recv()

    def halo_start(self, low_row, high_row, dst, ssem, rsem):
        up = lax.rem(self.a + self.A - 1, self.A)
        down = lax.rem(self.a + 1, self.A)
        return [
            self.send(low_row, dst.at[1], ssem.at[0], rsem.at[0], ha=up),
            self.send(high_row, dst.at[0], ssem.at[1], rsem.at[1], ha=down),
        ]


def column_sum(value):
    rows, width = value.shape
    return jnp.sum(value.reshape(rows // 8, 8, width), 0)


def no_sums(width):
    return jnp.zeros((8, width), f32), jnp.zeros((8, width), f32)


def totals(ref, k, q, width):
    i = 2 * k + q
    return [
        jnp.concatenate([ref[i, t : t + 1, :] for t in range(first, first + 4)], 1)[:, :width]
        for first in (0, 4)
    ]


def norm_rows(ref, k, q, width, count):
    total, square = totals(ref, k, q, width)
    center = total * (1.0 / count)
    variance = square * (1.0 / count) - center * center
    return center, lax.rsqrt(variance + epsilon)


def row_transform(bk, table, source, send):
    nbA = bk.nb * bk.A
    tab = (table[0], table[1])
    for h in range(bk.R):
        out = dot3(tab, split(source(h)), NN)
        out = jnp.concatenate([out[:nbA], out[nbA:]], 1)
        for b in range(bk.nb):
            put_strided(send, b * bk.R + h, bk.A, bk.Cp, out[b * bk.A : (b + 1) * bk.A])


def row_back(bk, table, recv, h):
    parts = [get_strided(recv, b * bk.R + h, bk.A, bk.Cp) for b in range(bk.nb)]
    block = jnp.concatenate(parts, 0) if len(parts) > 1 else parts[0]
    half = block.shape[1] // 2
    block = jnp.concatenate([block[:, :half], block[:, half:]], 0)
    return dot3((table[0], table[1]), split(block), NN)


def put_strided(ref, start, count, stride, value):
    for t in range(ref.shape[0]):
        ref[t, pl.ds(start, count, stride=stride), :] = value[:, 128 * t : 128 * (t + 1)]


def get_strided(ref, start, count, stride):
    return jnp.concatenate(
        [ref[t, pl.ds(start, count, stride=stride), :] for t in range(ref.shape[0])], 1
    )


def first_table(ref, other):
    return ref[other, 0], ref[other, 1]


def col_transform(bk, f_col, f_col0, other, recv, put):
    H = bk.H
    for b in range(bk.nb):
        block = jnp.concatenate(
            [get_strided(recv, b * bk.R + h, bk.A, bk.Cp) for h in range(bk.R)], 0
        )
        half = block.shape[1] // 2
        block = split(jnp.concatenate([block[:, :half], block[:, half:]], 0))
        if b == 0:
            out = dot3(first_table(f_col0, other), block, NN)
            put(bk.nb, jnp.concatenate([out[2 * H : 3 * H], out[3 * H :]], 1))
        else:
            out = dot3((f_col[0], f_col[1]), block, NN)
        put(b, jnp.concatenate([out[:H], out[H : 2 * H]], 1))


def col_back(bk, f_colT, f_col0T, other, get, scale, send):
    H = bk.H

    def halves(value):
        half = value.shape[1] // 2
        return [value[:, :half], value[:, half:]]

    for b in range(bk.nb):
        if b == 0:
            block = jnp.concatenate(halves(get(0)) + halves(get(bk.nb)), 0)
            out = dot3(first_table(f_col0T, other), split(block), NN)
        else:
            out = dot3((f_colT[0], f_colT[1]), split(jnp.concatenate(halves(get(b)), 0)), NN)
        out = jnp.concatenate([out[:H], out[H:]], 1)
        out = scale(b, out)
        for h in range(bk.R):
            put_strided(send, b * bk.R + h, bk.A, bk.Cp, out[h * bk.A : (h + 1) * bk.A])


def conv_forward(bk, zh, zl, knh, knl, koh, kol, out):
    MB, W = bk.MB, bk.W
    col = lax.broadcasted_iota(jnp.int32, (MB, 1), 0) % W

    def combine(value, n):
        low = jnp.where(col == 0, 0.0, pltpu.roll(value[:, :n], 1, 0))
        high = jnp.where(col == W - 1, 0.0, pltpu.roll(value[:, 2 * n :], MB - 1, 0))
        return low + value[:, n : 2 * n] + high

    def body(i, carry):
        r = pl.multiple_of(i * MB, 32)
        total = None
        for a in range(3):
            left = (zh[pl.ds(r + a * W, MB), :], zl[pl.ds(r + a * W, MB), :])
            n = knh.shape[2]
            right = (knh[:, a].reshape(3 * n, -1), knl[:, a].reshape(3 * n, -1))
            part = dot3(left, right, NT)
            total = part if total is None else total + part
        CL = knh.shape[2]
        out[pl.ds(r, MB), :CL] = combine(total, CL)
        left = tuple(
            jnp.concatenate([z[pl.ds(r + a * W, MB), :CL] for a in range(3)], 1) for z in (zh, zl)
        )
        cross = dot3(left, (koh[...], kol[...]), NT)
        out[pl.ds(r, MB), CL:] = combine(cross, koh.shape[0] // 3)
        return carry

    lax.fori_loop(0, bk.N // MB, body, 0)


GATHERED = (n.sq, n.nm, n.fo, n.ex, n.near, n.inw, n.outw)


class Loader:
    def __init__(self, sems):
        self.sems, self.copies = sems, {}

    def start(self, name, src, dst):
        copy = pltpu.make_async_copy(src, dst, self.sems.at[len(self.copies)])
        copy.start()
        self.copies[name] = copy

    def wait(self, *names):
        for name in names:
            self.copies[name].wait()


def whole_of(name):
    return n.g_ + name


def far_of(name):
    return name + n._hbm


def gather_first(c, f, name, i):
    nc = c.A // 2
    chip, core = c.a // 2, c.a % 2
    shard, whole = getattr(f, name), getattr(f, whole_of(name))
    whole[c.a] = shard[...]
    copies = [c.send(shard, whole.at[c.a], f.g1s.at[i, 0], f.g1r.at[i, 0], ha=2 * chip + 1 - core)]
    for d in range(1, nc):
        t = 2 * lax.rem(chip + d, nc) + core
        copies.append(c.send(shard, whole.at[c.a], f.g1s.at[i, d], f.g1r.at[i, d], ha=t))
    return copies


def gather_second(c, f, name, i, copies):
    nc = c.A // 2
    chip, core = c.a // 2, c.a % 2
    whole = getattr(f, whole_of(name))
    out = [copies[0]]
    for d in range(1, nc):
        copies[d].wait_recv()
        s = 2 * lax.rem(chip + nc - d, nc) + core
        out.append(
            c.send(whole.at[s], whole.at[s], f.g2s.at[i, d], f.g2r.at[i, d], ha=2 * chip + 1 - core)
        )
    return out


def gather_end(copies):
    for copy in copies:
        copy.wait_recv()


def forward_names():
    ins = [n.maps0, n.maps1, n.near, n.inw, n.outw, n.sq, n.fo, n.ex, n.nm] + for_both(*TABLES)
    outs = [n.joined0, n.joined1, n.sum_out, n.norms]
    kept = for_both(n.u, n.spec, n.mixed, n.s, n.halo)
    kept += [n.knh, n.knl, n.koh, n.kol, n.g_sq, n.g_fo, n.g_ex]
    scratch = [n.g_nm, n.g_near, n.g_inw, n.g_outw, n.ld]
    scratch += [n.sum_src, n.sum_a, n.sum_z, n.sum_as, n.sum_ar, n.sum_zs, n.sum_zr]
    scratch += [n.g1s, n.g1r, n.g2s, n.g2r, n.hs, n.hr, n.ws, n.wr]
    scratch += for_both(n.zh, n.zl, n.act, *SPECTRA)
    return ins, outs, kept, scratch


def forward_kernel(bks, A, B, sizes, save, *refs):
    ins, outs, kept, scratch = forward_names()
    names = ins + outs + ([far_of(k) for k in kept] if save else []) + kept + scratch
    f = take(names, refs)
    CL, CG, CH, NPd = sizes
    CT = CL + CG
    c = Comm(A, B)
    c.enter()
    other = jnp.minimum(c.a, 1)
    once = jnp.where(c.a == 0, 1.0, 2.0)
    cells = [B * bk.H * bk.W for bk in bks]
    freqs = [B * bk.H * (bk.W // 2 + 1) for bk in bks]
    views = [View(f, 0), View(f, 1)]
    both = (0, 1)
    keeper = Loader(f.ld)

    def keep(*which):
        if save:
            for k in which:
                keeper.start(k, getattr(f, k), getattr(f, far_of(k)))

    for q in both:
        bk, g = bks[q], views[q]

        def body(r, carry, bk=bk, g=g):
            src = pl.multiple_of(r * bk.W, bk.W)
            high, low = split(g.maps[pl.ds(src, bk.W), :])
            g.zh[pl.ds(src + bk.W, bk.W), :] = high
            g.zl[pl.ds(src + bk.W, bk.W), :] = low
            return carry

        lax.fori_loop(0, bk.R, body, 0)
    f.sum_src[...] = jnp.zeros_like(f.sum_src)
    c.entered()
    moving = {}
    for i in range(2):
        moving[i] = gather_first(c, f, GATHERED[i], i)
    halos = []
    for q in both:
        bk, g = bks[q], views[q]
        halos += c.halo_start(
            g.maps.at[pl.ds(0, bk.W)],
            g.maps.at[pl.ds(bk.N - bk.W, bk.W)],
            g.halo,
            f.hs.at[q],
            f.hr.at[q],
        )
    for i in (2, 3):
        moving[i] = gather_first(c, f, GATHERED[i], i)
    for i in range(2):
        moving[i] = gather_second(c, f, GATHERED[i], i, moving[i])
    for i in range(2):
        gather_end(moving[i])

    wsq = split(f.g_sq[...].reshape(CH, CG))
    keep(n.g_sq)
    adding = [None, None]
    for q in both:
        bk, g = bks[q], views[q]

        def body(r, carry, bk=bk, g=g):
            at = pl.multiple_of(r + bk.W, 32)
            value = dot3((g.zh[pl.ds(at, bk.MB), CL:], g.zl[pl.ds(at, bk.MB), CL:]), wsq, NT)
            g.s[pl.ds(r, bk.MB), :] = value
            return carry[0] + column_sum(value), carry[1] + column_sum(value * value)

        adding[q] = c.sum_start(f, 0, q, chunks(bk.N, bk.MB, body, no_sums(CH)))
        keep(n.s + str(q))
    for i in (4, 5, 6):
        moving[i] = gather_first(c, f, GATHERED[i], i)

    piece = f.g_nm.shape[2]
    span = pad_to(NPd * A, 128) + 128
    norms = None
    for d in range(A):
        part = jnp.concatenate([f.g_nm[d], jnp.zeros((8, span - piece), f32)], 1)
        if d:
            part = pltpu.roll(part, NPd * d, 1)
        norms = part if norms is None else norms + part
    f.norms[0] = norms[:, :CT]
    f.norms[1] = pltpu.roll(norms, span - CT, 1)[:, :CT]
    f.norms[2] = pltpu.roll(norms, span - CT - CH, 1)[:, :CT]

    for q in both:
        adding[q] = c.sum_cross(f, 0, q, adding[q])

    swaps = [None, None]
    for q in both:
        bk, g = bks[q], views[q]
        c.sum_end(f, 0, q, adding[q])
        center, inverse = norm_rows(f.sum_out, 0, q, CH, cells[q])

        def source(h, bk=bk, g=g, center=center, inverse=inverse):
            rows = slice(h * bk.W, (h + 1) * bk.W)
            v = (g.s[rows, :] - center) * inverse * f.norms[1, 0:1, :CH] + f.norms[1, 1:2, :CH]
            value = v * sigmoid(v)
            g.act[rows, :] = value
            return value

        row_transform(bk, g.row, source, g.sendA)
        swaps[q] = c.swap_start(g.sendA, g.recvA, f.ws.at[0, q], f.wr.at[0, q], bk.Cp)

    for i in (2, 3):
        moving[i] = gather_second(c, f, GATHERED[i], i, moving[i])
    for copy in halos:
        copy.wait_recv()
    for q in both:
        bk, g = bks[q], views[q]
        for side, at, edge in ((0, 0, 0), (1, bk.N + bk.W, A - 1)):
            g.halo[side] = jnp.where(c.a == edge, 0.0, g.halo[side])
            high, low = split(g.halo[side])
            g.zh[pl.ds(at, bk.W), :] = high
            g.zl[pl.ds(at, bk.W), :] = low
        keep(n.halo + str(q))
    for i in (2, 3):
        gather_end(moving[i])
    keep(n.g_fo, n.g_ex)
    wfo = split(f.g_fo[...].reshape(2 * CH, 2 * CH))
    for q in both:
        bk, g = bks[q], views[q]
        c.swap_end(swaps[q])

        def put(slot, value, g=g, bk=bk):
            g.spec[slot * bk.H : (slot + 1) * bk.H, :] = value

        col_transform(bk, g.col, g.col0, other, g.recvA, put)
        keep(n.spec + str(q))

        def body(r, carry, bk=bk, g=g):
            value = dot3(split(g.spec[pl.ds(r, bk.Q // 2), :]), wfo, NT)
            g.mixed[pl.ds(r, bk.Q // 2), :] = value
            return carry[0] + column_sum(value), carry[1] + column_sum(value * value)

        adding[q] = c.sum_start(f, 1, q, chunks(bk.Q, bk.Q // 2, body, no_sums(2 * CH)))
        keep(n.mixed + str(q))
    for q in both:
        adding[q] = c.sum_cross(f, 1, q, adding[q])
    for q in both:
        bk, g = bks[q], views[q]
        c.sum_end(f, 1, q, adding[q])
        center, inverse = norm_rows(f.sum_out, 1, q, 2 * CH, freqs[q])

        def get(slot, g=g, center=center, inverse=inverse, bk=bk):
            value = g.mixed[slot * bk.H : (slot + 1) * bk.H, :]
            v = (value - center) * inverse * f.norms[2, 0:1, : 2 * CH] + f.norms[2, 1:2, : 2 * CH]
            return v * sigmoid(v)

        def scale(b, value):
            return value * (once if b == 0 else 2.0)

        col_back(bk, g.colT, g.col0T, other, get, scale, g.sendB)
        swaps[q] = c.swap_start(g.sendB, g.recvB, f.ws.at[1, q], f.wr.at[1, q], bk.Cp)

    for i in (4, 5, 6):
        moving[i] = gather_second(c, f, GATHERED[i], i, moving[i])
    for i in (4, 5, 6):
        gather_end(moving[i])

    def taps(t, carry):
        a, b = t // 3, t % 3
        near = f.g_near[:, pl.ds(t, 1)].reshape(CL, CL)
        inward = f.g_inw[:, pl.ds(t, 1)].reshape(CL, CG)
        high, low = split(jnp.concatenate([near, inward], 1))
        f.knh[b, a] = high
        f.knl[b, a] = low
        return carry

    lax.fori_loop(0, 9, taps, 0)
    for a in range(3):
        for b in range(3):
            high, low = split(f.g_outw[:, 3 * a + b].reshape(CG, CL))
            f.koh[b * CG : (b + 1) * CG, a * CL : (a + 1) * CL] = high
            f.kol[b * CG : (b + 1) * CG, a * CL : (a + 1) * CL] = low
    keep(n.knh, n.knl, n.koh, n.kol)
    for q in both:
        bk, g = bks[q], views[q]
        conv_forward(bk, g.zh, g.zl, f.knh, f.knl, f.koh, f.kol, g.joined)

    wex = split(f.g_ex[...].reshape(CG, CH))
    for q in both:
        bk, g = bks[q], views[q]
        c.swap_end(swaps[q])
        for h in range(bk.R):
            rows = slice(h * bk.W, (h + 1) * bk.W)
            g.u[rows, :] = g.act[rows, :] + row_back(bk, g.rowT, g.recvB, h)
        keep(n.u + str(q))

        def body(r, carry, bk=bk, g=g):
            rows = pl.ds(r, bk.MB)
            value = g.joined[rows, CL:] + dot3(split(g.u[rows, :]), wex, NT)
            g.joined[rows, CL:] = value
            value = jnp.concatenate([g.joined[rows, :CL], value], 1)
            return carry[0] + column_sum(value), carry[1] + column_sum(value * value)

        adding[q] = c.sum_start(f, 2, q, chunks(bk.N, bk.MB, body, no_sums(CT)))
    for q in both:
        adding[q] = c.sum_cross(f, 2, q, adding[q])
    for q in both:
        c.sum_end(f, 2, q, adding[q])
    keeper.wait(*keeper.copies)
    c.finish()


def forward_shapes(bks, A, B, sizes):
    CL, CG, CH, NPd = sizes
    CT = CL + CG
    sd = {n.sum_out: (6, 8, 128), n.norms: (3, 8, CT)}
    sd[n.knh] = sd[n.knl] = (3, 3, CL, CT)
    sd[n.koh] = sd[n.kol] = (3 * CG, 3 * CL)
    for name, shape in (
        (n.sq, (CH // A, CG)),
        (n.fo, (2 * CH // A, 2 * CH)),
        (n.ex, (CG // A, CH)),
        (n.nm, (8, pad_to(NPd, 128))),
        (n.near, (9, CL // A, CL)),
        (n.inw, (9, CL // A, CG)),
        (n.outw, (9, CG // A, CL)),
    ):
        sd[whole_of(name)] = (A,) + shape
    for q, bk in enumerate(bks):
        here = {
            n.maps: (bk.N, CT),
            n.up: (bk.N, CT),
            n.joined: (bk.N, CT),
            n.u: (bk.N, CH),
            n.spec: (bk.Q, 2 * CH),
            n.mixed: (bk.Q, 2 * CH),
            n.s: (bk.N, CH),
            n.halo: (2, bk.W, CT),
            n.zh: ((bk.R + 2) * bk.W, CT),
            n.zl: ((bk.R + 2) * bk.W, CT),
            n.act: (bk.N, CH),
        }
        for name in SPECTRA:
            here[name] = (2 * CH // 128, A * bk.Cp, 128)
        for name, shape in here.items():
            sd[name + str(q)] = shape
    sd[n.sum_src] = (6, 8, 128)
    sd[n.sum_a] = (6, A, 8, 128)
    sd[n.sum_z] = (6, B, 8, 128)
    return sd


HALF = {n.knh, n.knl, n.koh, n.kol, n.dth, n.dtl, n.zh, n.zl} | set(for_both(n.zh, n.zl, n.dh, n.dl))


def memory(name, sd, sems):
    if name in sems:
        return pltpu.SemaphoreType.DMA(sems[name])
    return pltpu.VMEM(sd[name], bf16 if name in HALF else f32)


def result(name, sd):
    return jax.ShapeDtypeStruct(sd[name], bf16 if name in HALF else f32)


def sum_sems(A, B):
    return {
        n.sum_as: (6, A),
        n.sum_ar: (6, A),
        n.sum_zs: (6, B),
        n.sum_zr: (6, B),
        n.hs: (2, 2),
        n.hr: (2, 2),
        n.ws: (2, 2, A),
        n.wr: (2, 2, A),
    }


VM = pl.BlockSpec(memory_space=pltpu.VMEM)
FAR = pl.BlockSpec(memory_space=pl.ANY)


def forward_call(bks, A, B, sizes, save, cid, args):
    nc = A // 2
    sd = forward_shapes(bks, A, B, sizes)
    ins, outs, kept, scratch = forward_names()
    sems = sum_sems(A, B)
    sems[n.ld] = (len(kept),)
    for name in (n.g1s, n.g1r, n.g2s, n.g2r):
        sems[name] = (len(GATHERED), nc)
    results = outs + (kept if save else [])
    macs = sum(bk.N for bk in bks) * 1400000
    res = pl.pallas_call(
        functools.partial(forward_kernel, bks, A, B, sizes, save),
        out_shape=[result(name, sd) for name in results],
        in_specs=[VM] * len(ins),
        out_specs=[VM] * len(outs) + [FAR] * (len(results) - len(outs)),
        scratch_shapes=[memory(name, sd, sems) for name in kept + scratch],
        compiler_params=pltpu.CompilerParams(
            collective_id=cid, has_side_effects=True, vmem_limit_bytes=VMEM_LIMIT
        ),
        cost_estimate=pl.CostEstimate(flops=6 * macs, bytes_accessed=40_000_000, transcendentals=0),
        name=n.forward,
    )(*[args[name] for name in ins])
    return dict(zip(results, res))


def finish_kernel(counts, *refs):
    maps, joined, sums, norms, outs = refs[0:2], refs[2:4], refs[4], refs[5], refs[6:8]
    for q in (0, 1):
        center, inverse = norm_rows(sums, 2, q, norms.shape[2], counts[q])
        v = (joined[q][...] - center) * inverse * norms[0, 0:1, :] + norms[0, 1:2, :]
        outs[q][...] = maps[q][...] + v * sigmoid(v)


def finish_call(bks, images, maps, fwd):
    N, CT = maps[0].shape
    step = N // 3 if N % 24 == 0 else N
    block = pl.BlockSpec((step, CT), lambda i: (i, 0))
    counts = [images * bk.H * bk.W for bk in bks]
    return pl.pallas_call(
        functools.partial(finish_kernel, counts),
        out_shape=[jax.ShapeDtypeStruct(m.shape, f32) for m in maps],
        grid=(N // step,),
        in_specs=[block] * 4 + [VM] * 2,
        out_specs=[block] * 2,
        compiler_params=pltpu.CompilerParams(vmem_limit_bytes=VMEM_LIMIT),
        cost_estimate=pl.CostEstimate(
            flops=N * CT * 20, bytes_accessed=N * CT * 24, transcendentals=N * CT * 2
        ),
        name=n.finish,
    )(*maps, fwd[n.joined0], fwd[n.joined1], fwd[n.sum_out], fwd[n.norms])


def flat_plan(A, sizes):
    CL, CG, CH, NPd = sizes
    CT = CL + CG

    def rows(count, width):
        return pad_to(count // A, 8) * pad_to(width, 128) // 128

    near, outw = 9 * rows(CL, CT), 9 * rows(CG, CL)
    first = (0, near, near + outw)
    return first, near + outw + rows(CG, CH), rows(2 * CH, 2 * CH), rows(CH, CG)


LATE = for_both(n.maps, n.halo, n.u, n.mixed, n.spec, n.s)
LATE += [n.g_fo, n.knh, n.knl, n.koh, n.kol, n.g_sq]


def backward_names():
    ins = [n.joined0, n.joined1, n.up0, n.up1, n.sum_out, n.norms, n.g_ex] + for_both(*TABLES)
    outs = [n.back0, n.back1, n.flat1, n.flat2, n.flat3, n.gnorm]
    scratch = [n.sum_src, n.sum_a, n.sum_z, n.bsum, n.sum_as, n.sum_ar, n.sum_zs, n.sum_zr]
    scratch += [n.hs, n.hr, n.ws, n.wr, n.ld, n.rs1s, n.rs1r, n.rs2s, n.rs2r, n.rs3s, n.rs3r, n.rs4s, n.rs4r]
    scratch += [n.das, n.dar, n.dzs, n.dzr]
    scratch += [n.dth, n.dtl, n.zh, n.zl, n.gsq, n.gfo]
    scratch += [n.own1, n.sib1, n.far1, n.zin1, n.own2, n.far2, n.zin2, n.own3, n.far3, n.zin3]
    scratch += for_both(n.dh, n.dl, n.dhalo, n.du, n.dmix, *SPECTRA)
    return ins, outs, scratch


def silu_slope(v):
    sig = sigmoid(v)
    return sig * (1.0 + v * (1.0 - sig))


class Reduce:
    def __init__(self, c, f):
        self.c, self.f = c, f
        self.own, self.sib, self.far, self.zin, self.out = f.own1, f.sib1, f.far1, f.zin1, f.flat1
        self.rows = self.own.shape[1]
        self.nc = c.A // 2
        self.chip, self.core = c.a // 2, c.a % 2

    def to_sibling(self):
        f, c = self.f, self.c
        other = 1 - self.core
        self.copies = [
            c.send(
                self.own.at[2 * cc + other],
                self.sib.at[cc],
                f.rs1s.at[cc],
                f.rs1r.at[cc],
                ha=2 * self.chip + other,
            )
            for cc in range(self.nc)
        ]

    def to_chips(self):
        f, c = self.f, self.c
        for copy in self.copies:
            copy.wait_recv()
        copies = []
        for d in list(range(1, self.nc)) + [0]:
            cc = lax.rem(self.chip + d, self.nc)
            t = 2 * cc + self.core
            self.own[t] = self.own[t] + self.sib[cc]
            if d:
                copies.append(
                    c.send(self.own.at[t], self.far.at[d], f.rs2s.at[d], f.rs2r.at[d], ha=t)
                )
        self.copies = copies

    def to_images(self):
        f, c = self.f, self.c
        for copy in self.copies:
            copy.wait_recv()
        total = self.own[c.a]
        for d in range(1, self.nc):
            total = total + self.far[d]
        self.own[c.a] = total
        part = self.rows // c.B
        copies = []
        for d in range(1, c.B):
            zz = lax.rem(c.z + d, c.B)
            copies.append(
                c.send(
                    self.own.at[c.a, pl.ds(pl.multiple_of(zz * part, 8), part)],
                    self.zin.at[d],
                    f.rs3s.at[d],
                    f.rs3r.at[d],
                    img=zz,
                )
            )
        self.copies = copies

    def from_images(self):
        f, c = self.f, self.c
        for copy in self.copies:
            copy.wait_recv()
        part = self.rows // c.B
        mine = pl.ds(pl.multiple_of(c.z * part, 8), part)
        total = self.own[c.a, mine, :]
        for d in range(1, c.B):
            total = total + self.zin[d]
        self.out[mine, :] = total
        self.copies = [
            c.send(
                self.out.at[mine],
                self.out.at[mine],
                f.rs4s.at[d],
                f.rs4r.at[d],
                img=lax.rem(c.z + d, c.B),
            )
            for d in range(1, c.B)
        ]

    def end(self):
        for copy in self.copies:
            copy.wait_recv()


class Direct:
    def __init__(self, c, f, k, own, far, zin, out):
        self.c, self.f, self.k = c, f, k
        self.own, self.far, self.zin, self.out = own, far, zin, out

    def start(self):
        c, f = self.c, self.f
        self.copies = []
        for d in range(1, c.A):
            t = lax.rem(c.a + d, c.A)
            self.copies.append(
                c.send(
                    self.own.at[t], self.far.at[d], f.das.at[self.k, d], f.dar.at[self.k, d], ha=t
                )
            )

    def cross(self):
        c, f = self.c, self.f
        for copy in self.copies:
            copy.wait_recv()
        total = self.own[c.a]
        for d in range(1, c.A):
            total = total + self.far[d]
        self.zin[c.z] = total
        self.copies = [
            c.send(
                self.zin.at[c.z],
                self.zin.at[c.z],
                f.dzs.at[self.k, d],
                f.dzr.at[self.k, d],
                img=lax.rem(c.z + d, c.B),
            )
            for d in range(1, c.B)
        ]

    def end(self):
        for copy in self.copies:
            copy.wait_recv()
        total = self.zin[0]
        for d in range(1, self.c.B):
            total = total + self.zin[d]
        self.out[...] = total


def backward_kernel(bks, A, B, sizes, *refs):
    ins, outs, scratch = backward_names()
    f = take(ins + [far_of(name) for name in LATE] + outs + LATE + scratch, refs)
    CL, CG, CH, NPd = sizes
    CT = CL + CG
    c = Comm(A, B)
    c.enter()
    loader = Loader(f.ld)
    for name in LATE:
        loader.start(name, getattr(f, far_of(name)), getattr(f, name))
    other = jnp.minimum(c.a, 1)
    once = jnp.where(c.a == 0, 1.0, 2.0)
    cells = [B * bk.H * bk.W for bk in bks]
    freqs = [B * bk.H * (bk.W // 2 + 1) for bk in bks]
    views = [View(f, 0), View(f, 1)]
    both = (0, 1)
    sums = take(
        (n.sum_src, n.sum_a, n.sum_z, n.sum_as, n.sum_ar, n.sum_zs, n.sum_zr, n.sum_out),
        (f.sum_src, f.sum_a, f.sum_z, f.sum_as, f.sum_ar, f.sum_zs, f.sum_zr, f.bsum),
    )
    f.sum_src[...] = jnp.zeros_like(f.sum_src)
    adding, swaps = [None, None], [None, None]

    for q in both:
        bk, g = bks[q], views[q]
        center, inverse = norm_rows(f.sum_out, 2, q, CT, cells[q])

        def body(r, carry, g=g, center=center, inverse=inverse):
            rows = pl.ds(r, 32)
            x = (g.joined[rows, :] - center) * inverse
            dy = g.up[rows, :] * silu_slope(x * f.norms[0, 0:1, :] + f.norms[0, 1:2, :])
            g.back[rows, :] = dy
            return carry[0] + column_sum(dy), carry[1] + column_sum(dy * x)

        total = chunks(bk.N, 32, body, no_sums(CT))
        if q == 0:
            c.entered()
        adding[q] = c.sum_start(sums, 0, q, total)
    for q in both:
        adding[q] = c.sum_cross(sums, 0, q, adding[q])

    wex = split(f.g_ex[...].reshape(CG, CH))
    halos = []
    for q in both:
        bk, g = bks[q], views[q]
        c.sum_end(sums, 0, q, adding[q])
        center, inverse = norm_rows(f.sum_out, 2, q, CT, cells[q])
        gain = f.norms[0, 0:1, :] * inverse
        m1, m2 = (value * (1.0 / cells[q]) for value in totals(f.bsum, 0, q, CT))

        def body(r, carry, bk=bk, g=g, center=center, inverse=inverse, gain=gain, m1=m1, m2=m2):
            rows = pl.ds(r, 32)
            x = (g.joined[rows, :] - center) * inverse
            dz = gain * (g.back[rows, :] - m1 - x * m2)
            g.back[rows, :] = dz
            high, low = split(dz)
            at = pl.ds(pl.multiple_of(r + bk.W, 32), 32)
            g.dh[at, :] = high
            g.dl[at, :] = low
            return carry

        chunks(bk.N, 32, body, 0)
        halos += c.halo_start(
            g.back.at[pl.ds(0, bk.W)],
            g.back.at[pl.ds(bk.N - bk.W, bk.W)],
            g.dhalo,
            f.hs.at[q],
            f.hr.at[q],
        )

        def body2(r, carry, bk=bk, g=g):
            at = pl.ds(pl.multiple_of(r + bk.W, 32), bk.MB)
            g.du[pl.ds(r, bk.MB), :] = dot3((g.dh[at, CL:], g.dl[at, CL:]), wex, NN)
            return carry

        chunks(bk.N, bk.MB, body2, 0)
        row_transform(bk, g.row, lambda h, g=g, bk=bk: g.du[h * bk.W : (h + 1) * bk.W, :], g.sendA)
        swaps[q] = c.swap_start(g.sendA, g.recvA, f.ws.at[0, q], f.wr.at[0, q], bk.Cp)

    first, end1, rows2, rows3 = flat_plan(A, sizes)
    units = (pad_to(CL // A, 8) * (CT // 128), pad_to(CG // A, 8))

    def pack(own, at, value, more):
        rows = value.shape[0] // A
        for t in range(A):
            for k in range(value.shape[1] // 128):
                piece = value[t * rows : (t + 1) * rows, 128 * k : 128 * (k + 1)]
                to = pl.ds(at + k * pad_to(rows, 8), rows)
                own[t, to, :] = own[t, to, :] + piece if more else piece

    def kernel_gradients(q):
        bk, g = bks[q], views[q]
        step = min(bk.N, 384)
        col = lax.broadcasted_iota(jnp.int32, (step, 1), 0) % bk.W
        for i in range(bk.N // step):
            for t in range(CT // 128):
                value = g.back[i * step : (i + 1) * step, 128 * t : 128 * (t + 1)]
                moved = (
                    jnp.where(col == bk.W - 1, 0.0, pltpu.roll(value, step - 1, 0)),
                    value,
                    jnp.where(col == 0, 0.0, pltpu.roll(value, 1, 0)),
                )
                for b in range(3):
                    high, low = split(jnp.transpose(moved[b]))
                    at = b * CL if t == 0 else 3 * CL + b * CG + 128 * (t - 1)
                    f.dth[at : at + 128, i * step : (i + 1) * step] = high
                    f.dtl[at : at + 128, i * step : (i + 1) * step] = low
        loader.wait(n.maps + str(q), n.halo + str(q), n.u + str(q))

        def body(r, carry):
            src = pl.multiple_of(r * bk.W, bk.W)
            high, low = split(g.maps[pl.ds(src, bk.W), :])
            f.zh[pl.ds(src + bk.W, bk.W), :] = high
            f.zl[pl.ds(src + bk.W, bk.W), :] = low
            return carry

        lax.fori_loop(0, bk.R, body, 0)
        for side, at in ((0, 0), (1, bk.N + bk.W)):
            high, low = split(g.halo[side])
            f.zh[pl.ds(at, bk.W), :] = high
            f.zl[pl.ds(at, bk.W), :] = low

        def taps(a, carry):
            rows = pl.ds(pl.multiple_of(a * bk.W, 32), bk.N)
            right = (f.zh[rows, :], f.zl[rows, :])
            out = dot3((f.dth[: 3 * CL, :], f.dtl[: 3 * CL, :]), right, NN)
            for b in range(3):
                at = pl.multiple_of(first[0] + (3 * a + b) * units[0], 8)
                pack(f.own1, at, out[b * CL : (b + 1) * CL], q)
            right = (f.zh[rows, :CL], f.zl[rows, :CL])
            for b in range(3):
                at = 3 * CL + b * CG
                value = dot3((f.dth[at : at + CG, :], f.dtl[at : at + CG, :]), right, NN)
                at = pl.multiple_of(first[1] + (3 * a + b) * units[1], 8)
                pack(f.own1, at, value, q)
            return carry

        lax.fori_loop(0, 3, taps, 0)
        at = 3 * CL + CG
        value = dot3((f.dth[at : at + CG, :], f.dtl[at : at + CG, :]), split(g.u[...]), NN)
        value = jnp.concatenate([value, jnp.zeros((CG, pad_to(CH, 128) - CH), f32)], 1)
        pack(f.own1, first[2], value, q)

    def spectra_slopes(q):
        bk, g = bks[q], views[q]
        loader.wait(n.mixed + str(q))
        c.swap_end(swaps[q])
        center, inverse = norm_rows(f.sum_out, 1, q, 2 * CH, freqs[q])
        carry = [no_sums(2 * CH)]

        def put(slot, value):
            rows = slice(slot * bk.H, (slot + 1) * bk.H)
            x = (g.mixed[rows, :] - center) * inverse
            value = value * (once if slot in (0, bk.nb) else 2.0)
            dy = value * silu_slope(x * f.norms[2, 0:1, : 2 * CH] + f.norms[2, 1:2, : 2 * CH])
            g.dmix[rows, :] = dy
            carry[0] = (carry[0][0] + column_sum(dy), carry[0][1] + column_sum(dy * x))

        col_transform(bk, g.col, g.col0, other, g.recvA, put)
        adding[q] = c.sum_start(sums, 1, q, carry[0])

    def spectra_back(q, wfo):
        bk, g = bks[q], views[q]
        c.sum_end(sums, 1, q, adding[q])
        center, inverse = norm_rows(f.sum_out, 1, q, 2 * CH, freqs[q])
        gain = f.norms[2, 0:1, : 2 * CH] * inverse
        m1, m2 = (value * (1.0 / freqs[q]) for value in totals(f.bsum, 1, q, 2 * CH))

        def get(slot):
            rows = slice(slot * bk.H, (slot + 1) * bk.H)
            x = (g.mixed[rows, :] - center) * inverse
            dz = gain * (g.dmix[rows, :] - m1 - x * m2)
            g.dmix[rows, :] = dz
            return dot3(split(dz), wfo, NN)

        col_back(bk, g.colT, g.col0T, other, get, lambda b, v: v, g.sendB)
        swaps[q] = c.swap_start(g.sendB, g.recvB, f.ws.at[1, q], f.wr.at[1, q], bk.Cp)

    kernel_gradients(0)
    spectra_slopes(0)
    kernel_gradients(1)
    adding[0] = c.sum_cross(sums, 1, 0, adding[0])
    if f.own1.shape[1] > end1:
        f.own1[:, end1:, :] = jnp.zeros((A, f.own1.shape[1] - end1, 128), f32)
    red1 = Reduce(c, f)
    red1.to_sibling()
    spectra_slopes(1)
    loader.wait(n.g_fo)
    wfo = split(f.g_fo[...].reshape(2 * CH, 2 * CH))
    spectra_back(0, wfo)
    adding[1] = c.sum_cross(sums, 1, 1, adding[1])
    red1.to_chips()
    spectra_back(1, wfo)
    for q in both:
        bk, g = bks[q], views[q]
        loader.wait(n.spec + str(q))
        value = dot3(split(jnp.transpose(g.dmix[...])), split(g.spec[...]), NN)
        f.gfo[...] = value if q == 0 else f.gfo[...] + value
    pack(f.own2, 0, f.gfo, 0)
    red2 = Direct(c, f, 0, f.own2, f.far2, f.zin2, f.flat2)
    red2.start()

    for copy in halos:
        copy.wait_recv()
    c.sent(halos)
    loader.wait(n.knh, n.knl, n.koh, n.kol)

    def input_gradients(q):
        bk, g = bks[q], views[q]
        for side, at, edge in ((0, 0, 0), (1, bk.N + bk.W, A - 1)):
            high, low = split(jnp.where(c.a == edge, 0.0, g.dhalo[side]))
            g.dh[pl.ds(at, bk.W), :] = high
            g.dl[pl.ds(at, bk.W), :] = low
        conv_backward(bk, g.dh, g.dl, f.knh, f.knl, f.koh, f.kol, g.back)

    def active_slopes(q):
        bk, g = bks[q], views[q]
        loader.wait(n.s + str(q))
        c.swap_end(swaps[q])
        center, inverse = norm_rows(f.sum_out, 0, q, CH, cells[q])
        total = no_sums(CH)
        for h in range(bk.R):
            rows = slice(h * bk.W, (h + 1) * bk.W)
            x = (g.s[rows, :] - center) * inverse
            value = g.du[rows, :] + row_back(bk, g.rowT, g.recvB, h)
            dy = value * silu_slope(x * f.norms[1, 0:1, :CH] + f.norms[1, 1:2, :CH])
            g.du[rows, :] = dy
            total = (total[0] + column_sum(dy), total[1] + column_sum(dy * x))
        adding[q] = c.sum_start(sums, 2, q, total)

    def squeeze_back(q, wsq):
        bk, g = bks[q], views[q]
        c.sum_end(sums, 2, q, adding[q])
        center, inverse = norm_rows(f.sum_out, 0, q, CH, cells[q])
        gain = f.norms[1, 0:1, :CH] * inverse
        m1, m2 = (value * (1.0 / cells[q]) for value in totals(f.bsum, 2, q, CH))

        def body(r, carry):
            rows = pl.ds(r, bk.MB)
            x = (g.s[rows, :] - center) * inverse
            dz = gain * (g.du[rows, :] - m1 - x * m2)
            g.du[rows, :] = dz
            g.back[rows, CL:] += dot3(split(dz), wsq, NN)
            return carry

        chunks(bk.N, bk.MB, body, 0)
        value = dot3(split(jnp.transpose(g.du[...])), split(g.maps[:, CL:]), NN)
        f.gsq[...] = value if q == 0 else f.gsq[...] + value

    input_gradients(0)
    red1.to_images()
    active_slopes(0)
    input_gradients(1)
    adding[0] = c.sum_cross(sums, 2, 0, adding[0])
    active_slopes(1)
    loader.wait(n.g_sq)
    wsq = split(f.g_sq[...].reshape(CH, CG))
    red2.cross()
    squeeze_back(0, wsq)
    adding[1] = c.sum_cross(sums, 2, 1, adding[1])
    red1.from_images()
    squeeze_back(1, wsq)
    pack(f.own3, 0, f.gsq, 0)
    red3 = Direct(c, f, 1, f.own3, f.far3, f.zin3, f.flat3)
    red3.start()

    span = pad_to(NPd * A, 128) + 128
    lane = lax.broadcasted_iota(jnp.int32, (8, span), 1)
    out = []
    for i in (1, 0):
        rows = []
        for k, width in ((0, CT), (1, 2 * CH), (2, CH)):
            pair = [totals(f.bsum, k, q, CT)[i] for q in both]
            row = jnp.concatenate([pair[0] + pair[1], jnp.zeros((1, span - CT), f32)], 1)
            rows.append(jnp.where(lane < width, jnp.broadcast_to(row, (8, span)), 0.0))
        out.append(rows[0] + pltpu.roll(rows[2], CT, 1) + pltpu.roll(rows[1], CT + CH, 1))
    sub = lax.broadcasted_iota(jnp.int32, (8, span), 0)
    value = pltpu.roll(jnp.where(sub == 0, out[0], out[1]), lax.rem(span - NPd * c.a, span), 1)
    f.gnorm[...] = value[:, : f.gnorm.shape[1]]

    red1.end()
    red2.end()
    red3.cross()
    red3.end()
    c.finish()


def conv_backward(bk, dh, dl, knh, knl, koh, kol, out):
    MB, W = bk.MB, bk.W
    CL = knh.shape[2]
    CG = koh.shape[0] // 3
    CT = knh.shape[3]
    col = lax.broadcasted_iota(jnp.int32, (MB, 1), 0) % W

    def moved(value, b):
        if b == 0:
            return jnp.where(col == W - 1, 0.0, pltpu.roll(value, MB - 1, 0))
        if b == 2:
            return jnp.where(col == 0, 0.0, pltpu.roll(value, 1, 0))
        return value

    def body(i, carry):
        r = pl.multiple_of(i * MB, 32)
        rows = [pl.ds(pl.multiple_of(r + (2 - a) * W, 32), MB) for a in range(3)]
        left = tuple(jnp.concatenate([d[rows[a], :CL] for a in range(3)], 1) for d in (dh, dl))
        total = None
        for b in (1, 0, 2):
            right = (knh[b].reshape(3 * CL, CT), knl[b].reshape(3 * CL, CT))
            value = moved(dot3(left, right, NN), b)
            total = value if total is None else total + value
        out[pl.ds(r, MB), :] = total
        cross = None
        for a in range(3):
            left2 = (dh[rows[a], CL:], dl[rows[a], CL:])
            right = tuple(
                jnp.concatenate(
                    [k[b * CG : (b + 1) * CG, a * CL : (a + 1) * CL] for b in range(3)], 1
                )
                for k in (koh, kol)
            )
            value = dot3(left2, right, NN)
            cross = value if cross is None else cross + value
        total = None
        for b in range(3):
            value = moved(cross[:, b * CL : (b + 1) * CL], b)
            total = value if total is None else total + value
        out[pl.ds(r, MB), :CL] += total
        return carry

    lax.fori_loop(0, bk.N // MB, body, 0)


def backward_call(bks, A, B, sizes, cid, args):
    CL, CG, CH, NPd = sizes
    CT = CL + CG
    nc = A // 2
    first, end1, rows2, rows3 = flat_plan(A, sizes)
    rows1 = pad_to(end1, 8 * B)
    N = max(bk.N for bk in bks)
    big = max((bk.R + 2) * bk.W for bk in bks)
    sd = forward_shapes(bks, A, B, sizes)
    sd[n.bsum] = sd[n.sum_src]
    sd[n.gnorm] = (8, pad_to(NPd, 128))
    sd[n.dth] = sd[n.dtl] = (3 * CT, N)
    sd[n.zh] = sd[n.zl] = (big, CT)
    sd[n.gsq], sd[n.gfo] = (CH, CG), (2 * CH, 2 * CH)
    sd[n.flat1], sd[n.own1], sd[n.zin1] = (rows1, 128), (A, rows1, 128), (B, rows1 // B, 128)
    sd[n.sib1] = sd[n.far1] = (nc, rows1, 128)
    sd[n.flat2], sd[n.zin2] = (rows2, 128), (B, rows2, 128)
    sd[n.own2] = sd[n.far2] = (A, rows2, 128)
    sd[n.flat3], sd[n.zin3] = (rows3, 128), (B, rows3, 128)
    sd[n.own3] = sd[n.far3] = (A, rows3, 128)
    for q, bk in enumerate(bks):
        here = {
            n.back: (bk.N, CT),
            n.dh: ((bk.R + 2) * bk.W, CT),
            n.dl: ((bk.R + 2) * bk.W, CT),
            n.dhalo: (2, bk.W, CT),
            n.du: (bk.N, CH),
            n.dmix: (bk.Q, 2 * CH),
        }
        for name, shape in here.items():
            sd[name + str(q)] = shape
    sems = sum_sems(A, B)
    sems[n.ld] = (len(LATE),)
    for name in (n.rs1s, n.rs1r, n.rs2s, n.rs2r):
        sems[name] = (nc,)
    for name in (n.rs3s, n.rs3r, n.rs4s, n.rs4r):
        sems[name] = (B,)
    for name in (n.das, n.dar):
        sems[name] = (2, A)
    for name in (n.dzs, n.dzr):
        sems[name] = (2, B)
    ins, outs, scratch = backward_names()
    macs = sum(bk.N for bk in bks) * 2800000
    res = pl.pallas_call(
        functools.partial(backward_kernel, bks, A, B, sizes),
        out_shape=[result(name, sd) for name in outs],
        in_specs=[VM] * len(ins) + [FAR] * len(LATE),
        out_specs=[VM] * len(outs),
        scratch_shapes=[memory(name, sd, sems) for name in LATE + scratch],
        compiler_params=pltpu.CompilerParams(
            collective_id=cid, has_side_effects=True, vmem_limit_bytes=VMEM_LIMIT
        ),
        cost_estimate=pl.CostEstimate(flops=6 * macs, bytes_accessed=40_000_000, transcendentals=0),
        name=n.backward,
    )(*[args[name] for name in ins + LATE])
    return dict(zip(outs, res))


KINDS = (n.near, n.inw, n.outw, n.sq, n.fo, n.ex, n.nm)


def update_kernel(A, sizes, *refs):
    CL, CG, CH, NPd = sizes
    CT = CL + CG
    flat1, flat2, flat3, gnorm = refs[:4]
    weights, moments, averages = refs[4:11], refs[11:18], refs[18:25]
    updated, velocity, smoothed, half = refs[25:32], refs[32:39], refs[39:46], refs[46:53]
    packed = refs[53]
    first = flat_plan(A, sizes)[0]
    decay = min(0.5, (1.0 + STEP) / (10.0 + STEP))

    def step(i, at, grad):
        moving = momentum * moments[i][at] + grad
        new = weights[i][at] - learn_rate * (grad + momentum * moving)
        velocity[i][at] = moving
        updated[i][at] = new
        smoothed[i][at] = decay * averages[i][at] + (1.0 - decay) * new
        half[i][at] = new.astype(bf16)
        return new

    def rows(flat, at, count, tiles):
        unit = pad_to(count, 8)
        return jnp.concatenate(
            [flat[at + t * unit : at + t * unit + count, :] for t in range(tiles)], 1
        )

    o, p = CL // A, CG // A
    for k in range(9):
        grad = rows(flat1, first[0] + k * pad_to(o, 8) * (CT // 128), o, CT // 128)
        step(0, k, grad[:, :CL])
        step(1, k, grad[:, CL:])
        step(2, k, rows(flat1, first[1] + k * pad_to(p, 8), p, CL // 128))
    every = slice(None)
    step(5, every, rows(flat1, first[2], p, pad_to(CH, 128) // 128)[:, :CH])
    step(3, every, rows(flat3, 0, CH // A, CG // 128))
    step(4, every, rows(flat2, 0, 2 * CH // A, 2 * CH // 128))
    new = step(6, every, gnorm[0:2, :NPd])
    packed[...] = jnp.zeros_like(packed)
    packed[0:2, :NPd] = new


def update_call(A, sizes, bwd, weights, moments, averages):
    CL, CG, CH, NPd = sizes
    shapes = [w.shape for w in weights]
    outs = [jax.ShapeDtypeStruct(s, f32) for _ in range(3) for s in shapes]
    outs += [jax.ShapeDtypeStruct(s, bf16) for s in shapes]
    outs.append(jax.ShapeDtypeStruct((8, pad_to(NPd, 128)), f32))
    res = pl.pallas_call(
        functools.partial(update_kernel, A, sizes),
        out_shape=outs,
        in_specs=[VM] * 25,
        out_specs=[VM] * len(outs),
        compiler_params=pltpu.CompilerParams(vmem_limit_bytes=VMEM_LIMIT),
        cost_estimate=pl.CostEstimate(flops=3_000_000, bytes_accessed=5_000_000, transcendentals=0),
        name=n.update,
    )(bwd[n.flat1], bwd[n.flat2], bwd[n.flat3], bwd[n.gnorm], *weights, *moments, *averages)
    return res[0:7], res[7:14], res[14:21], res[21:28], res[28]


def as_rows(weight):
    return jnp.transpose(weight[0], (0, 1, 3, 2)).reshape(9, weight.shape[4], weight.shape[3])


def from_rows(value):
    return jnp.transpose(value.reshape(1, 3, 3, value.shape[1], value.shape[2]), (0, 1, 2, 4, 3))


def flat_rows(weight):
    return jnp.transpose(weight[0])


def from_flat(value):
    return jnp.transpose(value)[None]


def padded_norm(table):
    return jnp.pad(table, ((0, 6), (0, pad_to(table.shape[1], 128) - table.shape[1])))


def per_device(*arrays):
    A, B = lax.axis_size("ha"), lax.axis_size("img")
    maps, ups = arrays[0:2], arrays[2:4]
    groups = [arrays[4 + i :: 3] for i in range(3)]
    to_local = (as_rows,) * 3 + (flat_rows,) * 3 + (lambda w: w[0],)
    weights, moments, averages = (
        [change(w) for change, w in zip(to_local, group)] for group in groups
    )
    bks = [Bucket(m.shape[1], m.shape[2], A) for m in maps]
    CL, CG, CH, NPd = weights[0].shape[2], weights[1].shape[2], weights[5].shape[1], weights[6].shape[1]
    sizes = (CL, CG, CH, NPd)
    CT = CL + CG
    args = {}
    for q in (0, 1):
        args[n.maps + str(q)] = maps[q].reshape(-1, CT)
        args[n.up + str(q)] = ups[q].reshape(-1, CT)
        for name, table in zip(TABLES, tables_of(bks[q])):
            args[name + str(q)] = jnp.asarray(table)
    flat_maps = [args[n.maps0], args[n.maps1]]
    args.update(zip(KINDS, weights))
    args[n.nm] = padded_norm(weights[6])
    fwd = forward_call(bks, A, B, sizes, True, 1, args)
    block = finish_call(bks, B, flat_maps, fwd)
    bwd = backward_call(bks, A, B, sizes, 2, {**args, **fwd})
    back = [args[n.up + str(q)] + bwd[n.back + str(q)] for q in (0, 1)]
    updated, velocity, smoothed, half, packed = update_call(A, sizes, bwd, weights, moments, averages)
    again = dict(args)
    again.update(zip(KINDS, updated))
    again[n.nm] = packed
    fresh = forward_call(bks, A, B, sizes, False, 3, again)
    rerun = finish_call(bks, B, flat_maps, fresh)
    out = []
    for pair in (block, back, rerun):
        out += [value.reshape(m.shape) for value, m in zip(pair, maps)]
    to_outer = (from_rows,) * 3 + (from_flat,) * 3 + (lambda w: w[None],)
    for i in range(7):
        out += [to_outer[i](group[i]) for group in (updated, velocity, smoothed, half)]
    return tuple(out)


def solution(mesh):
    cells = P("img", "ha", None, None)
    kernel = P(None, None, None, None, "ha")
    matrix = P(None, None, "ha")
    return jax.shard_map(
        per_device,
        mesh=mesh,
        in_specs=(cells,) * 4 + (kernel,) * 9 + (matrix,) * 12,
        out_specs=(cells,) * 6 + (kernel,) * 12 + (matrix,) * 16,
        check_vma=False,
    )
```

```python
import functools
import math

import jax
import jax.numpy as jnp
import numpy as np
from jax import lax
from jax.experimental import pallas as pl
from jax.experimental.pallas import tpu as pltpu
from jax.sharding import PartitionSpec as P

STEP = 6

epsilon = 1e-05
learn_rate = 3e-05
momentum = 0.5

f32 = jnp.float32
bf16 = jnp.bfloat16
MESH = pl.DeviceIdType.MESH
VMEM_LIMIT = 60 * 1024 * 1024

NN = (((1,), (0,)), ((), ()))
NT = (((1,), (1,)), ((), ()))
TN = (((0,), (0,)), ((), ()))


def dg(left, right, dims):
    return lax.dot_general(left, right, dims, preferred_element_type=f32)


def split(value):
    high = value.astype(bf16)
    return high, (value - high.astype(f32)).astype(bf16)


def dot3(left, right, dims):
    lh, ll = left
    rh, rl = right
    return dg(lh, rh, dims) + dg(ll, rh, dims) + dg(lh, rl, dims)


def sigmoid(v):
    return 1.0 / (1.0 + jnp.exp(-v))


def pad_to(n, m):
    return -(-n // m) * m


def chunks(count, step, body, carry):
    def run(i, carry):
        return body(pl.multiple_of(i * step, 8), carry)

    return lax.fori_loop(0, count // step, run, carry)


class Bucket:
    def __init__(self, rows, width, group):
        self.R, self.W, self.A = rows, width, group
        self.H = rows * group
        self.N = rows * width
        self.nb = -(-(width // 2) // group)
        self.Cp = pad_to(self.nb * rows, 8)
        self.Q = (self.nb + 1) * self.H
        self.MB = max(r * width for r in range(1, rows + 1) if rows % r == 0 and r * width <= 384)


def hi_lo(table):
    table = np.asarray(table, np.float64)
    high = table.astype(np.float32).astype(jnp.bfloat16)
    low = (table - high.astype(np.float64)).astype(np.float32).astype(jnp.bfloat16)
    return np.stack([high, low])


def tables_of(bk):
    A, nb, W, H, R = bk.A, bk.nb, bk.W, bk.H, bk.R
    row = np.zeros((2, nb, A, W))
    w = np.arange(W)
    for b in range(nb):
        for d in range(A):
            j = d * nb + b
            if j == 0:
                row[0, b, d] = 1.0
                row[1, b, d] = np.cos(math.pi * w)
            elif 2 * j < W:
                row[0, b, d] = np.cos(2 * math.pi * (j * w % W) / W)
                row[1, b, d] = -np.sin(2 * math.pi * (j * w % W) / W)
    row = row.reshape(2 * nb * A, W) / math.sqrt(W)
    k = np.arange(H)[:, None]
    h = np.array([s * R + r for r in range(R) for s in range(A)])[None, :]
    phase = 2 * math.pi * (k * h % H) / H
    cos, sin = np.cos(phase) / math.sqrt(H), np.sin(phase) / math.sqrt(H)
    none = np.zeros_like(cos)
    plain = np.block([[cos, sin], [-sin, cos]])
    packed = np.block([[cos, none], [-sin, none], [none, cos], [none, -sin]])
    other = np.concatenate([plain, np.zeros_like(plain)], 0)
    first = np.stack([hi_lo(packed), hi_lo(other)])
    return (
        hi_lo(row),
        hi_lo(row.T),
        hi_lo(plain),
        hi_lo(plain.T),
        first,
        np.swapaxes(first, 2, 3),
    )


class Names:
    def __getattr__(self, name):
        return name


n = Names()
TABLES = (n.row, n.rowT, n.col, n.colT, n.col0, n.col0T)
SPECTRA = (n.sendA, n.recvA, n.sendB, n.recvB)


def for_both(*names):
    return [name + str(q) for q in (0, 1) for name in names]


class View:
    def __init__(self, refs, q):
        self.refs, self.q = refs, q

    def __getattr__(self, name):
        return getattr(self.refs, name + str(self.q))


class Fields:
    pass


def take(names, refs):
    out = Fields()
    for name, ref in zip(names, refs):
        setattr(out, name, ref)
    return out


class Group:
    def __init__(self, ssem, rsem, landed):
        self.ssem, self.rsem, self.landed = ssem, rsem, landed

    def wait_recv(self):
        pltpu.make_async_copy(self.landed, self.landed, self.rsem).wait()

    def wait_send(self):
        pltpu.make_async_copy(self.landed, self.landed, self.ssem).wait()


class Comm:
    def __init__(self, A, B):
        self.A, self.B = A, B
        self.a = lax.axis_index("ha")
        self.z = lax.axis_index("img")
        self.pending, self.halos = [], []

    def enter(self):
        bar = pltpu.get_barrier_semaphore()
        for d in range(1, self.A):
            pl.semaphore_signal(
                bar, inc=1, device_id=(self.z, lax.rem(self.a + d, self.A)), device_id_type=MESH
            )
        for d in range(1, self.B):
            pl.semaphore_signal(
                bar, inc=1, device_id=(lax.rem(self.z + d, self.B), self.a), device_id_type=MESH
            )

    def entered(self):
        pl.semaphore_wait(pltpu.get_barrier_semaphore(), self.A + self.B - 2)

    def make(self, src, dst, ssem, rsem, ha=None, img=None):
        return pltpu.make_async_remote_copy(
            src,
            dst,
            ssem,
            rsem,
            device_id=(self.z if img is None else img, self.a if ha is None else ha),
            device_id_type=MESH,
        )

    def send(self, *args, **kwargs):
        copy = self.make(*args, **kwargs)
        copy.start()
        self.pending.append(copy)
        return copy

    def group(self, moves, ssem, rsem, landed):
        for src, dst, where in moves:
            self.make(src, dst, ssem, rsem, **where).start()
        group = Group(ssem, rsem, landed)
        self.pending.append(group)
        return group

    def finish(self):
        self.halo_sent()
        for copy in self.pending:
            copy.wait_send()

    def sum_start(self, f, k, q, sums):
        i = 2 * k + q
        for part in (0, 1):
            value = jnp.sum(sums[part], 0, keepdims=True)
            for t in range(-(-value.shape[1] // 128)):
                piece = value[:, 128 * t : 128 * (t + 1)]
                f.sum_src[i, 4 * part + t : 4 * part + t + 1, : piece.shape[1]] = piece
        f.sum_a[i, self.a] = f.sum_src[i]
        moves = [
            (f.sum_src.at[i], f.sum_a.at[i, self.a], {n.ha: lax.rem(self.a + d, self.A)})
            for d in range(1, self.A)
        ]
        return self.group(moves, f.sum_as.at[i], f.sum_ar.at[i], f.sum_a.at[i, pl.ds(0, self.A - 1)])

    def sum_cross(self, f, k, q, copies):
        i = 2 * k + q
        copies.wait_recv()
        total = f.sum_a[i, 0]
        for d in range(1, self.A):
            total = total + f.sum_a[i, d]
        f.sum_z[i, self.z] = total
        mine = f.sum_z.at[i, self.z]
        moves = [(mine, mine, {n.img: lax.rem(self.z + d, self.B)}) for d in range(1, self.B)]
        if not moves:
            return None
        return self.group(moves, f.sum_zs.at[i], f.sum_zr.at[i], f.sum_z.at[i, pl.ds(0, self.B - 1)])

    def sum_end(self, f, k, q, copies):
        i = 2 * k + q
        if copies is not None:
            copies.wait_recv()
        total = f.sum_z[i, 0]
        for d in range(1, self.B):
            total = total + f.sum_z[i, d]
        f.sum_out[i] = total

    def swap_start(self, src, dst, ssem, rsem, rows):
        def block(ref, t):
            return ref.at[:, pl.ds(pl.multiple_of(t * rows, 8), rows)]

        moves = []
        for d in range(1, self.A):
            t = lax.rem(self.a + d, self.A)
            moves.append((block(src, t), block(dst, self.a), {n.ha: t}))
        group = self.group(moves, ssem, rsem, dst.at[:, pl.ds(0, (self.A - 1) * rows)])
        mine = pl.ds(pl.multiple_of(self.a * rows, 8), rows)
        dst[:, mine, :] = src[:, mine, :]
        return group

    def swap_end(self, group):
        group.wait_recv()

    def halo_start(self, low_row, high_row, dst, ssem, rsem):
        up = jnp.maximum(self.a - 1, 0)
        down = jnp.minimum(self.a + 1, self.A - 1)
        low = self.make(low_row, dst.at[1], ssem.at[0], rsem.at[0], ha=up)
        high = self.make(high_row, dst.at[0], ssem.at[1], rsem.at[1], ha=down)

        @pl.when(self.a > 0)
        def _():
            low.start()

        @pl.when(self.a < self.A - 1)
        def _():
            high.start()

        self.halos.append((low, high))
        return [(low, high)]

    def halo_end(self, pairs):
        for low, high in pairs:

            @pl.when(self.a < self.A - 1)
            def _():
                low.wait_recv()

            @pl.when(self.a > 0)
            def _():
                high.wait_recv()

    def halo_sent(self):
        for low, high in self.halos:

            @pl.when(self.a > 0)
            def _():
                low.wait_send()

            @pl.when(self.a < self.A - 1)
            def _():
                high.wait_send()

        self.halos = []


def column_sum(value):
    rows, width = value.shape
    return jnp.sum(value.reshape(rows // 8, 8, width), 0)


def no_sums(width):
    return jnp.zeros((8, width), f32), jnp.zeros((8, width), f32)


def totals(ref, k, q, width):
    i = 2 * k + q
    return [
        jnp.concatenate([ref[i, t : t + 1, :] for t in range(first, first + 4)], 1)[:, :width]
        for first in (0, 4)
    ]


def norm_rows(ref, k, q, width, count):
    total, square = totals(ref, k, q, width)
    center = total * (1.0 / count)
    variance = square * (1.0 / count) - center * center
    return center, lax.rsqrt(variance + epsilon)


def row_transform(bk, table, source, send):
    nbA = bk.nb * bk.A
    tab = (table[0], table[1])
    for h in range(bk.R):
        out = dot3(tab, split(source(h)), NN)
        out = jnp.concatenate([out[:nbA], out[nbA:]], 1)
        for b in range(bk.nb):
            put_strided(send, b * bk.R + h, bk.A, bk.Cp, out[b * bk.A : (b + 1) * bk.A])


def row_back(bk, table, recv, h):
    parts = [get_strided(recv, b * bk.R + h, bk.A, bk.Cp) for b in range(bk.nb)]
    block = jnp.concatenate(parts, 0) if len(parts) > 1 else parts[0]
    half = block.shape[1] // 2
    block = jnp.concatenate([block[:, :half], block[:, half:]], 0)
    return dot3((table[0], table[1]), split(block), NN)


def put_strided(ref, start, count, stride, value):
    for t in range(ref.shape[0]):
        ref[t, pl.ds(start, count, stride=stride), :] = value[:, 128 * t : 128 * (t + 1)]


def get_strided(ref, start, count, stride):
    return jnp.concatenate(
        [ref[t, pl.ds(start, count, stride=stride), :] for t in range(ref.shape[0])], 1
    )


def first_table(ref, other):
    return ref[other, 0], ref[other, 1]


def col_transform(bk, f_col, f_col0, other, recv, put):
    H = bk.H
    for b in range(bk.nb):
        block = jnp.concatenate(
            [get_strided(recv, b * bk.R + h, bk.A, bk.Cp) for h in range(bk.R)], 0
        )
        half = block.shape[1] // 2
        block = split(jnp.concatenate([block[:, :half], block[:, half:]], 0))
        if b == 0:
            out = dot3(first_table(f_col0, other), block, NN)
            put(bk.nb, jnp.concatenate([out[2 * H : 3 * H], out[3 * H :]], 1))
        else:
            out = dot3((f_col[0], f_col[1]), block, NN)
        put(b, jnp.concatenate([out[:H], out[H : 2 * H]], 1))


def col_back(bk, f_colT, f_col0T, other, get, scale, send):
    H = bk.H

    def halves(value):
        half = value.shape[1] // 2
        return [value[:, :half], value[:, half:]]

    for b in range(bk.nb):
        if b == 0:
            block = jnp.concatenate(halves(get(0)) + halves(get(bk.nb)), 0)
            out = dot3(first_table(f_col0T, other), split(block), NN)
        else:
            out = dot3((f_colT[0], f_colT[1]), split(jnp.concatenate(halves(get(b)), 0)), NN)
        out = jnp.concatenate([out[:H], out[H:]], 1)
        out = scale(b, out)
        for h in range(bk.R):
            put_strided(send, b * bk.R + h, bk.A, bk.Cp, out[h * bk.A : (h + 1) * bk.A])


def conv_forward(bk, zh, zl, knh, knl, koh, kol, out):
    MB, W = bk.MB, bk.W
    col = lax.broadcasted_iota(jnp.int32, (MB, 1), 0) % W

    def combine(value, n):
        low = jnp.where(col == 0, 0.0, pltpu.roll(value[:, :n], 1, 0))
        high = jnp.where(col == W - 1, 0.0, pltpu.roll(value[:, 2 * n :], MB - 1, 0))
        return low + value[:, n : 2 * n] + high

    def body(i, carry):
        r = pl.multiple_of(i * MB, 32)
        total = None
        for a in range(3):
            left = (zh[pl.ds(r + a * W, MB), :], zl[pl.ds(r + a * W, MB), :])
            n = knh.shape[2]
            right = (knh[:, a].reshape(3 * n, -1), knl[:, a].reshape(3 * n, -1))
            part = dot3(left, right, NT)
            total = part if total is None else total + part
        CL = knh.shape[2]
        out[pl.ds(r, MB), :CL] = combine(total, CL)
        left = tuple(
            jnp.concatenate([z[pl.ds(r + a * W, MB), :CL] for a in range(3)], 1) for z in (zh, zl)
        )
        cross = dot3(left, (koh[...], kol[...]), NT)
        out[pl.ds(r, MB), CL:] = combine(cross, koh.shape[0] // 3)
        return carry

    lax.fori_loop(0, bk.N // MB, body, 0)


GATHERED = (n.sq, n.nm, n.fo)


class Loader:
    def __init__(self, sems):
        self.sems, self.copies = sems, {}

    def start(self, name, src, dst):
        copy = pltpu.make_async_copy(src, dst, self.sems.at[len(self.copies)])
        copy.start()
        self.copies[name] = copy

    def wait(self, *names):
        for name in names:
            self.copies[name].wait()


KINDS = (n.near, n.inw, n.outw, n.sq, n.fo, n.ex, n.nm)


def old_of(name):
    return name + n._old


def moment_of(name):
    return name + n._moment


def whole_of(name):
    return n.g_ + name


def gather_direct(c, f, name, i):
    shard, whole = getattr(f, name), getattr(f, whole_of(name))
    whole[c.a] = shard[...]
    moves = [(shard, whole.at[c.a], {n.ha: lax.rem(c.a + d, c.A)}) for d in range(1, c.A)]
    return c.group(moves, f.g1s.at[i], f.g1r.at[i], whole.at[pl.ds(0, c.A - 1)])


def grid_of(chips):
    across = max(x for x in range(1, chips + 1) if chips % x == 0 and x * x <= chips)
    return chips // across, across


class Spread:
    def __init__(self, c, f, names):
        self.c, self.f, self.names = c, f, names
        self.Y, self.X = grid_of(c.A // 2)
        self.chip, self.core = c.a // 2, c.a % 2
        self.y, self.x = self.chip // self.X, lax.rem(self.chip, self.X)

    def device(self, dy, dx, core=None):
        y, x = lax.rem(self.y + dy + self.Y, self.Y), lax.rem(self.x + dx + self.X, self.X)
        return 2 * (y * self.X + x) + (self.core if core is None else core)

    def part(self, ref, half, slot):
        if len(ref.shape) == 3:
            return ref.at[slot]
        cut = ref.shape[1] // 2
        return ref.at[slot, pl.ds(0, cut) if half == 0 else pl.ds(cut, ref.shape[1] - cut)]

    def lines(self, half, first):
        along_x = (half == 0) == first
        return [(0, d) for d in range(1, self.X)] if along_x else [(d, 0) for d in range(1, self.Y)]

    def members(self, half):
        for i, name in enumerate(self.names):
            if half == 0 or len(getattr(self.f, name).shape) == 3:
                yield i, name

    def pass_on(self, half, slots, lines, ssem, rsem):
        groups = []
        for i, name in self.members(half):
            ref = getattr(self.f, whole_of(name))
            moves = []
            for dy, dx in lines:
                for slot in slots:
                    piece = self.part(ref, half, slot)
                    moves.append((piece, piece, {n.ha: self.device(dy, dx)}))
            if moves:
                landed = self.part(ref, half, pl.ds(0, len(moves)))
                groups.append(self.c.group(moves, ssem.at[i, half], rsem.at[i, half], landed))
        return groups

    def start(self):
        f = self.f
        for name in self.names:
            getattr(f, whole_of(name))[self.c.a] = getattr(f, name)[...]
        self.one = []
        for half in (0, 1):
            self.one += self.pass_on(half, [self.c.a], self.lines(half, True), f.t1s, f.t1r)

    def second(self):
        f = self.f
        for group in self.one:
            group.wait_recv()
        self.two = []
        for half in (0, 1):
            slots = [self.device(-dy, -dx) for dy, dx in [(0, 0)] + self.lines(half, True)]
            self.two += self.pass_on(half, slots, self.lines(half, False), f.t2s, f.t2r)

    def third(self):
        f, c = self.f, self.c
        for group in self.two:
            group.wait_recv()
        self.three = []
        sibling = self.device(0, 0, 1 - self.core)
        for i, name in enumerate(self.names):
            ref = getattr(f, whole_of(name))
            moves = []
            for dy in range(self.Y):
                for dx in range(self.X):
                    piece = ref.at[self.device(dy, dx)]
                    moves.append((piece, piece, {n.ha: sibling}))
            landed = ref.at[pl.ds(0, len(moves))]
            self.three.append(c.group(moves, f.t3s.at[i], f.t3r.at[i], landed))

    def end(self):
        for group in self.three:
            group.wait_recv()


def far_of(name):
    return name + n._hbm


def forward_names(save):
    weights = list(KINDS)
    ins = for_both(*TABLES)
    if save:
        ins += weights[:-1] + [n.nm_old]
    else:
        ins += [n.seg1, n.flat3, n.gnorm] + [old_of(w) for w in weights]
        ins += [moment_of(w) for w in weights]
    kept = for_both(n.joined) + [n.sum_out, n.norms]
    extra = for_both(n.u, n.spec, n.mixed, n.s, n.halo)
    extra += [n.knh, n.knl, n.koh, n.kol, n.g_sq, n.g_fo, n.g_ex]
    if save:
        kept, extra = kept + extra, [n.nm]
    else:
        kept, extra = kept + [n.flat1], extra + weights + [n.zgs, n.zgr]
    scratch = [n.g_nm, n.g_near, n.g_inw, n.g_outw, n.ld]
    scratch += [n.sum_src, n.sum_a, n.sum_z, n.sum_as, n.sum_ar, n.sum_zs, n.sum_zr]
    scratch += [n.g1s, n.g1r, n.t1s, n.t1r, n.t2s, n.t2r, n.t3s, n.t3r, n.hs, n.hr, n.ws, n.wr]
    scratch += extra + for_both(n.maps, n.zh, n.zl, n.act, *SPECTRA)
    return ins, kept, scratch


def forward_far(save):
    return for_both(n.maps) if save else for_both(n.maps, n.halo)


def forward_kernel(bks, A, B, sizes, save, *refs):
    ins, kept, scratch = forward_names(save)
    far = forward_far(save)
    names = ins + [far_of(k) for k in far] + [far_of(k) for k in kept] + kept + scratch
    f = take(names, refs)
    CL, CG, CH, NPd = sizes
    CT = CL + CG
    c = Comm(A, B)
    c.enter()
    keeper = Loader(f.ld)
    for name in far:
        keeper.start(name, getattr(f, far_of(name)), getattr(f, name))
    other = jnp.minimum(c.a, 1)
    once = jnp.where(c.a == 0, 1.0, 2.0)
    cells = [B * bk.H * bk.W for bk in bks]
    freqs = [B * bk.H * (bk.W // 2 + 1) for bk in bks]
    views = [View(f, 0), View(f, 1)]
    both = (0, 1)

    def keep(*which):
        for k in which:
            if k in kept:
                keeper.start(k, getattr(f, k), getattr(f, far_of(k)))

    f.sum_src[...] = jnp.zeros_like(f.sum_src)
    c.entered()
    if not save:
        shares = spread_images(c, f)
        renew_small(f, A, sizes)
    else:
        f.nm[...] = jnp.zeros_like(f.nm)
        f.nm[0:2, :NPd] = f.nm_old[...]
    small = [gather_direct(c, f, name, i) for i, name in enumerate((n.sq, n.nm))]
    if save:
        spread = Spread(c, f, (n.fo, n.ex, n.near, n.inw, n.outw))
        spread.start()
    for q in both:
        bk, g = bks[q], views[q]
        keeper.wait(n.maps + str(q))

        def body(r, carry, bk=bk, g=g):
            src = pl.multiple_of(r * bk.W, bk.W)
            high, low = split(g.maps[pl.ds(src, bk.W), :])
            g.zh[pl.ds(src + bk.W, bk.W), :] = high
            g.zl[pl.ds(src + bk.W, bk.W), :] = low
            return carry

        lax.fori_loop(0, bk.R, body, 0)
    for group in small:
        group.wait_recv()

    wsq = split(f.g_sq[...].reshape(CH, CG))
    keep(n.g_sq)
    adding = [None, None]
    for q in both:
        bk, g = bks[q], views[q]

        def body(r, carry, bk=bk, g=g):
            at = pl.multiple_of(r + bk.W, 32)
            value = dot3((g.zh[pl.ds(at, bk.MB), CL:], g.zl[pl.ds(at, bk.MB), CL:]), wsq, NT)
            g.s[pl.ds(r, bk.MB), :] = value
            return carry[0] + column_sum(value), carry[1] + column_sum(value * value)

        adding[q] = c.sum_start(f, 0, q, chunks(bk.N, bk.MB, body, no_sums(CH)))
        keep(n.s + str(q))
    if save:
        spread.second()

    piece = f.g_nm.shape[2]
    span = pad_to(NPd * A, 128) + 128
    norms = None
    for d in range(A):
        part = jnp.concatenate([f.g_nm[d], jnp.zeros((8, span - piece), f32)], 1)
        if d:
            part = pltpu.roll(part, NPd * d, 1)
        norms = part if norms is None else norms + part
    f.norms[0] = norms[:, :CT]
    f.norms[1] = pltpu.roll(norms, span - CT, 1)[:, :CT]
    f.norms[2] = pltpu.roll(norms, span - CT - CH, 1)[:, :CT]

    keep(n.norms)
    for q in both:
        adding[q] = c.sum_cross(f, 0, q, adding[q])
    if not save:
        shares.wait_recv()
        keep(n.flat1)
        renew_large(f, A, B, sizes)
        small = [gather_direct(c, f, n.fo, 2)]
        spread = Spread(c, f, (n.ex, n.near, n.inw, n.outw))
        spread.start()
    swaps = [None, None]
    for q in both:
        bk, g = bks[q], views[q]
        c.sum_end(f, 0, q, adding[q])
        center, inverse = norm_rows(f.sum_out, 0, q, CH, cells[q])

        def source(h, bk=bk, g=g, center=center, inverse=inverse):
            rows = slice(h * bk.W, (h + 1) * bk.W)
            v = (g.s[rows, :] - center) * inverse * f.norms[1, 0:1, :CH] + f.norms[1, 1:2, :CH]
            value = v * sigmoid(v)
            g.act[rows, :] = value
            return value

        row_transform(bk, g.row, source, g.sendA)
        swaps[q] = c.swap_start(g.sendA, g.recvA, f.ws.at[0, q], f.wr.at[0, q], bk.Cp)

    halos = []
    if save:
        for q in both:
            bk, g = bks[q], views[q]
            halos += c.halo_start(
                g.maps.at[pl.ds(0, bk.W)],
                g.maps.at[pl.ds(bk.N - bk.W, bk.W)],
                g.halo,
                f.hs.at[q],
                f.hr.at[q],
            )
    if save:
        spread.third()
        c.swap_end(swaps[0])
        spread.end()
    else:
        spread.second()
        c.swap_end(swaps[0])
        small[0].wait_recv()
    keep(n.g_fo, n.g_ex)
    wfo = split(f.g_fo[...].reshape(2 * CH, 2 * CH))
    for q in both:
        bk, g = bks[q], views[q]
        if q:
            c.swap_end(swaps[q])

        def put(slot, value, g=g, bk=bk):
            g.spec[slot * bk.H : (slot + 1) * bk.H, :] = value

        col_transform(bk, g.col, g.col0, other, g.recvA, put)
        keep(n.spec + str(q))

        def body(r, carry, bk=bk, g=g):
            value = dot3(split(g.spec[pl.ds(r, bk.Q // 2), :]), wfo, NT)
            g.mixed[pl.ds(r, bk.Q // 2), :] = value
            return carry[0] + column_sum(value), carry[1] + column_sum(value * value)

        adding[q] = c.sum_start(f, 1, q, chunks(bk.Q, bk.Q // 2, body, no_sums(2 * CH)))
        keep(n.mixed + str(q))
    def convolve(q):
        bk, g = bks[q], views[q]
        conv_forward(bk, g.zh, g.zl, f.knh, f.knl, f.koh, f.kol, g.joined)

    def spectra_back(q):
        bk, g = bks[q], views[q]
        c.sum_end(f, 1, q, adding[q])
        center, inverse = norm_rows(f.sum_out, 1, q, 2 * CH, freqs[q])

        def get(slot, g=g, center=center, inverse=inverse, bk=bk):
            value = g.mixed[slot * bk.H : (slot + 1) * bk.H, :]
            v = (value - center) * inverse * f.norms[2, 0:1, : 2 * CH] + f.norms[2, 1:2, : 2 * CH]
            return v * sigmoid(v)

        def scale(b, value):
            return value * (once if b == 0 else 2.0)

        col_back(bk, g.colT, g.col0T, other, get, scale, g.sendB)
        swaps[q] = c.swap_start(g.sendB, g.recvB, f.ws.at[1, q], f.wr.at[1, q], bk.Cp)

    for q in both:
        adding[q] = c.sum_cross(f, 1, q, adding[q])
    if not save:
        spread.third()
    c.halo_end(halos)
    for q in both:
        bk, g = bks[q], views[q]
        if not save:
            keeper.wait(n.halo + str(q))
        for side, at, edge in ((0, 0, 0), (1, bk.N + bk.W, A - 1)):
            if save:
                g.halo[side] = jnp.where(c.a == edge, 0.0, g.halo[side])
            high, low = split(g.halo[side])
            g.zh[pl.ds(at, bk.W), :] = high
            g.zl[pl.ds(at, bk.W), :] = low
        keep(n.halo + str(q))
    if not save:
        spectra_back(0)
        spectra_back(1)
        spread.end()

    def taps(t, carry):
        a, b = t // 3, t % 3
        near = f.g_near[:, pl.ds(t, 1)].reshape(CL, CL)
        inward = f.g_inw[:, pl.ds(t, 1)].reshape(CL, CG)
        high, low = split(jnp.concatenate([near, inward], 1))
        f.knh[b, a] = high
        f.knl[b, a] = low
        return carry

    lax.fori_loop(0, 9, taps, 0)
    for a in range(3):
        for b in range(3):
            high, low = split(f.g_outw[:, 3 * a + b].reshape(CG, CL))
            f.koh[b * CG : (b + 1) * CG, a * CL : (a + 1) * CL] = high
            f.kol[b * CG : (b + 1) * CG, a * CL : (a + 1) * CL] = low
    keep(n.knh, n.knl, n.koh, n.kol)
    if save:
        convolve(0)
        spectra_back(0)
        spectra_back(1)
    convolve(1 if save else 0)
    if not save:
        convolve(1)

    wex = split(f.g_ex[...].reshape(CG, CH))
    for q in both:
        bk, g = bks[q], views[q]
        c.swap_end(swaps[q])
        for h in range(bk.R):
            rows = slice(h * bk.W, (h + 1) * bk.W)
            g.u[rows, :] = g.act[rows, :] + row_back(bk, g.rowT, g.recvB, h)
        keep(n.u + str(q))

        def body(r, carry, bk=bk, g=g):
            rows = pl.ds(r, bk.MB)
            value = g.joined[rows, CL:] + dot3(split(g.u[rows, :]), wex, NT)
            g.joined[rows, CL:] = value
            value = jnp.concatenate([g.joined[rows, :CL], value], 1)
            return carry[0] + column_sum(value), carry[1] + column_sum(value * value)

        adding[q] = c.sum_start(f, 2, q, chunks(bk.N, bk.MB, body, no_sums(CT)))
        keep(n.joined + str(q))
    for q in both:
        adding[q] = c.sum_cross(f, 2, q, adding[q])
    for q in both:
        c.sum_end(f, 2, q, adding[q])
    keep(n.sum_out)
    keeper.wait(*[k for k in keeper.copies if k in kept])
    c.finish()


def renewed(weight, moment, grad):
    return weight - learn_rate * (grad + momentum * (momentum * moment + grad))


def piece_of(flat, A, B, sizes, second, at, count):
    part1, part2 = (rows // B for rows in flat_rows_of(A, B, sizes))
    part, skip = (part2, part1) if second else (part1, 0)
    pieces = []
    while count:
        z, off = divmod(at, part)
        take_now = min(count, part - off)
        start = z * (part1 + part2) + skip + off
        pieces.append(flat[start : start + take_now, :])
        at, count = at + take_now, count - take_now
    return jnp.concatenate(pieces, 0) if len(pieces) > 1 else pieces[0]


def unpack(flat, A, B, sizes, second, at, count, tiles):
    unit = pad_to(count, 8)
    return jnp.concatenate(
        [piece_of(flat, A, B, sizes, second, at + t * unit, count) for t in range(tiles)], 1
    )


def unpack_tap(flat, A, B, sizes, k):
    CL, CG, CH, NPd = sizes
    first = flat_plan(A, sizes)[0]
    o, p, tiles = CL // A, CG // A, (CL + CG) // 128
    return (
        unpack(flat, A, B, sizes, False, first[0] + k * pad_to(o, 8) * tiles, o, tiles),
        unpack(flat, A, B, sizes, False, first[1] + k * pad_to(p, 8), p, CL // 128),
    )


def unpack_squeeze(flat, A, sizes):
    CH, CG = sizes[2], sizes[1]
    o = CH // A
    unit = pad_to(o, 8)
    return jnp.concatenate([flat[t * unit : t * unit + o, :] for t in range(CG // 128)], 1)


def unpack_matrices(flat1, flat3, A, B, sizes):
    CL, CG, CH, NPd = sizes
    first = flat_plan(A, sizes)[0]
    return (
        unpack_squeeze(flat3, A, sizes) if flat3 is not None else None,
        unpack(flat1, A, B, sizes, True, 0, 2 * CH // A, 2 * CH // 128),
        unpack(flat1, A, B, sizes, False, first[2], CG // A, pad_to(CH, 128) // 128)[:, :CH],
    )


def spread_images(c, f):
    part = f.seg1.shape[0]
    mine = pl.ds(pl.multiple_of(c.z * part, 8), part)
    f.flat1[mine, :] = f.seg1[...]
    moves = [
        (f.seg1, f.flat1.at[mine], {n.img: lax.rem(c.z + d, c.B)}) for d in range(1, c.B)
    ]
    return c.group(moves, f.zgs.at[0], f.zgr.at[0], f.flat1.at[pl.ds(0, (c.B - 1) * part)])


def renew_small(f, A, sizes):
    f.sq[...] = renewed(f.sq_old[...], f.sq_moment[...], unpack_squeeze(f.flat3, A, sizes))
    P = sizes[3]
    f.nm[...] = jnp.zeros_like(f.nm)
    f.nm[0:2, :P] = renewed(f.nm_old[...], f.nm_moment[...], f.gnorm[0:2, :P])


def renew_large(f, A, B, sizes):
    CL = sizes[0]
    for k in range(9):
        both, out = unpack_tap(f.flat1, A, B, sizes, k)
        f.near[k] = renewed(f.near_old[k], f.near_moment[k], both[:, :CL])
        f.inw[k] = renewed(f.inw_old[k], f.inw_moment[k], both[:, CL:])
        f.outw[k] = renewed(f.outw_old[k], f.outw_moment[k], out)
    sq, fo, ex = unpack_matrices(f.flat1, None, A, B, sizes)
    f.fo[...] = renewed(f.fo_old[...], f.fo_moment[...], fo)
    f.ex[...] = renewed(f.ex_old[...], f.ex_moment[...], ex)


def forward_shapes(bks, A, B, sizes):
    CL, CG, CH, NPd = sizes
    CT = CL + CG
    sd = {n.sum_out: (6, 8, 128), n.norms: (3, 8, CT)}
    sd[n.knh] = sd[n.knl] = (3, 3, CL, CT)
    sd[n.koh] = sd[n.kol] = (3 * CG, 3 * CL)
    for name, shape in (
        (n.sq, (CH // A, CG)),
        (n.fo, (2 * CH // A, 2 * CH)),
        (n.ex, (CG // A, CH)),
        (n.nm, (8, pad_to(NPd, 128))),
        (n.near, (9, CL // A, CL)),
        (n.inw, (9, CL // A, CG)),
        (n.outw, (9, CG // A, CL)),
    ):
        sd[name] = shape
        sd[whole_of(name)] = (A,) + shape
    sd[n.flat1] = (sum(flat_rows_of(A, B, sizes)), 128)
    sd[n.seg1] = (sum(flat_rows_of(A, B, sizes)) // B, 128)
    for q, bk in enumerate(bks):
        here = {
            n.maps: (bk.N, CT),
            n.up: (bk.N, CT),
            n.joined: (bk.N, CT),
            n.u: (bk.N, CH),
            n.spec: (bk.Q, 2 * CH),
            n.mixed: (bk.Q, 2 * CH),
            n.s: (bk.N, CH),
            n.halo: (2, bk.W, CT),
            n.zh: ((bk.R + 2) * bk.W, CT),
            n.zl: ((bk.R + 2) * bk.W, CT),
            n.act: (bk.N, CH),
        }
        for name in SPECTRA:
            here[name] = (2 * CH // 128, A * bk.Cp, 128)
        for name, shape in here.items():
            sd[name + str(q)] = shape
    sd[n.sum_src] = (6, 8, 128)
    sd[n.sum_a] = (6, A, 8, 128)
    sd[n.sum_z] = (6, B, 8, 128)
    return sd


HALF = {n.knh, n.knl, n.koh, n.kol, n.dth, n.dtl, n.zh, n.zl} | set(for_both(n.zh, n.zl, n.dh, n.dl))


def memory(name, sd, sems):
    if name in sems:
        return pltpu.SemaphoreType.DMA(sems[name])
    return pltpu.VMEM(sd[name], bf16 if name in HALF else f32)


def result(name, sd):
    return jax.ShapeDtypeStruct(sd[name], bf16 if name in HALF else f32)


def sum_sems(A, B):
    return {
        n.sum_as: (6,),
        n.sum_ar: (6,),
        n.sum_zs: (6,),
        n.sum_zr: (6,),
        n.hs: (2, 2),
        n.hr: (2, 2),
        n.ws: (2, 2),
        n.wr: (2, 2),
    }


VM = pl.BlockSpec(memory_space=pltpu.VMEM)
FAR = pl.BlockSpec(memory_space=pl.ANY)


def forward_call(bks, A, B, sizes, save, cid, args):
    sd = forward_shapes(bks, A, B, sizes)
    ins, kept, scratch = forward_names(save)
    sems = sum_sems(A, B)
    far = forward_far(save)
    sems[n.ld] = (len(kept) + len(far),)
    sems[n.g1s] = sems[n.g1r] = (3,)
    for name in (n.t1s, n.t1r, n.t2s, n.t2r):
        sems[name] = (5, 2)
    sems[n.t3s] = sems[n.t3r] = (5,)
    sems[n.zgs] = sems[n.zgr] = (1,)
    results = kept
    macs = sum(bk.N for bk in bks) * 1400000
    res = pl.pallas_call(
        functools.partial(forward_kernel, bks, A, B, sizes, save),
        out_shape=[result(name, sd) for name in results],
        in_specs=[VM] * len(ins) + [FAR] * len(far),
        out_specs=[FAR] * len(kept),
        scratch_shapes=[memory(name, sd, sems) for name in kept + scratch],
        compiler_params=pltpu.CompilerParams(
            collective_id=cid, has_side_effects=True, vmem_limit_bytes=VMEM_LIMIT
        ),
        cost_estimate=pl.CostEstimate(flops=6 * macs, bytes_accessed=40_000_000, transcendentals=0),
        name=n.forward,
    )(*[args[name] for name in ins + far])
    return dict(zip(results, res))


def finish_kernel(counts, *refs):
    maps, joined, sums, norms, outs = refs[0:2], refs[2:4], refs[4], refs[5], refs[6:8]
    for q in (0, 1):
        center, inverse = norm_rows(sums, 2, q, norms.shape[2], counts[q])
        v = (joined[q][...] - center) * inverse * norms[0, 0:1, :] + norms[0, 1:2, :]
        outs[q][...] = maps[q][...] + v * sigmoid(v)


def finish_call(bks, images, maps, fwd):
    N, CT = maps[0].shape
    step = N // 3 if N % 24 == 0 else N
    block = pl.BlockSpec((step, CT), lambda i: (i, 0))
    counts = [images * bk.H * bk.W for bk in bks]
    return pl.pallas_call(
        functools.partial(finish_kernel, counts),
        out_shape=[jax.ShapeDtypeStruct(m.shape, f32) for m in maps],
        grid=(N // step,),
        in_specs=[block] * 4 + [VM] * 2,
        out_specs=[block] * 2,
        compiler_params=pltpu.CompilerParams(vmem_limit_bytes=VMEM_LIMIT),
        cost_estimate=pl.CostEstimate(
            flops=N * CT * 20, bytes_accessed=N * CT * 24, transcendentals=N * CT * 2
        ),
        name=n.finish,
    )(*maps, fwd[n.joined0], fwd[n.joined1], fwd[n.sum_out], fwd[n.norms])


def flat_plan(A, sizes):
    CL, CG, CH, NPd = sizes
    CT = CL + CG

    def rows(count, width):
        return pad_to(count // A, 8) * pad_to(width, 128) // 128

    near, outw = 9 * rows(CL, CT), 9 * rows(CG, CL)
    first = (0, near, near + outw)
    return first, near + outw + rows(CG, CH), rows(2 * CH, 2 * CH), rows(CH, CG)


def flat_rows_of(A, B, sizes):
    first, end1, rows2, rows3 = flat_plan(A, sizes)
    return pad_to(end1, 16 * B), pad_to(rows2, 8 * B)


LATE = for_both(n.joined, n.up) + for_both(n.maps, n.halo, n.u, n.mixed, n.spec, n.s)
LATE += [n.g_fo, n.knh, n.knl, n.koh, n.kol, n.g_sq]


def backward_names():
    ins = [n.sum_out, n.norms, n.g_ex] + for_both(*TABLES)
    outs = []
    kept = [n.seg1, n.flat3, n.gnorm] + for_both(n.back)
    scratch = [n.sum_src, n.sum_a, n.sum_z, n.bsum, n.sum_as, n.sum_ar, n.sum_zs, n.sum_zr]
    scratch += [n.hs, n.hr, n.ws, n.wr, n.ld, n.rs1s, n.rs1r, n.rs2s, n.rs2r, n.rs3s, n.rs3r, n.rs5s, n.rs5r]
    scratch += [n.das, n.dar, n.dzs, n.dzr]
    scratch += [n.dth, n.dtl, n.zh, n.zl, n.gsq, n.gfo]
    scratch += [n.own1, n.sib1, n.far1, n.last1, n.zin1, n.own2, n.far2, n.zin2, n.own3, n.far3, n.zin3]
    scratch += [n.seg1, n.flat3, n.gnorm, n.tot2]
    scratch += for_both(n.dh, n.dl, n.dhalo, n.du, n.dmix, *SPECTRA)
    return ins, outs, kept, scratch


def silu_slope(v):
    sig = sigmoid(v)
    return sig * (1.0 + v * (1.0 - sig))


class Reduce:
    def __init__(self, c, f):
        self.c, self.f = c, f
        self.own, self.sib, self.far, self.last = f.own1, f.sib1, f.far1, f.last1
        self.zin = f.zin1
        self.rows = self.own.shape[1]
        self.nc = c.A // 2
        self.chip, self.core = c.a // 2, c.a % 2
        self.Y, self.X = grid_of(self.nc)
        self.y, self.x = self.chip // self.X, lax.rem(self.chip, self.X)

    def to_sibling(self):
        f, c = self.f, self.c
        other = 1 - self.core
        moves = [
            (self.own.at[2 * cc + other], self.sib.at[cc], {n.ha: 2 * self.chip + other})
            for cc in range(self.nc)
        ]
        self.copies = [c.group(moves, f.rs1s.at[0], f.rs1r.at[0], self.sib.at[pl.ds(0, self.nc)])]

    def device(self, dy, dx):
        y, x = lax.rem(self.y + dy + self.Y, self.Y), lax.rem(self.x + dx + self.X, self.X)
        return 2 * (y * self.X + x) + self.core

    def lines(self, half, first):
        along_x = (half == 0) == first
        return [(0, d) for d in range(1, self.X)] if along_x else [(d, 0) for d in range(1, self.Y)]

    def part(self, half):
        h = self.rows // 2
        return pl.ds(half * h, h)

    def to_lines(self):
        f, c = self.f, self.c
        for copy in self.copies:
            copy.wait_recv()
        for dy in range(self.Y):
            for dx in range(self.X):
                t = self.device(dy, dx)
                self.own[t] = self.own[t] + self.sib[t // 2]
        self.copies = []
        for half in (0, 1):
            rest = [(0, 0)] + self.lines(half, False)
            moves = []
            for k, (dy, dx) in enumerate(self.lines(half, True)):
                for j, (ry, rx) in enumerate(rest):
                    t = self.device(dy + ry, dx + rx)
                    moves.append(
                        (
                            self.own.at[t, self.part(half)],
                            self.far.at[half, k * len(rest) + j],
                            {n.ha: self.device(dy, dx)},
                        )
                    )
            if moves:
                landed = self.far.at[half, pl.ds(0, len(moves))]
                self.copies.append(c.group(moves, f.rs2s.at[half], f.rs2r.at[half], landed))

    def to_owners(self):
        f, c = self.f, self.c
        for copy in self.copies:
            copy.wait_recv()
        self.copies = []
        for half in (1, 0):
            rows = self.part(half)
            rest = [(0, 0)] + self.lines(half, False)
            lines = self.lines(half, True)
            moves = []
            for j, (ry, rx) in enumerate(rest):
                t = self.device(ry, rx)
                total = self.own[t, rows, :]
                for k in range(len(lines)):
                    total = total + self.far[half, k * len(rest) + j]
                self.own[t, rows, :] = total
                if j:
                    moves.append((self.own.at[t, rows], self.last.at[half, j], {n.ha: t}))
            if moves:
                landed = self.last.at[half, pl.ds(1, len(moves))]
                self.copies.append(c.group(moves, f.rs5s.at[half], f.rs5r.at[half], landed))

    def to_images(self):
        f, c = self.f, self.c
        for copy in self.copies:
            copy.wait_recv()
        for half in (0, 1):
            rows = self.part(half)
            total = self.own[c.a, rows, :]
            for j in range(1, 1 + len(self.lines(half, False))):
                total = total + self.last[half, j]
            self.own[c.a, rows, :] = total
        self.copies = to_images(c, self.own.at[c.a], self.zin, f.rs3s.at[0], f.rs3r.at[0])


def to_images(c, total, zin, ssem, rsem):
    part = total.shape[0] // c.B
    moves = []
    for d in range(1, c.B):
        zz = lax.rem(c.z + d, c.B)
        piece = total.at[pl.ds(pl.multiple_of(zz * part, 8), part)]
        moves.append((piece, zin.at[d], {n.img: zz}))
    return [c.group(moves, ssem, rsem, zin.at[pl.ds(1, c.B - 1)])] if moves else []


def from_images(c, copies, total, zin, out):
    for copy in copies:
        copy.wait_recv()
    part = total.shape[0] // c.B
    value = total[pl.ds(pl.multiple_of(c.z * part, 8), part), :]
    for d in range(1, c.B):
        value = value + zin[d]
    out[...] = value


class Direct:
    def __init__(self, c, f, k, own, far):
        self.c, self.f, self.k = c, f, k
        self.own, self.far = own, far

    def start(self):
        c, f = self.c, self.f
        moves = []
        for d in range(1, c.A):
            t = lax.rem(c.a + d, c.A)
            moves.append((self.own.at[t], self.far.at[d], {n.ha: t}))
        landed = self.far.at[pl.ds(1, c.A - 1)]
        self.copies = c.group(moves, f.das.at[self.k], f.dar.at[self.k], landed)

    def owned(self):
        self.copies.wait_recv()
        total = self.own[self.c.a]
        for d in range(1, self.c.A):
            total = total + self.far[d]
        return total

    def cross(self, zin):
        c, f = self.c, self.f
        zin[c.z] = self.owned()
        mine = zin.at[c.z]
        moves = [(mine, mine, {n.img: lax.rem(c.z + d, c.B)}) for d in range(1, c.B)]
        self.copies = []
        if moves:
            landed = zin.at[pl.ds(0, c.B - 1)]
            self.copies = [c.group(moves, f.dzs.at[0], f.dzr.at[0], landed)]

    def end(self, zin, out):
        for copy in self.copies:
            copy.wait_recv()
        total = zin[0]
        for d in range(1, self.c.B):
            total = total + zin[d]
        out[...] = total


def backward_kernel(bks, A, B, sizes, *refs):
    ins, outs, kept, scratch = backward_names()
    near = ins + [far_of(name) for name in LATE] + [far_of(name) for name in kept]
    f = take(near + LATE + scratch, refs)
    CL, CG, CH, NPd = sizes
    CT = CL + CG
    c = Comm(A, B)
    c.enter()
    loader = Loader(f.ld)
    for name in LATE:
        loader.start(name, getattr(f, far_of(name)), getattr(f, name))
    other = jnp.minimum(c.a, 1)
    once = jnp.where(c.a == 0, 1.0, 2.0)
    cells = [B * bk.H * bk.W for bk in bks]
    freqs = [B * bk.H * (bk.W // 2 + 1) for bk in bks]
    views = [View(f, 0), View(f, 1)]
    both = (0, 1)
    sums = take(
        (n.sum_src, n.sum_a, n.sum_z, n.sum_as, n.sum_ar, n.sum_zs, n.sum_zr, n.sum_out),
        (f.sum_src, f.sum_a, f.sum_z, f.sum_as, f.sum_ar, f.sum_zs, f.sum_zr, f.bsum),
    )
    f.sum_src[...] = jnp.zeros_like(f.sum_src)
    adding, swaps = [None, None], [None, None]

    for q in both:
        bk, g = bks[q], views[q]
        center, inverse = norm_rows(f.sum_out, 2, q, CT, cells[q])
        loader.wait(n.joined + str(q), n.up + str(q))

        def body(r, carry, g=g, center=center, inverse=inverse):
            rows = pl.ds(r, 32)
            x = (g.joined[rows, :] - center) * inverse
            dy = g.up[rows, :] * silu_slope(x * f.norms[0, 0:1, :] + f.norms[0, 1:2, :])
            g.up[rows, :] = dy
            return carry[0] + column_sum(dy), carry[1] + column_sum(dy * x)

        total = chunks(bk.N, 32, body, no_sums(CT))
        if q == 0:
            c.entered()
        adding[q] = c.sum_start(sums, 0, q, total)
    for q in both:
        adding[q] = c.sum_cross(sums, 0, q, adding[q])

    wex = split(f.g_ex[...].reshape(CG, CH))
    halos = []
    for q in both:
        bk, g = bks[q], views[q]
        c.sum_end(sums, 0, q, adding[q])
        center, inverse = norm_rows(f.sum_out, 2, q, CT, cells[q])
        gain = f.norms[0, 0:1, :] * inverse
        m1, m2 = (value * (1.0 / cells[q]) for value in totals(f.bsum, 0, q, CT))

        def body(r, carry, bk=bk, g=g, center=center, inverse=inverse, gain=gain, m1=m1, m2=m2):
            rows = pl.ds(r, 32)
            x = (g.joined[rows, :] - center) * inverse
            dz = gain * (g.up[rows, :] - m1 - x * m2)
            g.up[rows, :] = dz
            high, low = split(dz)
            at = pl.ds(pl.multiple_of(r + bk.W, 32), 32)
            g.dh[at, :] = high
            g.dl[at, :] = low
            return carry

        chunks(bk.N, 32, body, 0)
        halos += c.halo_start(
            g.up.at[pl.ds(0, bk.W)],
            g.up.at[pl.ds(bk.N - bk.W, bk.W)],
            g.dhalo,
            f.hs.at[q],
            f.hr.at[q],
        )

        def body2(r, carry, bk=bk, g=g):
            at = pl.ds(pl.multiple_of(r + bk.W, 32), bk.MB)
            g.du[pl.ds(r, bk.MB), :] = dot3((g.dh[at, CL:], g.dl[at, CL:]), wex, NN)
            return carry

        chunks(bk.N, bk.MB, body2, 0)
        row_transform(bk, g.row, lambda h, g=g, bk=bk: g.du[h * bk.W : (h + 1) * bk.W, :], g.sendA)
        swaps[q] = c.swap_start(g.sendA, g.recvA, f.ws.at[0, q], f.wr.at[0, q], bk.Cp)

    first, end1, rows2, rows3 = flat_plan(A, sizes)
    units = (pad_to(CL // A, 8) * (CT // 128), pad_to(CG // A, 8))

    def pack(own, at, value, more):
        rows = value.shape[0] // A
        for t in range(A):
            for k in range(value.shape[1] // 128):
                piece = value[t * rows : (t + 1) * rows, 128 * k : 128 * (k + 1)]
                to = pl.ds(at + k * pad_to(rows, 8), rows)
                own[t, to, :] = own[t, to, :] + piece if more else piece

    def kernel_gradients(q):
        bk, g = bks[q], views[q]
        step = min(bk.N, 384)
        col = lax.broadcasted_iota(jnp.int32, (step, 1), 0) % bk.W
        for i in range(bk.N // step):
            for t in range(CT // 128):
                value = g.up[i * step : (i + 1) * step, 128 * t : 128 * (t + 1)]
                moved = (
                    jnp.where(col == bk.W - 1, 0.0, pltpu.roll(value, step - 1, 0)),
                    value,
                    jnp.where(col == 0, 0.0, pltpu.roll(value, 1, 0)),
                )
                for b in range(3):
                    high, low = split(jnp.transpose(moved[b]))
                    at = b * CL if t == 0 else 3 * CL + b * CG + 128 * (t - 1)
                    f.dth[at : at + 128, i * step : (i + 1) * step] = high
                    f.dtl[at : at + 128, i * step : (i + 1) * step] = low
        loader.wait(n.maps + str(q), n.halo + str(q), n.u + str(q))

        def body(r, carry):
            src = pl.multiple_of(r * bk.W, bk.W)
            high, low = split(g.maps[pl.ds(src, bk.W), :])
            f.zh[pl.ds(src + bk.W, bk.W), :] = high
            f.zl[pl.ds(src + bk.W, bk.W), :] = low
            return carry

        lax.fori_loop(0, bk.R, body, 0)
        for side, at in ((0, 0), (1, bk.N + bk.W)):
            high, low = split(g.halo[side])
            f.zh[pl.ds(at, bk.W), :] = high
            f.zl[pl.ds(at, bk.W), :] = low

        def taps(a, carry):
            rows = pl.ds(pl.multiple_of(a * bk.W, 32), bk.N)
            right = (f.zh[rows, :], f.zl[rows, :])
            out = dot3((f.dth[: 3 * CL, :], f.dtl[: 3 * CL, :]), right, NN)
            for b in range(3):
                at = pl.multiple_of(first[0] + (3 * a + b) * units[0], 8)
                pack(f.own1, at, out[b * CL : (b + 1) * CL], q)
            right = (f.zh[rows, :CL], f.zl[rows, :CL])
            for b in range(3):
                at = 3 * CL + b * CG
                value = dot3((f.dth[at : at + CG, :], f.dtl[at : at + CG, :]), right, NN)
                at = pl.multiple_of(first[1] + (3 * a + b) * units[1], 8)
                pack(f.own1, at, value, q)
            return carry

        lax.fori_loop(0, 3, taps, 0)
        at = 3 * CL + CG
        value = dot3((f.dth[at : at + CG, :], f.dtl[at : at + CG, :]), split(g.u[...]), NN)
        value = jnp.concatenate([value, jnp.zeros((CG, pad_to(CH, 128) - CH), f32)], 1)
        pack(f.own1, first[2], value, q)

    def spectra_slopes(q):
        bk, g = bks[q], views[q]
        loader.wait(n.mixed + str(q))
        c.swap_end(swaps[q])
        center, inverse = norm_rows(f.sum_out, 1, q, 2 * CH, freqs[q])
        carry = [no_sums(2 * CH)]

        def put(slot, value):
            rows = slice(slot * bk.H, (slot + 1) * bk.H)
            x = (g.mixed[rows, :] - center) * inverse
            value = value * (once if slot in (0, bk.nb) else 2.0)
            dy = value * silu_slope(x * f.norms[2, 0:1, : 2 * CH] + f.norms[2, 1:2, : 2 * CH])
            g.dmix[rows, :] = dy
            carry[0] = (carry[0][0] + column_sum(dy), carry[0][1] + column_sum(dy * x))

        col_transform(bk, g.col, g.col0, other, g.recvA, put)
        adding[q] = c.sum_start(sums, 1, q, carry[0])

    def spectra_back(q, wfo):
        bk, g = bks[q], views[q]
        c.sum_end(sums, 1, q, adding[q])
        center, inverse = norm_rows(f.sum_out, 1, q, 2 * CH, freqs[q])
        gain = f.norms[2, 0:1, : 2 * CH] * inverse
        m1, m2 = (value * (1.0 / freqs[q]) for value in totals(f.bsum, 1, q, 2 * CH))

        def get(slot):
            rows = slice(slot * bk.H, (slot + 1) * bk.H)
            x = (g.mixed[rows, :] - center) * inverse
            dz = gain * (g.dmix[rows, :] - m1 - x * m2)
            g.dmix[rows, :] = dz
            return dot3(split(dz), wfo, NN)

        col_back(bk, g.colT, g.col0T, other, get, lambda b, v: v, g.sendB)
        swaps[q] = c.swap_start(g.sendB, g.recvB, f.ws.at[1, q], f.wr.at[1, q], bk.Cp)

    kernel_gradients(0)
    spectra_slopes(0)
    kernel_gradients(1)
    adding[0] = c.sum_cross(sums, 1, 0, adding[0])
    if f.own1.shape[1] > end1:
        f.own1[:, end1:, :] = jnp.zeros((A, f.own1.shape[1] - end1, 128), f32)
    red1 = Reduce(c, f)
    red1.to_sibling()
    spectra_slopes(1)
    loader.wait(n.g_fo)
    wfo = split(f.g_fo[...].reshape(2 * CH, 2 * CH))
    adding[1] = c.sum_cross(sums, 1, 1, adding[1])
    red1.to_lines()
    spectra_back(0, wfo)
    spectra_back(1, wfo)
    for q in both:
        bk, g = bks[q], views[q]
        loader.wait(n.spec + str(q))
        value = dot3(split(jnp.transpose(g.dmix[...])), split(g.spec[...]), NN)
        f.gfo[...] = value if q == 0 else f.gfo[...] + value
    pack(f.own2, 0, f.gfo, 0)
    red2 = Direct(c, f, 0, f.own2, f.far2)

    c.halo_end(halos)
    c.halo_sent()
    loader.wait(n.knh, n.knl, n.koh, n.kol)

    def input_gradients(q):
        bk, g = bks[q], views[q]
        for side, at, edge in ((0, 0, 0), (1, bk.N + bk.W, A - 1)):
            high, low = split(jnp.where(c.a == edge, 0.0, g.dhalo[side]))
            g.dh[pl.ds(at, bk.W), :] = high
            g.dl[pl.ds(at, bk.W), :] = low
        conv_backward(bk, g.dh, g.dl, f.knh, f.knl, f.koh, f.kol, g.up)

    def active_slopes(q):
        bk, g = bks[q], views[q]
        loader.wait(n.s + str(q))
        c.swap_end(swaps[q])
        center, inverse = norm_rows(f.sum_out, 0, q, CH, cells[q])
        total = no_sums(CH)
        for h in range(bk.R):
            rows = slice(h * bk.W, (h + 1) * bk.W)
            x = (g.s[rows, :] - center) * inverse
            value = g.du[rows, :] + row_back(bk, g.rowT, g.recvB, h)
            dy = value * silu_slope(x * f.norms[1, 0:1, :CH] + f.norms[1, 1:2, :CH])
            g.du[rows, :] = dy
            total = (total[0] + column_sum(dy), total[1] + column_sum(dy * x))
        adding[q] = c.sum_start(sums, 2, q, total)

    def squeeze_back(q, wsq):
        bk, g = bks[q], views[q]
        c.sum_end(sums, 2, q, adding[q])
        center, inverse = norm_rows(f.sum_out, 0, q, CH, cells[q])
        gain = f.norms[1, 0:1, :CH] * inverse
        m1, m2 = (value * (1.0 / cells[q]) for value in totals(f.bsum, 2, q, CH))

        def body(r, carry):
            rows = pl.ds(r, bk.MB)
            x = (g.s[rows, :] - center) * inverse
            dz = gain * (g.du[rows, :] - m1 - x * m2)
            g.du[rows, :] = dz
            g.up[rows, CL:] += dot3(split(dz), wsq, NN)
            return carry

        chunks(bk.N, bk.MB, body, 0)
        value = dot3(split(jnp.transpose(g.du[...])), split(g.maps[:, CL:]), NN)
        f.gsq[...] = value if q == 0 else f.gsq[...] + value

    input_gradients(0)
    red1.to_owners()
    input_gradients(1)
    active_slopes(0)
    active_slopes(1)
    loader.wait(n.g_sq)
    wsq = split(f.g_sq[...].reshape(CH, CG))
    for q in both:
        adding[q] = c.sum_cross(sums, 2, q, adding[q])
    red1.to_images()
    red2.start()
    squeeze_back(0, wsq)
    squeeze_back(1, wsq)
    for q in both:
        name = n.back + str(q)
        loader.start(name, views[q].up, getattr(f, far_of(name)))
    pack(f.own3, 0, f.gsq, 0)
    red3 = Direct(c, f, 1, f.own3, f.far3)
    red3.start()
    f.tot2[: f.own2.shape[1], :] = red2.owned()
    if f.tot2.shape[0] > f.own2.shape[1]:
        f.tot2[f.own2.shape[1] :, :] = jnp.zeros((f.tot2.shape[0] - f.own2.shape[1], 128), f32)
    copies2 = to_images(c, f.tot2, f.zin2, f.rs3s.at[1], f.rs3r.at[1])

    span = pad_to(NPd * A, 128) + 128
    lane = lax.broadcasted_iota(jnp.int32, (8, span), 1)
    out = []
    for i in (1, 0):
        rows = []
        for k, width in ((0, CT), (1, 2 * CH), (2, CH)):
            pair = [totals(f.bsum, k, q, CT)[i] for q in both]
            row = jnp.concatenate([pair[0] + pair[1], jnp.zeros((1, span - CT), f32)], 1)
            rows.append(jnp.where(lane < width, jnp.broadcast_to(row, (8, span)), 0.0))
        out.append(rows[0] + pltpu.roll(rows[2], CT, 1) + pltpu.roll(rows[1], CT + CH, 1))
    sub = lax.broadcasted_iota(jnp.int32, (8, span), 0)
    value = pltpu.roll(jnp.where(sub == 0, out[0], out[1]), lax.rem(span - NPd * c.a, span), 1)
    f.gnorm[...] = value[:, : f.gnorm.shape[1]]

    def keep(name):
        loader.start(name, getattr(f, name), getattr(f, far_of(name)))

    keep(n.gnorm)
    red3.cross(f.zin3)
    part1 = f.zin1.shape[1]
    from_images(c, red1.copies, f.own1.at[c.a], f.zin1, f.seg1.at[pl.ds(0, part1)])
    from_images(c, copies2, f.tot2, f.zin2, f.seg1.at[pl.ds(part1, f.zin2.shape[1])])
    keep(n.seg1)
    red3.end(f.zin3, f.flat3)
    keep(n.flat3)
    loader.wait(*kept)
    c.finish()


def conv_backward(bk, dh, dl, knh, knl, koh, kol, out):
    MB, W = bk.MB, bk.W
    CL = knh.shape[2]
    CG = koh.shape[0] // 3
    CT = knh.shape[3]
    col = lax.broadcasted_iota(jnp.int32, (MB, 1), 0) % W

    def moved(value, b):
        if b == 0:
            return jnp.where(col == W - 1, 0.0, pltpu.roll(value, MB - 1, 0))
        if b == 2:
            return jnp.where(col == 0, 0.0, pltpu.roll(value, 1, 0))
        return value

    def body(i, carry):
        r = pl.multiple_of(i * MB, 32)
        rows = [pl.ds(pl.multiple_of(r + (2 - a) * W, 32), MB) for a in range(3)]
        left = tuple(jnp.concatenate([d[rows[a], :CL] for a in range(3)], 1) for d in (dh, dl))
        total = None
        for b in (1, 0, 2):
            right = (knh[b].reshape(3 * CL, CT), knl[b].reshape(3 * CL, CT))
            value = moved(dot3(left, right, NN), b)
            total = value if total is None else total + value
        out[pl.ds(r, MB), :] = total
        cross = None
        for a in range(3):
            left2 = (dh[rows[a], CL:], dl[rows[a], CL:])
            right = tuple(
                jnp.concatenate(
                    [k[b * CG : (b + 1) * CG, a * CL : (a + 1) * CL] for b in range(3)], 1
                )
                for k in (koh, kol)
            )
            value = dot3(left2, right, NN)
            cross = value if cross is None else cross + value
        total = None
        for b in range(3):
            value = moved(cross[:, b * CL : (b + 1) * CL], b)
            total = value if total is None else total + value
        out[pl.ds(r, MB), :CL] += total
        return carry

    lax.fori_loop(0, bk.N // MB, body, 0)


def backward_call(bks, A, B, sizes, cid, args):
    CL, CG, CH, NPd = sizes
    CT = CL + CG
    nc = A // 2
    first, end1, rows2, rows3 = flat_plan(A, sizes)
    rows1, padded2 = flat_rows_of(A, B, sizes)
    N = max(bk.N for bk in bks)
    big = max((bk.R + 2) * bk.W for bk in bks)
    sd = forward_shapes(bks, A, B, sizes)
    sd[n.bsum] = sd[n.sum_src]
    sd[n.gnorm] = (8, pad_to(NPd, 128))
    sd[n.dth] = sd[n.dtl] = (3 * CT, N)
    sd[n.zh] = sd[n.zl] = (big, CT)
    sd[n.gsq], sd[n.gfo] = (CH, CG), (2 * CH, 2 * CH)
    sd[n.own1], sd[n.zin1] = (A, rows1, 128), (B, rows1 // B, 128)
    sd[n.sib1] = (nc, rows1, 128)
    sd[n.far1] = (2, nc, rows1 // 2, 128)
    sd[n.last1] = (2, max(grid_of(nc)), rows1 // 2, 128)
    sd[n.tot2], sd[n.zin2] = (padded2, 128), (B, padded2 // B, 128)
    sd[n.own2] = sd[n.far2] = (A, rows2, 128)
    sd[n.flat3], sd[n.zin3] = (rows3, 128), (B, rows3, 128)
    sd[n.own3] = sd[n.far3] = (A, rows3, 128)
    for q, bk in enumerate(bks):
        here = {
            n.back: (bk.N, CT),
            n.dh: ((bk.R + 2) * bk.W, CT),
            n.dl: ((bk.R + 2) * bk.W, CT),
            n.dhalo: (2, bk.W, CT),
            n.du: (bk.N, CH),
            n.dmix: (bk.Q, 2 * CH),
        }
        for name, shape in here.items():
            sd[name + str(q)] = shape
    ins, outs, kept, scratch = backward_names()
    results = outs + kept
    sems = sum_sems(A, B)
    sems[n.ld] = (len(LATE) + len(kept),)
    for name in (n.rs1s, n.rs1r, n.dzs, n.dzr):
        sems[name] = (1,)
    for name in (n.rs2s, n.rs2r, n.rs3s, n.rs3r, n.rs5s, n.rs5r, n.das, n.dar):
        sems[name] = (2,)
    macs = sum(bk.N for bk in bks) * 2800000
    res = pl.pallas_call(
        functools.partial(backward_kernel, bks, A, B, sizes),
        out_shape=[result(name, sd) for name in results],
        in_specs=[VM] * len(ins) + [FAR] * len(LATE),
        out_specs=[VM] * len(outs) + [FAR] * len(kept),
        scratch_shapes=[memory(name, sd, sems) for name in LATE + scratch],
        compiler_params=pltpu.CompilerParams(
            collective_id=cid, has_side_effects=True, vmem_limit_bytes=VMEM_LIMIT
        ),
        cost_estimate=pl.CostEstimate(flops=6 * macs, bytes_accessed=40_000_000, transcendentals=0),
        name=n.backward,
    )(*[args[name] for name in ins + LATE])
    return dict(zip(results, res))


def update_kernel(A, B, sizes, *refs):
    CL, CG, CH, NPd = sizes
    flat1, flat3, gnorm = refs[:3]
    weights, moments, averages = refs[3:10], refs[10:17], refs[17:24]
    updated, velocity, smoothed, half = refs[24:31], refs[31:38], refs[38:45], refs[45:52]
    decay = min(0.5, (1.0 + STEP) / (10.0 + STEP))

    def step(i, at, grad):
        new = renewed(weights[i][at], moments[i][at], grad)
        velocity[i][at] = momentum * moments[i][at] + grad
        updated[i][at] = new
        smoothed[i][at] = decay * averages[i][at] + (1.0 - decay) * new
        half[i][at] = new.astype(bf16)

    for k in range(9):
        both, out = unpack_tap(flat1, A, B, sizes, k)
        step(0, k, both[:, :CL])
        step(1, k, both[:, CL:])
        step(2, k, out)
    every = slice(None)
    for i, grad in zip((3, 4, 5), unpack_matrices(flat1, flat3, A, B, sizes)):
        step(i, every, grad)
    step(6, every, gnorm[0:2, :NPd])


def update_call(A, B, sizes, grads, weights, moments, averages):
    shapes = [w.shape for w in weights]
    outs = [jax.ShapeDtypeStruct(s, f32) for _ in range(3) for s in shapes]
    outs += [jax.ShapeDtypeStruct(s, bf16) for s in shapes]
    res = pl.pallas_call(
        functools.partial(update_kernel, A, B, sizes),
        out_shape=outs,
        in_specs=[VM] * 24,
        out_specs=[VM] * len(outs),
        compiler_params=pltpu.CompilerParams(vmem_limit_bytes=VMEM_LIMIT),
        cost_estimate=pl.CostEstimate(flops=3_000_000, bytes_accessed=5_000_000, transcendentals=0),
        name=n.update,
    )(*grads, *weights, *moments, *averages)
    return res[0:7], res[7:14], res[14:21], res[21:28]


def as_rows(weight):
    return jnp.transpose(weight[0], (0, 1, 3, 2)).reshape(9, weight.shape[4], weight.shape[3])


def from_rows(value):
    return jnp.transpose(value.reshape(1, 3, 3, value.shape[1], value.shape[2]), (0, 1, 2, 4, 3))


def flat_rows(weight):
    return jnp.transpose(weight[0])


def from_flat(value):
    return jnp.transpose(value)[None]


def per_device(*arrays):
    A, B = lax.axis_size("ha"), lax.axis_size("img")
    maps, ups = arrays[0:2], arrays[2:4]
    groups = [arrays[4 + i :: 3] for i in range(3)]
    to_local = (as_rows,) * 3 + (flat_rows,) * 3 + (lambda w: w[0],)
    weights, moments, averages = (
        [change(w) for change, w in zip(to_local, group)] for group in groups
    )
    bks = [Bucket(m.shape[1], m.shape[2], A) for m in maps]
    CL, CG, CH, NPd = weights[0].shape[2], weights[1].shape[2], weights[5].shape[1], weights[6].shape[1]
    sizes = (CL, CG, CH, NPd)
    CT = CL + CG
    args = {}
    for q in (0, 1):
        args[n.maps + str(q)] = maps[q].reshape(-1, CT)
        args[n.up + str(q)] = ups[q].reshape(-1, CT)
        for name, table in zip(TABLES, tables_of(bks[q])):
            args[name + str(q)] = jnp.asarray(table)
    flat_maps = [args[n.maps0], args[n.maps1]]
    args.update(zip(KINDS, weights))
    args[old_of(n.nm)] = weights[6]
    fwd = forward_call(bks, A, B, sizes, True, 1, args)
    block = finish_call(bks, B, flat_maps, fwd)
    bwd = backward_call(bks, A, B, sizes, 2, {**args, **fwd})
    back = [args[n.up + str(q)] + bwd[n.back + str(q)] for q in (0, 1)]
    again = {**args, **bwd, n.halo0: fwd[n.halo0], n.halo1: fwd[n.halo1]}
    for name, weight, moment in zip(KINDS, weights, moments):
        again[old_of(name)] = weight
        again[moment_of(name)] = moment
    fresh = forward_call(bks, A, B, sizes, False, 3, again)
    grads = (fresh[n.flat1], bwd[n.flat3], bwd[n.gnorm])
    updated, velocity, smoothed, half = update_call(A, B, sizes, grads, weights, moments, averages)
    rerun = finish_call(bks, B, flat_maps, fresh)
    out = []
    for pair in (block, back, rerun):
        out += [value.reshape(m.shape) for value, m in zip(pair, maps)]
    to_outer = (from_rows,) * 3 + (from_flat,) * 3 + (lambda w: w[None],)
    for i in range(7):
        out += [to_outer[i](group[i]) for group in (updated, velocity, smoothed, half)]
    return tuple(out)


def solution(mesh):
    cells = P("img", "ha", None, None)
    kernel = P(None, None, None, None, "ha")
    matrix = P(None, None, "ha")
    return jax.shard_map(
        per_device,
        mesh=mesh,
        in_specs=(cells,) * 4 + (kernel,) * 9 + (matrix,) * 12,
        out_specs=(cells,) * 6 + (kernel,) * 12 + (matrix,) * 16,
        check_vma=False,
    )
```

```python
import functools
import math

import jax
import jax.numpy as jnp
import numpy as np
from jax import lax
from jax.experimental import pallas as pl
from jax.experimental.pallas import tpu as pltpu
from jax.sharding import PartitionSpec as P

STEP = 6

epsilon = 1e-05
learn_rate = 3e-05
momentum = 0.5

f32 = jnp.float32
bf16 = jnp.bfloat16
MESH = pl.DeviceIdType.MESH
VMEM_LIMIT = 60 * 1024 * 1024

NN = (((1,), (0,)), ((), ()))
NT = (((1,), (1,)), ((), ()))
TN = (((0,), (0,)), ((), ()))


def dg(left, right, dims):
    return lax.dot_general(left, right, dims, preferred_element_type=f32)


def split(value):
    high = value.astype(bf16)
    return high, (value - high.astype(f32)).astype(bf16)


def dot3(left, right, dims):
    lh, ll = left
    rh, rl = right
    return dg(lh, rh, dims) + dg(ll, rh, dims) + dg(lh, rl, dims)


def sigmoid(v):
    return 1.0 / (1.0 + jnp.exp(-v))


def pad_to(n, m):
    return -(-n // m) * m


def chunks(count, step, body, carry):
    def run(i, carry):
        return body(pl.multiple_of(i * step, 8), carry)

    return lax.fori_loop(0, count // step, run, carry)


class Bucket:
    def __init__(self, rows, width, group):
        self.R, self.W, self.A = rows, width, group
        self.H = rows * group
        self.N = rows * width
        self.nb = -(-(width // 2) // group)
        self.Cp = pad_to(self.nb * rows, 8)
        self.Q = (self.nb + 1) * self.H
        self.MB = max(r * width for r in range(1, rows + 1) if rows % r == 0 and r * width <= 384)


def hi_lo(table):
    table = np.asarray(table, np.float64)
    high = table.astype(np.float32).astype(jnp.bfloat16)
    low = (table - high.astype(np.float64)).astype(np.float32).astype(jnp.bfloat16)
    return np.stack([high, low])


def tables_of(bk):
    A, nb, W, H, R = bk.A, bk.nb, bk.W, bk.H, bk.R
    row = np.zeros((2, nb, A, W))
    w = np.arange(W)
    for b in range(nb):
        for d in range(A):
            j = d * nb + b
            if j == 0:
                row[0, b, d] = 1.0
                row[1, b, d] = np.cos(math.pi * w)
            elif 2 * j < W:
                row[0, b, d] = np.cos(2 * math.pi * (j * w % W) / W)
                row[1, b, d] = -np.sin(2 * math.pi * (j * w % W) / W)
    row = row.reshape(2 * nb * A, W) / math.sqrt(W)
    k = np.arange(H)[:, None]
    h = np.array([s * R + r for r in range(R) for s in range(A)])[None, :]
    phase = 2 * math.pi * (k * h % H) / H
    cos, sin = np.cos(phase) / math.sqrt(H), np.sin(phase) / math.sqrt(H)
    none = np.zeros_like(cos)
    plain = np.block([[cos, sin], [-sin, cos]])
    packed = np.block([[cos, none], [-sin, none], [none, cos], [none, -sin]])
    other = np.concatenate([plain, np.zeros_like(plain)], 0)
    first = np.stack([hi_lo(packed), hi_lo(other)])
    return (
        hi_lo(row),
        hi_lo(row.T),
        hi_lo(plain),
        hi_lo(plain.T),
        first,
        np.swapaxes(first, 2, 3),
    )


class Names:
    def __getattr__(self, name):
        return name


n = Names()
TABLES = (n.row, n.rowT, n.col, n.colT, n.col0, n.col0T)
SPECTRA = (n.sendA, n.recvA, n.sendB, n.recvB)


def for_both(*names):
    return [name + str(q) for q in (0, 1) for name in names]


class View:
    def __init__(self, refs, q):
        self.refs, self.q = refs, q

    def __getattr__(self, name):
        return getattr(self.refs, name + str(self.q))


class Fields:
    pass


def take(names, refs):
    out = Fields()
    for name, ref in zip(names, refs):
        setattr(out, name, ref)
    return out


class Group:
    def __init__(self, ssem, rsem, landed):
        self.ssem, self.rsem, self.landed = ssem, rsem, landed

    def wait_recv(self):
        pltpu.make_async_copy(self.landed, self.landed, self.rsem).wait()

    def wait_send(self):
        pltpu.make_async_copy(self.landed, self.landed, self.ssem).wait()


class Comm:
    def __init__(self, A, B):
        self.A, self.B = A, B
        self.a = lax.axis_index("ha")
        self.z = lax.axis_index("img")
        self.pending, self.halos = [], []

    def enter(self):
        bar = pltpu.get_barrier_semaphore()
        for d in range(1, self.A):
            pl.semaphore_signal(
                bar, inc=1, device_id=(self.z, lax.rem(self.a + d, self.A)), device_id_type=MESH
            )
        for d in range(1, self.B):
            pl.semaphore_signal(
                bar, inc=1, device_id=(lax.rem(self.z + d, self.B), self.a), device_id_type=MESH
            )

    def entered(self):
        pl.semaphore_wait(pltpu.get_barrier_semaphore(), self.A + self.B - 2)

    def make(self, src, dst, ssem, rsem, ha=None, img=None):
        return pltpu.make_async_remote_copy(
            src,
            dst,
            ssem,
            rsem,
            device_id=(self.z if img is None else img, self.a if ha is None else ha),
            device_id_type=MESH,
        )

    def send(self, *args, **kwargs):
        copy = self.make(*args, **kwargs)
        copy.start()
        self.pending.append(copy)
        return copy

    def group(self, moves, ssem, rsem, landed):
        for src, dst, where in moves:
            self.make(src, dst, ssem, rsem, **where).start()
        group = Group(ssem, rsem, landed)
        self.pending.append(group)
        return group

    def finish(self):
        self.halo_sent()
        for copy in self.pending:
            copy.wait_send()

    def sum_start(self, f, k, q, sums, first=True):
        i = 2 * k + q
        for part in (0, 1):
            value = jnp.sum(sums[part], 0, keepdims=True)
            for t in range(-(-value.shape[1] // 128)):
                piece = value[:, 128 * t : 128 * (t + 1)]
                f.sum_src[i, 4 * part + t : 4 * part + t + 1, : piece.shape[1]] = piece
        return self.sum_stage(f, i, first, f.sum_src[i])

    def sum_stage(self, f, i, rows, value):
        count, me = (self.A, self.a) if rows else (self.B, self.z)
        buf, ssem, rsem = (f.sum_a, f.sum_as, f.sum_ar) if rows else (f.sum_z, f.sum_zs, f.sum_zr)
        buf[i, me] = value
        mine = buf.at[i, me]
        name = n.ha if rows else n.img
        moves = [(mine, mine, {name: lax.rem(me + d, count)}) for d in range(1, count)]
        group = None
        if moves:
            group = self.group(moves, ssem.at[i], rsem.at[i], buf.at[i, pl.ds(0, count - 1)])
        return rows, buf, count, group

    def sum_total(self, i, stage):
        rows, buf, count, group = stage
        if group is not None:
            group.wait_recv()
        total = buf[i, 0]
        for d in range(1, count):
            total = total + buf[i, d]
        return total

    def sum_cross(self, f, k, q, stage):
        i = 2 * k + q
        return self.sum_stage(f, i, not stage[0], self.sum_total(i, stage))

    def sum_end(self, f, k, q, stage):
        i = 2 * k + q
        f.sum_out[i] = self.sum_total(i, stage)

    def swap_start(self, src, dst, ssem, rsem, rows):
        def block(ref, t):
            return ref.at[:, pl.ds(pl.multiple_of(t * rows, 8), rows)]

        moves = []
        for d in range(1, self.A):
            t = lax.rem(self.a + d, self.A)
            moves.append((block(src, t), block(dst, self.a), {n.ha: t}))
        group = self.group(moves, ssem, rsem, dst.at[:, pl.ds(0, (self.A - 1) * rows)])
        mine = pl.ds(pl.multiple_of(self.a * rows, 8), rows)
        dst[:, mine, :] = src[:, mine, :]
        return group

    def swap_end(self, group):
        group.wait_recv()

    def halo_start(self, low_row, high_row, dst, ssem, rsem):
        up = jnp.maximum(self.a - 1, 0)
        down = jnp.minimum(self.a + 1, self.A - 1)
        low = self.make(low_row, dst.at[1], ssem.at[0], rsem.at[0], ha=up)
        high = self.make(high_row, dst.at[0], ssem.at[1], rsem.at[1], ha=down)

        @pl.when(self.a > 0)
        def _():
            low.start()

        @pl.when(self.a < self.A - 1)
        def _():
            high.start()

        self.halos.append((low, high))
        return [(low, high)]

    def halo_end(self, pairs):
        for low, high in pairs:

            @pl.when(self.a < self.A - 1)
            def _():
                low.wait_recv()

            @pl.when(self.a > 0)
            def _():
                high.wait_recv()

    def halo_sent(self):
        for low, high in self.halos:

            @pl.when(self.a > 0)
            def _():
                low.wait_send()

            @pl.when(self.a < self.A - 1)
            def _():
                high.wait_send()

        self.halos = []


def column_sum(value):
    rows, width = value.shape
    return jnp.sum(value.reshape(rows // 8, 8, width), 0)


def no_sums(width):
    return jnp.zeros((8, width), f32), jnp.zeros((8, width), f32)


def totals(ref, k, q, width):
    i = 2 * k + q
    return [
        jnp.concatenate([ref[i, t : t + 1, :] for t in range(first, first + 4)], 1)[:, :width]
        for first in (0, 4)
    ]


def norm_rows(ref, k, q, width, count):
    total, square = totals(ref, k, q, width)
    center = total * (1.0 / count)
    variance = square * (1.0 / count) - center * center
    return center, lax.rsqrt(variance + epsilon)


def row_transform(bk, table, source, send):
    nbA = bk.nb * bk.A
    tab = (table[0], table[1])
    for h in range(bk.R):
        out = dot3(tab, split(source(h)), NN)
        out = jnp.concatenate([out[:nbA], out[nbA:]], 1)
        for b in range(bk.nb):
            put_strided(send, b * bk.R + h, bk.A, bk.Cp, out[b * bk.A : (b + 1) * bk.A])


def row_back(bk, table, recv, h):
    parts = [get_strided(recv, b * bk.R + h, bk.A, bk.Cp) for b in range(bk.nb)]
    block = jnp.concatenate(parts, 0) if len(parts) > 1 else parts[0]
    half = block.shape[1] // 2
    block = jnp.concatenate([block[:, :half], block[:, half:]], 0)
    return dot3((table[0], table[1]), split(block), NN)


def put_strided(ref, start, count, stride, value):
    for t in range(ref.shape[0]):
        ref[t, pl.ds(start, count, stride=stride), :] = value[:, 128 * t : 128 * (t + 1)]


def get_strided(ref, start, count, stride):
    return jnp.concatenate(
        [ref[t, pl.ds(start, count, stride=stride), :] for t in range(ref.shape[0])], 1
    )


def first_table(ref, other):
    return ref[other, 0], ref[other, 1]


def col_transform(bk, f_col, f_col0, other, recv, put):
    H = bk.H
    for b in range(bk.nb):
        block = jnp.concatenate(
            [get_strided(recv, b * bk.R + h, bk.A, bk.Cp) for h in range(bk.R)], 0
        )
        half = block.shape[1] // 2
        block = split(jnp.concatenate([block[:, :half], block[:, half:]], 0))
        if b == 0:
            out = dot3(first_table(f_col0, other), block, NN)
            put(bk.nb, jnp.concatenate([out[2 * H : 3 * H], out[3 * H :]], 1))
        else:
            out = dot3((f_col[0], f_col[1]), block, NN)
        put(b, jnp.concatenate([out[:H], out[H : 2 * H]], 1))


def col_back(bk, f_colT, f_col0T, other, get, scale, send):
    H = bk.H

    def halves(value):
        half = value.shape[1] // 2
        return [value[:, :half], value[:, half:]]

    for b in range(bk.nb):
        if b == 0:
            block = jnp.concatenate(halves(get(0)) + halves(get(bk.nb)), 0)
            out = dot3(first_table(f_col0T, other), split(block), NN)
        else:
            out = dot3((f_colT[0], f_colT[1]), split(jnp.concatenate(halves(get(b)), 0)), NN)
        out = jnp.concatenate([out[:H], out[H:]], 1)
        out = scale(b, out)
        for h in range(bk.R):
            put_strided(send, b * bk.R + h, bk.A, bk.Cp, out[h * bk.A : (h + 1) * bk.A])


def conv_forward(bk, zh, zl, knh, knl, koh, kol, out):
    MB, W = bk.MB, bk.W
    col = lax.broadcasted_iota(jnp.int32, (MB, 1), 0) % W

    def combine(value, n):
        low = jnp.where(col == 0, 0.0, pltpu.roll(value[:, :n], 1, 0))
        high = jnp.where(col == W - 1, 0.0, pltpu.roll(value[:, 2 * n :], MB - 1, 0))
        return low + value[:, n : 2 * n] + high

    def body(i, carry):
        r = pl.multiple_of(i * MB, 32)
        total = None
        for a in range(3):
            left = (zh[pl.ds(r + a * W, MB), :], zl[pl.ds(r + a * W, MB), :])
            n = knh.shape[2]
            right = (knh[:, a].reshape(3 * n, -1), knl[:, a].reshape(3 * n, -1))
            part = dot3(left, right, NT)
            total = part if total is None else total + part
        CL = knh.shape[2]
        out[pl.ds(r, MB), :CL] = combine(total, CL)
        left = tuple(
            jnp.concatenate([z[pl.ds(r + a * W, MB), :CL] for a in range(3)], 1) for z in (zh, zl)
        )
        cross = dot3(left, (koh[...], kol[...]), NT)
        out[pl.ds(r, MB), CL:] = combine(cross, koh.shape[0] // 3)
        return carry

    lax.fori_loop(0, bk.N // MB, body, 0)


GATHERED = (n.sq, n.nm, n.fo)


class Loader:
    def __init__(self, sems):
        self.sems, self.copies, self.done = sems, {}, set()

    def start(self, name, src, dst):
        copy = pltpu.make_async_copy(src, dst, self.sems.at[len(self.copies)])
        copy.start()
        self.copies[name] = copy

    def wait(self, *names):
        for name in names:
            if name not in self.done:
                self.copies[name].wait()
                self.done.add(name)


KINDS = (n.near, n.inw, n.outw, n.sq, n.fo, n.ex, n.nm)


def old_of(name):
    return name + n._old


def moment_of(name):
    return name + n._moment


def whole_of(name):
    return n.g_ + name


def gather_direct(c, f, name, i):
    shard, whole = getattr(f, name), getattr(f, whole_of(name))
    whole[c.a] = shard[...]
    moves = [(shard, whole.at[c.a], {n.ha: lax.rem(c.a + d, c.A)}) for d in range(1, c.A)]
    return c.group(moves, f.g1s.at[i], f.g1r.at[i], whole.at[pl.ds(0, c.A - 1)])


class Pair:
    def __init__(self, c, f, name, i):
        self.c, self.f, self.i = c, f, i
        self.nc = c.A // 2
        self.chip, self.core = c.a // 2, c.a % 2
        self.sibling = 2 * self.chip + 1 - self.core
        self.whole = getattr(f, whole_of(name))
        shard, mine = getattr(f, name), self.whole.at[c.a]
        self.whole[c.a] = shard[...]
        moves = []
        for d in range(1, self.nc):
            moves.append((shard, mine, {n.ha: 2 * lax.rem(self.chip + d, self.nc) + self.core}))
        self.far = self.group(moves, 0)
        self.near = self.group([(shard, mine, {n.ha: self.sibling})], 1)

    def group(self, moves, k):
        f, i = self.f, self.i
        landed = self.whole.at[pl.ds(0, len(moves))]
        return self.c.group(moves, f.p1s.at[i, k], f.p1r.at[i, k], landed)

    def second(self):
        self.far.wait_recv()
        moves = []
        for d in range(1, self.nc):
            piece = self.whole.at[2 * lax.rem(self.chip + d, self.nc) + self.core]
            moves.append((piece, piece, {n.ha: self.sibling}))
        self.passed = self.group(moves, 2)

    def end(self):
        self.near.wait_recv()
        self.passed.wait_recv()


def grid_of(chips):
    across = max(x for x in range(1, chips + 1) if chips % x == 0 and x * x <= chips)
    return chips // across, across


class Spread:
    def __init__(self, c, f, names):
        self.c, self.f, self.names = c, f, names
        self.Y, self.X = grid_of(c.A // 2)
        self.chip, self.core = c.a // 2, c.a % 2
        self.y, self.x = self.chip // self.X, lax.rem(self.chip, self.X)

    def device(self, dy, dx, core=None):
        y, x = lax.rem(self.y + dy + self.Y, self.Y), lax.rem(self.x + dx + self.X, self.X)
        return 2 * (y * self.X + x) + (self.core if core is None else core)

    def part(self, ref, half, slot):
        if len(ref.shape) == 3:
            return ref.at[slot]
        cut = ref.shape[1] // 2
        return ref.at[slot, pl.ds(0, cut) if half == 0 else pl.ds(cut, ref.shape[1] - cut)]

    def lines(self, half, first):
        along_x = (half == 0) == first
        return [(0, d) for d in range(1, self.X)] if along_x else [(d, 0) for d in range(1, self.Y)]

    def members(self, half):
        for i, name in enumerate(self.names):
            if half == 0 or len(getattr(self.f, name).shape) == 3:
                yield i, name

    def pass_on(self, half, slots, lines, ssem, rsem):
        groups = []
        for i, name in self.members(half):
            ref = getattr(self.f, whole_of(name))
            moves = []
            for dy, dx in lines:
                for slot in slots:
                    piece = self.part(ref, half, slot)
                    moves.append((piece, piece, {n.ha: self.device(dy, dx)}))
            if moves:
                landed = self.part(ref, half, pl.ds(0, len(moves)))
                groups.append(self.c.group(moves, ssem.at[i, half], rsem.at[i, half], landed))
        return groups

    def start(self):
        f = self.f
        for name in self.names:
            getattr(f, whole_of(name))[self.c.a] = getattr(f, name)[...]
        self.one = []
        for half in (0, 1):
            self.one += self.pass_on(half, [self.c.a], self.lines(half, True), f.t1s, f.t1r)

    def second(self):
        f = self.f
        for group in self.one:
            group.wait_recv()
        self.two = []
        for half in (0, 1):
            slots = [self.device(-dy, -dx) for dy, dx in [(0, 0)] + self.lines(half, True)]
            self.two += self.pass_on(half, slots, self.lines(half, False), f.t2s, f.t2r)

    def third(self):
        f, c = self.f, self.c
        for group in self.two:
            group.wait_recv()
        self.three = []
        sibling = self.device(0, 0, 1 - self.core)
        for i, name in enumerate(self.names):
            ref = getattr(f, whole_of(name))
            moves = []
            for dy in range(self.Y):
                for dx in range(self.X):
                    piece = ref.at[self.device(dy, dx)]
                    moves.append((piece, piece, {n.ha: sibling}))
            landed = ref.at[pl.ds(0, len(moves))]
            self.three.append(c.group(moves, f.t3s.at[i], f.t3r.at[i], landed))

    def end(self):
        for group in self.three:
            group.wait_recv()


def far_of(name):
    return name + n._hbm


def forward_names(save):
    weights = list(KINDS)
    ins = for_both(*TABLES)
    if save:
        ins += weights[:-1] + [n.nm_old]
    else:
        ins += [n.seg1, n.flat3, n.gnorm] + [old_of(w) for w in weights]
        ins += [moment_of(w) for w in weights]
    kept = for_both(n.joined) + [n.sum_out, n.norms]
    extra = for_both(n.u, n.spec, n.mixed, n.s, n.halo)
    extra += [n.knh, n.knl, n.koh, n.kol, n.g_sq, n.g_fo, n.g_ex]
    if save:
        kept, extra = kept + extra, [n.nm]
    else:
        kept, extra = kept + [n.flat1], extra + weights + [n.zgs, n.zgr]
    scratch = [n.g_nm, n.g_near, n.g_inw, n.g_outw, n.ld]
    scratch += [n.sum_src, n.sum_a, n.sum_z, n.sum_as, n.sum_ar, n.sum_zs, n.sum_zr]
    scratch += [n.g1s, n.g1r, n.p1s, n.p1r, n.t1s, n.t1r, n.t2s, n.t2r, n.t3s, n.t3r, n.hs, n.hr, n.ws, n.wr]
    scratch += extra + for_both(n.maps, n.zh, n.zl, n.act, *SPECTRA)
    return ins, kept, scratch


def forward_far(save):
    return for_both(n.maps) if save else for_both(n.maps, n.halo)


def forward_kernel(bks, A, B, sizes, save, *refs):
    ins, kept, scratch = forward_names(save)
    far = forward_far(save)
    names = ins + [far_of(k) for k in far] + [far_of(k) for k in kept] + kept + scratch
    f = take(names, refs)
    CL, CG, CH, NPd = sizes
    CT = CL + CG
    c = Comm(A, B)
    c.enter()
    keeper = Loader(f.ld)
    for name in far:
        keeper.start(name, getattr(f, far_of(name)), getattr(f, name))
    other = jnp.minimum(c.a, 1)
    once = jnp.where(c.a == 0, 1.0, 2.0)
    cells = [B * bk.H * bk.W for bk in bks]
    freqs = [B * bk.H * (bk.W // 2 + 1) for bk in bks]
    views = [View(f, 0), View(f, 1)]
    both = (0, 1)

    def keep(*which):
        for k in which:
            if k in kept:
                keeper.start(k, getattr(f, k), getattr(f, far_of(k)))

    f.sum_src[...] = jnp.zeros_like(f.sum_src)
    c.entered()
    if not save:
        shares = spread_images(c, f)
        renew_small(f, A, sizes)
    else:
        f.nm[...] = jnp.zeros_like(f.nm)
        f.nm[0:2, :NPd] = f.nm_old[...]
    first = Pair(c, f, n.sq, 0)
    table = gather_direct(c, f, n.nm, 0)
    if save:
        middle = Pair(c, f, n.fo, 1)
        spread = Spread(c, f, (n.ex, n.near, n.inw, n.outw))
        spread.start()
    for q in both:
        bk, g = bks[q], views[q]
        keeper.wait(n.maps + str(q))

        def body(r, carry, bk=bk, g=g):
            src = pl.multiple_of(r * bk.W, bk.W)
            high, low = split(g.maps[pl.ds(src, bk.W), :])
            g.zh[pl.ds(src + bk.W, bk.W), :] = high
            g.zl[pl.ds(src + bk.W, bk.W), :] = low
            return carry

        lax.fori_loop(0, bk.R, body, 0)
    first.second()
    first.end()

    wsq = split(f.g_sq[...].reshape(CH, CG))
    keep(n.g_sq)
    adding = [None, None]
    for q in both:
        bk, g = bks[q], views[q]

        def body(r, carry, bk=bk, g=g):
            at = pl.multiple_of(r + bk.W, 32)
            value = dot3((g.zh[pl.ds(at, bk.MB), CL:], g.zl[pl.ds(at, bk.MB), CL:]), wsq, NT)
            g.s[pl.ds(r, bk.MB), :] = value
            return carry[0] + column_sum(value), carry[1] + column_sum(value * value)

        adding[q] = c.sum_start(f, 0, q, chunks(bk.N, bk.MB, body, no_sums(CH)))
        keep(n.s + str(q))

    table.wait_recv()
    piece = f.g_nm.shape[2]
    span = pad_to(NPd * A, 128) + 128
    norms = None
    for d in range(A):
        part = jnp.concatenate([f.g_nm[d], jnp.zeros((8, span - piece), f32)], 1)
        if d:
            part = pltpu.roll(part, NPd * d, 1)
        norms = part if norms is None else norms + part
    f.norms[0] = norms[:, :CT]
    f.norms[1] = pltpu.roll(norms, span - CT, 1)[:, :CT]
    f.norms[2] = pltpu.roll(norms, span - CT - CH, 1)[:, :CT]

    keep(n.norms)
    for q in both:
        adding[q] = c.sum_cross(f, 0, q, adding[q])
    if not save:
        shares.wait_recv()
        keep(n.flat1)
        renew_large(f, A, B, sizes)
        middle = Pair(c, f, n.fo, 1)
        spread = Spread(c, f, (n.ex, n.near, n.inw, n.outw))
        spread.start()
    swaps = [None, None]
    for q in both:
        bk, g = bks[q], views[q]
        c.sum_end(f, 0, q, adding[q])
        center, inverse = norm_rows(f.sum_out, 0, q, CH, cells[q])

        def source(h, bk=bk, g=g, center=center, inverse=inverse):
            rows = slice(h * bk.W, (h + 1) * bk.W)
            v = (g.s[rows, :] - center) * inverse * f.norms[1, 0:1, :CH] + f.norms[1, 1:2, :CH]
            value = v * sigmoid(v)
            g.act[rows, :] = value
            return value

        row_transform(bk, g.row, source, g.sendA)
        swaps[q] = c.swap_start(g.sendA, g.recvA, f.ws.at[0, q], f.wr.at[0, q], bk.Cp)

    middle.second()
    spread.second()
    c.swap_end(swaps[0])
    middle.end()
    keep(n.g_fo)
    wfo = split(f.g_fo[...].reshape(2 * CH, 2 * CH))
    for q in both:
        bk, g = bks[q], views[q]
        if q:
            c.swap_end(swaps[q])

        def put(slot, value, g=g, bk=bk):
            g.spec[slot * bk.H : (slot + 1) * bk.H, :] = value

        col_transform(bk, g.col, g.col0, other, g.recvA, put)
        keep(n.spec + str(q))

        def body(r, carry, bk=bk, g=g):
            value = dot3(split(g.spec[pl.ds(r, bk.Q // 2), :]), wfo, NT)
            g.mixed[pl.ds(r, bk.Q // 2), :] = value
            return carry[0] + column_sum(value), carry[1] + column_sum(value * value)

        adding[q] = c.sum_start(f, 1, q, chunks(bk.Q, bk.Q // 2, body, no_sums(2 * CH)), False)
        keep(n.mixed + str(q))
    def convolve(q):
        bk, g = bks[q], views[q]
        conv_forward(bk, g.zh, g.zl, f.knh, f.knl, f.koh, f.kol, g.joined)

    def spectra_back(q):
        bk, g = bks[q], views[q]
        c.sum_end(f, 1, q, adding[q])
        center, inverse = norm_rows(f.sum_out, 1, q, 2 * CH, freqs[q])

        def get(slot, g=g, center=center, inverse=inverse, bk=bk):
            value = g.mixed[slot * bk.H : (slot + 1) * bk.H, :]
            v = (value - center) * inverse * f.norms[2, 0:1, : 2 * CH] + f.norms[2, 1:2, : 2 * CH]
            return v * sigmoid(v)

        def scale(b, value):
            return value * (once if b == 0 else 2.0)

        col_back(bk, g.colT, g.col0T, other, get, scale, g.sendB)
        swaps[q] = c.swap_start(g.sendB, g.recvB, f.ws.at[1, q], f.wr.at[1, q], bk.Cp)

    halos = []
    if save:
        for q in both:
            bk, g = bks[q], views[q]
            halos += c.halo_start(
                g.maps.at[pl.ds(0, bk.W)],
                g.maps.at[pl.ds(bk.N - bk.W, bk.W)],
                g.halo,
                f.hs.at[q],
                f.hr.at[q],
            )
    for q in both:
        adding[q] = c.sum_cross(f, 1, q, adding[q])
    spread.third()
    c.halo_end(halos)
    for q in both:
        bk, g = bks[q], views[q]
        if not save:
            keeper.wait(n.halo + str(q))
        for side, at, edge in ((0, 0, 0), (1, bk.N + bk.W, A - 1)):
            if save:
                g.halo[side] = jnp.where(c.a == edge, 0.0, g.halo[side])
            high, low = split(g.halo[side])
            g.zh[pl.ds(at, bk.W), :] = high
            g.zl[pl.ds(at, bk.W), :] = low
        keep(n.halo + str(q))
    spectra_back(0)
    spectra_back(1)
    spread.end()
    keep(n.g_ex)

    def taps(t, carry):
        a, b = t // 3, t % 3
        near = f.g_near[:, pl.ds(t, 1)].reshape(CL, CL)
        inward = f.g_inw[:, pl.ds(t, 1)].reshape(CL, CG)
        high, low = split(jnp.concatenate([near, inward], 1))
        f.knh[b, a] = high
        f.knl[b, a] = low
        return carry

    lax.fori_loop(0, 9, taps, 0)
    for a in range(3):
        for b in range(3):
            high, low = split(f.g_outw[:, 3 * a + b].reshape(CG, CL))
            f.koh[b * CG : (b + 1) * CG, a * CL : (a + 1) * CL] = high
            f.kol[b * CG : (b + 1) * CG, a * CL : (a + 1) * CL] = low
    keep(n.knh, n.knl, n.koh, n.kol)
    convolve(0)
    convolve(1)

    wex = split(f.g_ex[...].reshape(CG, CH))
    for q in both:
        bk, g = bks[q], views[q]
        c.swap_end(swaps[q])
        for h in range(bk.R):
            rows = slice(h * bk.W, (h + 1) * bk.W)
            g.u[rows, :] = g.act[rows, :] + row_back(bk, g.rowT, g.recvB, h)
        keep(n.u + str(q))

        def body(r, carry, bk=bk, g=g):
            rows = pl.ds(r, bk.MB)
            value = g.joined[rows, CL:] + dot3(split(g.u[rows, :]), wex, NT)
            g.joined[rows, CL:] = value
            value = jnp.concatenate([g.joined[rows, :CL], value], 1)
            return carry[0] + column_sum(value), carry[1] + column_sum(value * value)

        adding[q] = c.sum_start(f, 2, q, chunks(bk.N, bk.MB, body, no_sums(CT)))
        keep(n.joined + str(q))
    for q in both:
        adding[q] = c.sum_cross(f, 2, q, adding[q])
    for q in both:
        c.sum_end(f, 2, q, adding[q])
    keep(n.sum_out)
    keeper.wait(*[k for k in keeper.copies if k in kept])
    c.finish()


def renewed(weight, moment, grad):
    return weight - learn_rate * (grad + momentum * (momentum * moment + grad))


def piece_of(flat, A, B, sizes, second, at, count):
    rows = flat_rows_of(A, B, sizes)
    pieces = []
    while count:
        k, off = (2, at) if second else divmod(at, rows[0])
        part = rows[k] // B
        z, off = divmod(off, part)
        take_now = min(count, part - off)
        start = (z * sum(rows) + sum(rows[:k])) // B + off
        pieces.append(flat[start : start + take_now, :])
        at, count = at + take_now, count - take_now
    return jnp.concatenate(pieces, 0) if len(pieces) > 1 else pieces[0]


def unpack(flat, A, B, sizes, second, at, count, tiles):
    unit = pad_to(count, 8)
    return jnp.concatenate(
        [piece_of(flat, A, B, sizes, second, at + t * unit, count) for t in range(tiles)], 1
    )


def unpack_tap(flat, A, B, sizes, k):
    CL, CG, CH, NPd = sizes
    first = flat_plan(A, sizes)[0]
    o, p, tiles = CL // A, CG // A, (CL + CG) // 128
    return (
        unpack(flat, A, B, sizes, False, first[0] + k * pad_to(o, 8) * tiles, o, tiles),
        unpack(flat, A, B, sizes, False, first[1] + k * pad_to(p, 8), p, CL // 128),
    )


def unpack_squeeze(flat, A, sizes):
    CH, CG = sizes[2], sizes[1]
    o = CH // A
    unit = pad_to(o, 8)
    return jnp.concatenate([flat[t * unit : t * unit + o, :] for t in range(CG // 128)], 1)


def unpack_matrices(flat1, flat3, A, B, sizes):
    CL, CG, CH, NPd = sizes
    first = flat_plan(A, sizes)[0]
    return (
        unpack_squeeze(flat3, A, sizes) if flat3 is not None else None,
        unpack(flat1, A, B, sizes, True, 0, 2 * CH // A, 2 * CH // 128),
        unpack(flat1, A, B, sizes, False, first[2], CG // A, pad_to(CH, 128) // 128)[:, :CH],
    )


def spread_images(c, f):
    part = f.seg1.shape[0]
    mine = pl.ds(pl.multiple_of(c.z * part, 8), part)
    f.flat1[mine, :] = f.seg1[...]
    moves = [
        (f.seg1, f.flat1.at[mine], {n.img: lax.rem(c.z + d, c.B)}) for d in range(1, c.B)
    ]
    return c.group(moves, f.zgs.at[0], f.zgr.at[0], f.flat1.at[pl.ds(0, (c.B - 1) * part)])


def renew_small(f, A, sizes):
    f.sq[...] = renewed(f.sq_old[...], f.sq_moment[...], unpack_squeeze(f.flat3, A, sizes))
    P = sizes[3]
    f.nm[...] = jnp.zeros_like(f.nm)
    f.nm[0:2, :P] = renewed(f.nm_old[...], f.nm_moment[...], f.gnorm[0:2, :P])


def renew_large(f, A, B, sizes):
    CL = sizes[0]
    for k in range(9):
        both, out = unpack_tap(f.flat1, A, B, sizes, k)
        f.near[k] = renewed(f.near_old[k], f.near_moment[k], both[:, :CL])
        f.inw[k] = renewed(f.inw_old[k], f.inw_moment[k], both[:, CL:])
        f.outw[k] = renewed(f.outw_old[k], f.outw_moment[k], out)
    sq, fo, ex = unpack_matrices(f.flat1, None, A, B, sizes)
    f.fo[...] = renewed(f.fo_old[...], f.fo_moment[...], fo)
    f.ex[...] = renewed(f.ex_old[...], f.ex_moment[...], ex)


def forward_shapes(bks, A, B, sizes):
    CL, CG, CH, NPd = sizes
    CT = CL + CG
    sd = {n.sum_out: (6, 8, 128), n.norms: (3, 8, CT)}
    sd[n.knh] = sd[n.knl] = (3, 3, CL, CT)
    sd[n.koh] = sd[n.kol] = (3 * CG, 3 * CL)
    for name, shape in (
        (n.sq, (CH // A, CG)),
        (n.fo, (2 * CH // A, 2 * CH)),
        (n.ex, (CG // A, CH)),
        (n.nm, (8, pad_to(NPd, 128))),
        (n.near, (9, CL // A, CL)),
        (n.inw, (9, CL // A, CG)),
        (n.outw, (9, CG // A, CL)),
    ):
        sd[name] = shape
        sd[whole_of(name)] = (A,) + shape
    sd[n.flat1] = (sum(flat_rows_of(A, B, sizes)), 128)
    sd[n.seg1] = (sum(flat_rows_of(A, B, sizes)) // B, 128)
    for q, bk in enumerate(bks):
        here = {
            n.maps: (bk.N, CT),
            n.up: (bk.N, CT),
            n.joined: (bk.N, CT),
            n.u: (bk.N, CH),
            n.spec: (bk.Q, 2 * CH),
            n.mixed: (bk.Q, 2 * CH),
            n.s: (bk.N, CH),
            n.halo: (2, bk.W, CT),
            n.zh: ((bk.R + 2) * bk.W, CT),
            n.zl: ((bk.R + 2) * bk.W, CT),
            n.act: (bk.N, CH),
        }
        for name in SPECTRA:
            here[name] = (2 * CH // 128, A * bk.Cp, 128)
        for name, shape in here.items():
            sd[name + str(q)] = shape
    sd[n.sum_src] = (6, 8, 128)
    sd[n.sum_a] = (6, A, 8, 128)
    sd[n.sum_z] = (6, B, 8, 128)
    return sd


HALF = {n.knh, n.knl, n.koh, n.kol, n.dth, n.dtl, n.zh, n.zl} | set(for_both(n.zh, n.zl, n.dh, n.dl))


def memory(name, sd, sems):
    if name in sems:
        return pltpu.SemaphoreType.DMA(sems[name])
    return pltpu.VMEM(sd[name], bf16 if name in HALF else f32)


def result(name, sd):
    return jax.ShapeDtypeStruct(sd[name], bf16 if name in HALF else f32)


def sum_sems(A, B):
    return {
        n.sum_as: (6,),
        n.sum_ar: (6,),
        n.sum_zs: (6,),
        n.sum_zr: (6,),
        n.hs: (2, 2),
        n.hr: (2, 2),
        n.ws: (2, 2),
        n.wr: (2, 2),
    }


VM = pl.BlockSpec(memory_space=pltpu.VMEM)
FAR = pl.BlockSpec(memory_space=pl.ANY)


def forward_call(bks, A, B, sizes, save, cid, args):
    sd = forward_shapes(bks, A, B, sizes)
    ins, kept, scratch = forward_names(save)
    sems = sum_sems(A, B)
    far = forward_far(save)
    sems[n.ld] = (len(kept) + len(far),)
    sems[n.g1s] = sems[n.g1r] = (1,)
    sems[n.p1s] = sems[n.p1r] = (2, 3)
    for name in (n.t1s, n.t1r, n.t2s, n.t2r):
        sems[name] = (5, 2)
    sems[n.t3s] = sems[n.t3r] = (5,)
    sems[n.zgs] = sems[n.zgr] = (1,)
    results = kept
    macs = sum(bk.N for bk in bks) * 1400000
    res = pl.pallas_call(
        functools.partial(forward_kernel, bks, A, B, sizes, save),
        out_shape=[result(name, sd) for name in results],
        in_specs=[VM] * len(ins) + [FAR] * len(far),
        out_specs=[FAR] * len(kept),
        scratch_shapes=[memory(name, sd, sems) for name in kept + scratch],
        compiler_params=pltpu.CompilerParams(
            collective_id=cid, has_side_effects=True, vmem_limit_bytes=VMEM_LIMIT
        ),
        cost_estimate=pl.CostEstimate(flops=6 * macs, bytes_accessed=40_000_000, transcendentals=0),
        name=n.forward,
    )(*[args[name] for name in ins + far])
    return dict(zip(results, res))


def finish_kernel(counts, *refs):
    maps, joined, sums, norms, outs = refs[0:2], refs[2:4], refs[4], refs[5], refs[6:8]
    for q in (0, 1):
        center, inverse = norm_rows(sums, 2, q, norms.shape[2], counts[q])
        v = (joined[q][...] - center) * inverse * norms[0, 0:1, :] + norms[0, 1:2, :]
        outs[q][...] = maps[q][...] + v * sigmoid(v)


def finish_call(bks, images, maps, fwd):
    N, CT = maps[0].shape
    step = N // 3 if N % 24 == 0 else N
    block = pl.BlockSpec((step, CT), lambda i: (i, 0))
    counts = [images * bk.H * bk.W for bk in bks]
    return pl.pallas_call(
        functools.partial(finish_kernel, counts),
        out_shape=[jax.ShapeDtypeStruct(m.shape, f32) for m in maps],
        grid=(N // step,),
        in_specs=[block] * 4 + [VM] * 2,
        out_specs=[block] * 2,
        compiler_params=pltpu.CompilerParams(vmem_limit_bytes=VMEM_LIMIT),
        cost_estimate=pl.CostEstimate(
            flops=N * CT * 20, bytes_accessed=N * CT * 24, transcendentals=N * CT * 2
        ),
        name=n.finish,
    )(*maps, fwd[n.joined0], fwd[n.joined1], fwd[n.sum_out], fwd[n.norms])


def flat_plan(A, sizes):
    CL, CG, CH, NPd = sizes
    CT = CL + CG

    def rows(count, width):
        return pad_to(count // A, 8) * pad_to(width, 128) // 128

    near, outw = 9 * rows(CL, CT), 9 * rows(CG, CL)
    first = (0, near, near + outw)
    return first, near + outw + rows(CG, CH), rows(2 * CH, 2 * CH), rows(CH, CG)


def flat_rows_of(A, B, sizes):
    first, end1, rows2, rows3 = flat_plan(A, sizes)
    half = pad_to(end1, 16 * B) // 2
    return half, half, pad_to(rows2, 8 * B)


LATE = for_both(n.joined, n.up) + for_both(n.maps, n.halo, n.u, n.mixed, n.spec, n.s)
LATE += [n.g_fo, n.knh, n.knl, n.koh, n.kol, n.g_sq]


def backward_names():
    ins = [n.sum_out, n.norms, n.g_ex] + for_both(*TABLES)
    outs = []
    kept = [n.seg1, n.flat3, n.gnorm] + for_both(n.back, n.block)
    scratch = [n.sum_src, n.sum_a, n.sum_z, n.bsum, n.sum_as, n.sum_ar, n.sum_zs, n.sum_zr]
    scratch += [n.hs, n.hr, n.ws, n.wr, n.ld, n.rs1s, n.rs1r, n.rs2s, n.rs2r, n.rs3s, n.rs3r, n.rs5s, n.rs5r]
    scratch += [n.das, n.dar, n.dzs, n.dzr, n.cs, n.cr]
    scratch += [n.dth, n.dtl, n.zh, n.zl, n.gsq, n.gfo]
    scratch += [n.own1, n.sib1, n.far1, n.last1, n.zin1, n.own2, n.sib2, n.far2, n.zin2, n.own3, n.far3, n.zin3]
    scratch += [n.seg1, n.flat3, n.gnorm, n.tot2]
    scratch += for_both(n.dh, n.dl, n.dhalo, n.du, n.dmix, *SPECTRA)
    return ins, outs, kept, scratch


def silu_slope(v):
    sig = sigmoid(v)
    return sig * (1.0 + v * (1.0 - sig))


class Reduce:
    def __init__(self, c, f):
        self.c, self.f = c, f
        self.own, self.sib, self.far, self.last = f.own1, f.sib1, f.far1, f.last1
        self.zin = f.zin1
        self.rows = self.own.shape[1]
        self.nc = c.A // 2
        self.chip, self.core = c.a // 2, c.a % 2
        self.Y, self.X = grid_of(self.nc)
        self.y, self.x = self.chip // self.X, lax.rem(self.chip, self.X)

    def to_sibling(self):
        f, c = self.f, self.c
        other = 1 - self.core
        moves = [
            (self.own.at[2 * cc + other], self.sib.at[cc], {n.ha: 2 * self.chip + other})
            for cc in range(self.nc)
        ]
        self.copies = [c.group(moves, f.rs1s.at[0], f.rs1r.at[0], self.sib.at[pl.ds(0, self.nc)])]

    def device(self, dy, dx):
        y, x = lax.rem(self.y + dy + self.Y, self.Y), lax.rem(self.x + dx + self.X, self.X)
        return 2 * (y * self.X + x) + self.core

    def lines(self, half, first):
        along_x = (half == 0) == first
        return [(0, d) for d in range(1, self.X)] if along_x else [(d, 0) for d in range(1, self.Y)]

    def part(self, half):
        h = self.rows // 2
        return pl.ds(half * h, h)

    def to_lines(self):
        f, c = self.f, self.c
        for copy in self.copies:
            copy.wait_recv()
        for dy in range(self.Y):
            for dx in range(self.X):
                t = self.device(dy, dx)
                self.own[t] = self.own[t] + self.sib[t // 2]
        self.copies = []
        for half in (0, 1):
            rest = [(0, 0)] + self.lines(half, False)
            moves = []
            for k, (dy, dx) in enumerate(self.lines(half, True)):
                for j, (ry, rx) in enumerate(rest):
                    t = self.device(dy + ry, dx + rx)
                    moves.append(
                        (
                            self.own.at[t, self.part(half)],
                            self.far.at[half, k * len(rest) + j],
                            {n.ha: self.device(dy, dx)},
                        )
                    )
            if moves:
                landed = self.far.at[half, pl.ds(0, len(moves))]
                self.copies.append(c.group(moves, f.rs2s.at[half], f.rs2r.at[half], landed))

    def to_owners(self):
        f, c = self.f, self.c
        for copy in self.copies:
            copy.wait_recv()
        self.copies = []
        for half in (1, 0):
            rows = self.part(half)
            rest = [(0, 0)] + self.lines(half, False)
            lines = self.lines(half, True)
            moves = []
            for j, (ry, rx) in enumerate(rest):
                t = self.device(ry, rx)
                total = self.own[t, rows, :]
                for k in range(len(lines)):
                    total = total + self.far[half, k * len(rest) + j]
                self.own[t, rows, :] = total
                if j:
                    moves.append((self.own.at[t, rows], self.last.at[half, j], {n.ha: t}))
            if moves:
                landed = self.last.at[half, pl.ds(1, len(moves))]
                self.copies.append(c.group(moves, f.rs5s.at[half], f.rs5r.at[half], landed))

    def collect(self):
        f, c = self.f, self.c
        for copy in self.copies:
            copy.wait_recv()
        for half in (0, 1):
            rows = self.part(half)
            total = self.own[c.a, rows, :]
            for j in range(1, 1 + len(self.lines(half, False))):
                total = total + self.last[half, j]
            self.own[c.a, rows, :] = total

    def to_images(self, k):
        f, c = self.f, self.c
        return to_images(
            c, self.own.at[c.a, self.part(k)], self.zin.at[k], f.rs3s.at[k], f.rs3r.at[k]
        )


def to_images(c, total, zin, ssem, rsem):
    part = total.shape[0] // c.B
    moves = []
    for d in range(1, c.B):
        zz = lax.rem(c.z + d, c.B)
        piece = total.at[pl.ds(pl.multiple_of(zz * part, 8), part)]
        moves.append((piece, zin.at[d], {n.img: zz}))
    return [c.group(moves, ssem, rsem, zin.at[pl.ds(1, c.B - 1)])] if moves else []


def from_images(c, copies, total, zin, out):
    for copy in copies:
        copy.wait_recv()
    part = total.shape[0] // c.B
    value = total[pl.ds(pl.multiple_of(c.z * part, 8), part), :]
    for d in range(1, c.B):
        value = value + zin[d]
    out[...] = value


class Direct:
    def __init__(self, c, f, own, far):
        self.c, self.f = c, f
        self.own, self.far = own, far

    def start(self):
        c, f = self.c, self.f
        moves = []
        for d in range(1, c.A):
            t = lax.rem(c.a + d, c.A)
            moves.append((self.own.at[t], self.far.at[d], {n.ha: t}))
        landed = self.far.at[pl.ds(1, c.A - 1)]
        self.copies = c.group(moves, f.das.at[0], f.dar.at[0], landed)

    def cross(self, zin):
        c, f = self.c, self.f
        self.copies.wait_recv()
        total = self.own[c.a]
        for d in range(1, c.A):
            total = total + self.far[d]
        zin[c.z] = total
        mine = zin.at[c.z]
        moves = [(mine, mine, {n.img: lax.rem(c.z + d, c.B)}) for d in range(1, c.B)]
        self.copies = []
        if moves:
            landed = zin.at[pl.ds(0, c.B - 1)]
            self.copies = [c.group(moves, f.dzs.at[0], f.dzr.at[0], landed)]

    def end(self, zin, out):
        for copy in self.copies:
            copy.wait_recv()
        total = zin[0]
        for d in range(1, self.c.B):
            total = total + zin[d]
        out[...] = total


class Chips:
    def __init__(self, c, f, own, sib, far):
        self.c, self.f = c, f
        self.own, self.sib, self.far = own, sib, far
        self.nc = c.A // 2
        self.chip, self.core = c.a // 2, c.a % 2

    def to_sibling(self):
        f, c = self.f, self.c
        other = 1 - self.core
        moves = [
            (self.own.at[2 * cc + other], self.sib.at[cc], {n.ha: 2 * self.chip + other})
            for cc in range(self.nc)
        ]
        self.copies = c.group(moves, f.cs.at[0], f.cr.at[0], self.sib.at[pl.ds(0, self.nc)])

    def start(self):
        f, c = self.f, self.c
        self.copies.wait_recv()
        moves = []
        for d in range(self.nc):
            cc = lax.rem(self.chip + d, self.nc)
            t = 2 * cc + self.core
            self.own[t] = self.own[t] + self.sib[cc]
            if d:
                moves.append((self.own.at[t], self.far.at[d], {n.ha: t}))
        self.copies = c.group(moves, f.cs.at[1], f.cr.at[1], self.far.at[pl.ds(1, self.nc - 1)])

    def owned(self):
        self.copies.wait_recv()
        total = self.own[self.c.a]
        for d in range(1, self.nc):
            total = total + self.far[d]
        return total


def backward_kernel(bks, A, B, sizes, *refs):
    ins, outs, kept, scratch = backward_names()
    near = ins + [far_of(name) for name in LATE] + [far_of(name) for name in kept]
    f = take(near + LATE + scratch, refs)
    CL, CG, CH, NPd = sizes
    CT = CL + CG
    c = Comm(A, B)
    c.enter()
    loader = Loader(f.ld)
    for name in LATE:
        loader.start(name, getattr(f, far_of(name)), getattr(f, name))
    other = jnp.minimum(c.a, 1)
    once = jnp.where(c.a == 0, 1.0, 2.0)
    cells = [B * bk.H * bk.W for bk in bks]
    freqs = [B * bk.H * (bk.W // 2 + 1) for bk in bks]
    views = [View(f, 0), View(f, 1)]
    both = (0, 1)
    sums = take(
        (n.sum_src, n.sum_a, n.sum_z, n.sum_as, n.sum_ar, n.sum_zs, n.sum_zr, n.sum_out),
        (f.sum_src, f.sum_a, f.sum_z, f.sum_as, f.sum_ar, f.sum_zs, f.sum_zr, f.bsum),
    )
    f.sum_src[...] = jnp.zeros_like(f.sum_src)
    adding, swaps = [None, None], [None, None]

    for q in both:
        bk, g = bks[q], views[q]
        center, inverse = norm_rows(f.sum_out, 2, q, CT, cells[q])
        loader.wait(n.joined + str(q), n.up + str(q))

        def body(r, carry, g=g, center=center, inverse=inverse):
            rows = pl.ds(r, 32)
            x = (g.joined[rows, :] - center) * inverse
            dy = g.up[rows, :] * silu_slope(x * f.norms[0, 0:1, :] + f.norms[0, 1:2, :])
            g.up[rows, :] = dy
            return carry[0] + column_sum(dy), carry[1] + column_sum(dy * x)

        total = chunks(bk.N, 32, body, no_sums(CT))
        if q == 0:
            c.entered()
        adding[q] = c.sum_start(sums, 0, q, total)
    for q in both:
        adding[q] = c.sum_cross(sums, 0, q, adding[q])

    wex = split(f.g_ex[...].reshape(CG, CH))
    halos = []
    for q in both:
        bk, g = bks[q], views[q]
        c.sum_end(sums, 0, q, adding[q])
        center, inverse = norm_rows(f.sum_out, 2, q, CT, cells[q])
        gain = f.norms[0, 0:1, :] * inverse
        m1, m2 = (value * (1.0 / cells[q]) for value in totals(f.bsum, 0, q, CT))
        loader.wait(n.maps + str(q))

        def body(r, carry, bk=bk, g=g, center=center, inverse=inverse, gain=gain, m1=m1, m2=m2):
            rows = pl.ds(r, 32)
            x = (g.joined[rows, :] - center) * inverse
            dz = gain * (g.up[rows, :] - m1 - x * m2)
            g.up[rows, :] = dz
            high, low = split(dz)
            at = pl.ds(pl.multiple_of(r + bk.W, 32), 32)
            g.dh[at, :] = high
            g.dl[at, :] = low
            v = x * f.norms[0, 0:1, :] + f.norms[0, 1:2, :]
            g.joined[rows, :] = g.maps[rows, :] + v * sigmoid(v)
            return carry

        chunks(bk.N, 32, body, 0)
        name = n.block + str(q)
        loader.start(name, g.joined, getattr(f, far_of(name)))
        halos += c.halo_start(
            g.up.at[pl.ds(0, bk.W)],
            g.up.at[pl.ds(bk.N - bk.W, bk.W)],
            g.dhalo,
            f.hs.at[q],
            f.hr.at[q],
        )

        def body2(r, carry, bk=bk, g=g):
            at = pl.ds(pl.multiple_of(r + bk.W, 32), bk.MB)
            g.du[pl.ds(r, bk.MB), :] = dot3((g.dh[at, CL:], g.dl[at, CL:]), wex, NN)
            return carry

        chunks(bk.N, bk.MB, body2, 0)
        row_transform(bk, g.row, lambda h, g=g, bk=bk: g.du[h * bk.W : (h + 1) * bk.W, :], g.sendA)
        swaps[q] = c.swap_start(g.sendA, g.recvA, f.ws.at[0, q], f.wr.at[0, q], bk.Cp)

    first, end1, rows2, rows3 = flat_plan(A, sizes)
    units = (pad_to(CL // A, 8) * (CT // 128), pad_to(CG // A, 8))

    def pack(own, at, value, more):
        rows = value.shape[0] // A
        for t in range(A):
            for k in range(value.shape[1] // 128):
                piece = value[t * rows : (t + 1) * rows, 128 * k : 128 * (k + 1)]
                to = pl.ds(at + k * pad_to(rows, 8), rows)
                own[t, to, :] = own[t, to, :] + piece if more else piece

    def kernel_gradients(q):
        bk, g = bks[q], views[q]
        step = min(bk.N, 384)
        col = lax.broadcasted_iota(jnp.int32, (step, 1), 0) % bk.W
        for i in range(bk.N // step):
            for t in range(CT // 128):
                value = g.up[i * step : (i + 1) * step, 128 * t : 128 * (t + 1)]
                moved = (
                    jnp.where(col == bk.W - 1, 0.0, pltpu.roll(value, step - 1, 0)),
                    value,
                    jnp.where(col == 0, 0.0, pltpu.roll(value, 1, 0)),
                )
                for b in range(3):
                    high, low = split(jnp.transpose(moved[b]))
                    at = b * CL if t == 0 else 3 * CL + b * CG + 128 * (t - 1)
                    f.dth[at : at + 128, i * step : (i + 1) * step] = high
                    f.dtl[at : at + 128, i * step : (i + 1) * step] = low
        loader.wait(n.maps + str(q), n.halo + str(q), n.u + str(q))

        def body(r, carry):
            src = pl.multiple_of(r * bk.W, bk.W)
            high, low = split(g.maps[pl.ds(src, bk.W), :])
            f.zh[pl.ds(src + bk.W, bk.W), :] = high
            f.zl[pl.ds(src + bk.W, bk.W), :] = low
            return carry

        lax.fori_loop(0, bk.R, body, 0)
        for side, at in ((0, 0), (1, bk.N + bk.W)):
            high, low = split(g.halo[side])
            f.zh[pl.ds(at, bk.W), :] = high
            f.zl[pl.ds(at, bk.W), :] = low

        def taps(a, carry):
            rows = pl.ds(pl.multiple_of(a * bk.W, 32), bk.N)
            right = (f.zh[rows, :], f.zl[rows, :])
            out = dot3((f.dth[: 3 * CL, :], f.dtl[: 3 * CL, :]), right, NN)
            for b in range(3):
                at = pl.multiple_of(first[0] + (3 * a + b) * units[0], 8)
                pack(f.own1, at, out[b * CL : (b + 1) * CL], q)
            return carry

        lax.fori_loop(0, 3, taps, 0)
        right = tuple(
            jnp.concatenate([z[a * bk.W : a * bk.W + bk.N, :CL] for a in range(3)], 1)
            for z in (f.zh, f.zl)
        )
        for b in range(3):
            at = 3 * CL + b * CG
            value = dot3((f.dth[at : at + CG, :], f.dtl[at : at + CG, :]), right, NN)
            for a in range(3):
                piece = value[:, a * CL : (a + 1) * CL]
                pack(f.own1, first[1] + (3 * a + b) * units[1], piece, q)
        at = 3 * CL + CG
        value = dot3((f.dth[at : at + CG, :], f.dtl[at : at + CG, :]), split(g.u[...]), NN)
        value = jnp.concatenate([value, jnp.zeros((CG, pad_to(CH, 128) - CH), f32)], 1)
        pack(f.own1, first[2], value, q)

    def spectra_slopes(q):
        bk, g = bks[q], views[q]
        loader.wait(n.mixed + str(q))
        c.swap_end(swaps[q])
        center, inverse = norm_rows(f.sum_out, 1, q, 2 * CH, freqs[q])
        carry = [no_sums(2 * CH)]

        def put(slot, value):
            rows = slice(slot * bk.H, (slot + 1) * bk.H)
            x = (g.mixed[rows, :] - center) * inverse
            value = value * (once if slot in (0, bk.nb) else 2.0)
            dy = value * silu_slope(x * f.norms[2, 0:1, : 2 * CH] + f.norms[2, 1:2, : 2 * CH])
            g.dmix[rows, :] = dy
            carry[0] = (carry[0][0] + column_sum(dy), carry[0][1] + column_sum(dy * x))

        col_transform(bk, g.col, g.col0, other, g.recvA, put)
        adding[q] = c.sum_start(sums, 1, q, carry[0])

    def spectra_back(q, wfo):
        bk, g = bks[q], views[q]
        c.sum_end(sums, 1, q, adding[q])
        center, inverse = norm_rows(f.sum_out, 1, q, 2 * CH, freqs[q])
        gain = f.norms[2, 0:1, : 2 * CH] * inverse
        m1, m2 = (value * (1.0 / freqs[q]) for value in totals(f.bsum, 1, q, 2 * CH))

        def get(slot):
            rows = slice(slot * bk.H, (slot + 1) * bk.H)
            x = (g.mixed[rows, :] - center) * inverse
            dz = gain * (g.dmix[rows, :] - m1 - x * m2)
            g.dmix[rows, :] = dz
            return dot3(split(dz), wfo, NN)

        col_back(bk, g.colT, g.col0T, other, get, lambda b, v: v, g.sendB)
        swaps[q] = c.swap_start(g.sendB, g.recvB, f.ws.at[1, q], f.wr.at[1, q], bk.Cp)

    kernel_gradients(0)
    spectra_slopes(0)
    kernel_gradients(1)
    adding[0] = c.sum_cross(sums, 1, 0, adding[0])
    if f.own1.shape[1] > end1:
        f.own1[:, end1:, :] = jnp.zeros((A, f.own1.shape[1] - end1, 128), f32)
    red1 = Reduce(c, f)
    red1.to_sibling()
    spectra_slopes(1)
    loader.wait(n.g_fo)
    wfo = split(f.g_fo[...].reshape(2 * CH, 2 * CH))
    adding[1] = c.sum_cross(sums, 1, 1, adding[1])
    red1.to_lines()
    spectra_back(0, wfo)
    spectra_back(1, wfo)
    for q in both:
        bk, g = bks[q], views[q]
        loader.wait(n.spec + str(q))
        value = dot3(split(jnp.transpose(g.dmix[...])), split(g.spec[...]), NN)
        f.gfo[...] = value if q == 0 else f.gfo[...] + value
    pack(f.own2, 0, f.gfo, 0)
    red2 = Chips(c, f, f.own2, f.sib2, f.far2)
    red2.to_sibling()

    c.halo_end(halos)
    c.halo_sent()
    loader.wait(n.knh, n.knl, n.koh, n.kol)

    def input_gradients(q):
        bk, g = bks[q], views[q]
        for side, at, edge in ((0, 0, 0), (1, bk.N + bk.W, A - 1)):
            high, low = split(jnp.where(c.a == edge, 0.0, g.dhalo[side]))
            g.dh[pl.ds(at, bk.W), :] = high
            g.dl[pl.ds(at, bk.W), :] = low
        conv_backward(bk, g.dh, g.dl, f.knh, f.knl, f.koh, f.kol, g.up)

    def active_slopes(q):
        bk, g = bks[q], views[q]
        loader.wait(n.s + str(q))
        c.swap_end(swaps[q])
        center, inverse = norm_rows(f.sum_out, 0, q, CH, cells[q])
        total = no_sums(CH)
        for h in range(bk.R):
            rows = slice(h * bk.W, (h + 1) * bk.W)
            x = (g.s[rows, :] - center) * inverse
            value = g.du[rows, :] + row_back(bk, g.rowT, g.recvB, h)
            dy = value * silu_slope(x * f.norms[1, 0:1, :CH] + f.norms[1, 1:2, :CH])
            g.du[rows, :] = dy
            total = (total[0] + column_sum(dy), total[1] + column_sum(dy * x))
        adding[q] = c.sum_start(sums, 2, q, total, False)

    def squeeze_back(q, wsq):
        bk, g = bks[q], views[q]
        c.sum_end(sums, 2, q, adding[q])
        center, inverse = norm_rows(f.sum_out, 0, q, CH, cells[q])
        gain = f.norms[1, 0:1, :CH] * inverse
        m1, m2 = (value * (1.0 / cells[q]) for value in totals(f.bsum, 2, q, CH))

        def body(r, carry):
            rows = pl.ds(r, bk.MB)
            x = (g.s[rows, :] - center) * inverse
            dz = gain * (g.du[rows, :] - m1 - x * m2)
            g.du[rows, :] = dz
            g.up[rows, CL:] += dot3(split(dz), wsq, NN)
            return carry

        chunks(bk.N, bk.MB, body, 0)
        value = dot3(split(jnp.transpose(g.du[...])), split(g.maps[:, CL:]), NN)
        f.gsq[...] = value if q == 0 else f.gsq[...] + value

    input_gradients(0)
    red1.to_owners()
    input_gradients(1)
    active_slopes(0)
    active_slopes(1)
    red1.collect()
    images = [red1.to_images(0), red1.to_images(1)]
    loader.wait(n.g_sq)
    wsq = split(f.g_sq[...].reshape(CH, CG))
    for q in both:
        adding[q] = c.sum_cross(sums, 2, q, adding[q])
    red2.start()
    squeeze_back(0, wsq)
    squeeze_back(1, wsq)
    for q in both:
        name = n.back + str(q)
        loader.start(name, views[q].up, getattr(f, far_of(name)))
    pack(f.own3, 0, f.gsq, 0)
    red3 = Direct(c, f, f.own3, f.far3)
    red3.start()
    f.tot2[: f.own2.shape[1], :] = red2.owned()
    if f.tot2.shape[0] > f.own2.shape[1]:
        f.tot2[f.own2.shape[1] :, :] = jnp.zeros((f.tot2.shape[0] - f.own2.shape[1], 128), f32)
    images.append(to_images(c, f.tot2, f.zin2, f.rs3s.at[2], f.rs3r.at[2]))

    span = pad_to(NPd * A, 128) + 128
    lane = lax.broadcasted_iota(jnp.int32, (8, span), 1)
    out = []
    for i in (1, 0):
        rows = []
        for k, width in ((0, CT), (1, 2 * CH), (2, CH)):
            pair = [totals(f.bsum, k, q, CT)[i] for q in both]
            row = jnp.concatenate([pair[0] + pair[1], jnp.zeros((1, span - CT), f32)], 1)
            rows.append(jnp.where(lane < width, jnp.broadcast_to(row, (8, span)), 0.0))
        out.append(rows[0] + pltpu.roll(rows[2], CT, 1) + pltpu.roll(rows[1], CT + CH, 1))
    sub = lax.broadcasted_iota(jnp.int32, (8, span), 0)
    value = pltpu.roll(jnp.where(sub == 0, out[0], out[1]), lax.rem(span - NPd * c.a, span), 1)
    f.gnorm[...] = value[:, : f.gnorm.shape[1]]

    def keep(name):
        loader.start(name, getattr(f, name), getattr(f, far_of(name)))

    keep(n.gnorm)
    red3.cross(f.zin3)
    at = 0
    for k, (total, zin) in enumerate(
        (
            (f.own1.at[c.a, red1.part(0)], f.zin1.at[0]),
            (f.own1.at[c.a, red1.part(1)], f.zin1.at[1]),
            (f.tot2, f.zin2),
        )
    ):
        from_images(c, images[k], total, zin, f.seg1.at[pl.ds(at, zin.shape[1])])
        at += zin.shape[1]
    keep(n.seg1)
    red3.end(f.zin3, f.flat3)
    keep(n.flat3)
    loader.wait(*kept)
    c.finish()


def conv_backward(bk, dh, dl, knh, knl, koh, kol, out):
    MB, W = bk.MB, bk.W
    CL = knh.shape[2]
    CG = koh.shape[0] // 3
    CT = knh.shape[3]
    col = lax.broadcasted_iota(jnp.int32, (MB, 1), 0) % W

    def moved(value, b):
        if b == 0:
            return jnp.where(col == W - 1, 0.0, pltpu.roll(value, MB - 1, 0))
        if b == 2:
            return jnp.where(col == 0, 0.0, pltpu.roll(value, 1, 0))
        return value

    def body(i, carry):
        r = pl.multiple_of(i * MB, 32)
        rows = [pl.ds(pl.multiple_of(r + (2 - a) * W, 32), MB) for a in range(3)]
        left = tuple(jnp.concatenate([d[rows[a], :CL] for a in range(3)], 1) for d in (dh, dl))
        total = None
        for b in (1, 0, 2):
            right = (knh[b].reshape(3 * CL, CT), knl[b].reshape(3 * CL, CT))
            value = moved(dot3(left, right, NN), b)
            total = value if total is None else total + value
        out[pl.ds(r, MB), :] = total
        cross = None
        for a in range(3):
            left2 = (dh[rows[a], CL:], dl[rows[a], CL:])
            right = tuple(
                jnp.concatenate(
                    [k[b * CG : (b + 1) * CG, a * CL : (a + 1) * CL] for b in range(3)], 1
                )
                for k in (koh, kol)
            )
            value = dot3(left2, right, NN)
            cross = value if cross is None else cross + value
        total = None
        for b in range(3):
            value = moved(cross[:, b * CL : (b + 1) * CL], b)
            total = value if total is None else total + value
        out[pl.ds(r, MB), :CL] += total
        return carry

    lax.fori_loop(0, bk.N // MB, body, 0)


def backward_call(bks, A, B, sizes, cid, args):
    CL, CG, CH, NPd = sizes
    CT = CL + CG
    nc = A // 2
    first, end1, rows2, rows3 = flat_plan(A, sizes)
    half1, _, padded2 = flat_rows_of(A, B, sizes)
    rows1 = 2 * half1
    N = max(bk.N for bk in bks)
    big = max((bk.R + 2) * bk.W for bk in bks)
    sd = forward_shapes(bks, A, B, sizes)
    sd[n.bsum] = sd[n.sum_src]
    sd[n.gnorm] = (8, pad_to(NPd, 128))
    sd[n.dth] = sd[n.dtl] = (3 * CT, N)
    sd[n.zh] = sd[n.zl] = (big, CT)
    sd[n.gsq], sd[n.gfo] = (CH, CG), (2 * CH, 2 * CH)
    sd[n.own1], sd[n.zin1] = (A, rows1, 128), (2, B, half1 // B, 128)
    sd[n.sib1] = (nc, rows1, 128)
    sd[n.far1] = (2, nc, rows1 // 2, 128)
    sd[n.last1] = (2, max(grid_of(nc)), rows1 // 2, 128)
    sd[n.tot2], sd[n.zin2] = (padded2, 128), (B, padded2 // B, 128)
    sd[n.own2] = (A, rows2, 128)
    sd[n.sib2] = sd[n.far2] = (nc, rows2, 128)
    sd[n.flat3], sd[n.zin3] = (rows3, 128), (B, rows3, 128)
    sd[n.own3] = sd[n.far3] = (A, rows3, 128)
    for q, bk in enumerate(bks):
        here = {
            n.back: (bk.N, CT),
            n.block: (bk.N, CT),
            n.dh: ((bk.R + 2) * bk.W, CT),
            n.dl: ((bk.R + 2) * bk.W, CT),
            n.dhalo: (2, bk.W, CT),
            n.du: (bk.N, CH),
            n.dmix: (bk.Q, 2 * CH),
        }
        for name, shape in here.items():
            sd[name + str(q)] = shape
    ins, outs, kept, scratch = backward_names()
    results = outs + kept
    sems = sum_sems(A, B)
    sems[n.ld] = (len(LATE) + len(kept),)
    for name in (n.rs1s, n.rs1r, n.das, n.dar, n.dzs, n.dzr):
        sems[name] = (1,)
    sems[n.rs3s] = sems[n.rs3r] = (3,)
    for name in (n.rs2s, n.rs2r, n.rs5s, n.rs5r, n.cs, n.cr):
        sems[name] = (2,)
    macs = sum(bk.N for bk in bks) * 2800000
    res = pl.pallas_call(
        functools.partial(backward_kernel, bks, A, B, sizes),
        out_shape=[result(name, sd) for name in results],
        in_specs=[VM] * len(ins) + [FAR] * len(LATE),
        out_specs=[VM] * len(outs) + [FAR] * len(kept),
        scratch_shapes=[memory(name, sd, sems) for name in LATE + scratch],
        compiler_params=pltpu.CompilerParams(
            collective_id=cid, has_side_effects=True, vmem_limit_bytes=VMEM_LIMIT
        ),
        cost_estimate=pl.CostEstimate(flops=6 * macs, bytes_accessed=40_000_000, transcendentals=0),
        name=n.backward,
    )(*[args[name] for name in ins + LATE])
    return dict(zip(results, res))


def update_kernel(A, B, sizes, *refs):
    CL, CG, CH, NPd = sizes
    flat1, flat3, gnorm = refs[:3]
    weights, moments, averages = refs[3:10], refs[10:17], refs[17:24]
    updated, velocity, smoothed, half = refs[24:31], refs[31:38], refs[38:45], refs[45:52]
    decay = min(0.5, (1.0 + STEP) / (10.0 + STEP))

    def step(i, at, grad):
        new = renewed(weights[i][at], moments[i][at], grad)
        velocity[i][at] = momentum * moments[i][at] + grad
        updated[i][at] = new
        smoothed[i][at] = decay * averages[i][at] + (1.0 - decay) * new
        half[i][at] = new.astype(bf16)

    for k in range(9):
        both, out = unpack_tap(flat1, A, B, sizes, k)
        step(0, k, both[:, :CL])
        step(1, k, both[:, CL:])
        step(2, k, out)
    every = slice(None)
    for i, grad in zip((3, 4, 5), unpack_matrices(flat1, flat3, A, B, sizes)):
        step(i, every, grad)
    step(6, every, gnorm[0:2, :NPd])


def update_call(A, B, sizes, grads, weights, moments, averages):
    shapes = [w.shape for w in weights]
    outs = [jax.ShapeDtypeStruct(s, f32) for _ in range(3) for s in shapes]
    outs += [jax.ShapeDtypeStruct(s, bf16) for s in shapes]
    res = pl.pallas_call(
        functools.partial(update_kernel, A, B, sizes),
        out_shape=outs,
        in_specs=[VM] * 24,
        out_specs=[VM] * len(outs),
        compiler_params=pltpu.CompilerParams(vmem_limit_bytes=VMEM_LIMIT),
        cost_estimate=pl.CostEstimate(flops=3_000_000, bytes_accessed=5_000_000, transcendentals=0),
        name=n.update,
    )(*grads, *weights, *moments, *averages)
    return res[0:7], res[7:14], res[14:21], res[21:28]


def as_rows(weight):
    return jnp.transpose(weight[0], (0, 1, 3, 2)).reshape(9, weight.shape[4], weight.shape[3])


def from_rows(value):
    return jnp.transpose(value.reshape(1, 3, 3, value.shape[1], value.shape[2]), (0, 1, 2, 4, 3))


def flat_rows(weight):
    return jnp.transpose(weight[0])


def from_flat(value):
    return jnp.transpose(value)[None]


def per_device(*arrays):
    A, B = lax.axis_size("ha"), lax.axis_size("img")
    maps, ups = arrays[0:2], arrays[2:4]
    groups = [arrays[4 + i :: 3] for i in range(3)]
    to_local = (as_rows,) * 3 + (flat_rows,) * 3 + (lambda w: w[0],)
    weights, moments, averages = (
        [change(w) for change, w in zip(to_local, group)] for group in groups
    )
    bks = [Bucket(m.shape[1], m.shape[2], A) for m in maps]
    CL, CG, CH, NPd = weights[0].shape[2], weights[1].shape[2], weights[5].shape[1], weights[6].shape[1]
    sizes = (CL, CG, CH, NPd)
    CT = CL + CG
    args = {}
    for q in (0, 1):
        args[n.maps + str(q)] = maps[q].reshape(-1, CT)
        args[n.up + str(q)] = ups[q].reshape(-1, CT)
        for name, table in zip(TABLES, tables_of(bks[q])):
            args[name + str(q)] = jnp.asarray(table)
    flat_maps = [args[n.maps0], args[n.maps1]]
    args.update(zip(KINDS, weights))
    args[old_of(n.nm)] = weights[6]
    fwd = forward_call(bks, A, B, sizes, True, 1, args)
    bwd = backward_call(bks, A, B, sizes, 2, {**args, **fwd})
    block = [bwd[n.block0], bwd[n.block1]]
    back = [args[n.up + str(q)] + bwd[n.back + str(q)] for q in (0, 1)]
    again = {**args, **bwd, n.halo0: fwd[n.halo0], n.halo1: fwd[n.halo1]}
    for name, weight, moment in zip(KINDS, weights, moments):
        again[old_of(name)] = weight
        again[moment_of(name)] = moment
    fresh = forward_call(bks, A, B, sizes, False, 3, again)
    grads = (fresh[n.flat1], bwd[n.flat3], bwd[n.gnorm])
    updated, velocity, smoothed, half = update_call(A, B, sizes, grads, weights, moments, averages)
    rerun = finish_call(bks, B, flat_maps, fresh)
    out = []
    for pair in (block, back, rerun):
        out += [value.reshape(m.shape) for value, m in zip(pair, maps)]
    to_outer = (from_rows,) * 3 + (from_flat,) * 3 + (lambda w: w[None],)
    for i in range(7):
        out += [to_outer[i](group[i]) for group in (updated, velocity, smoothed, half)]
    return tuple(out)


def solution(mesh):
    cells = P("img", "ha", None, None)
    kernel = P(None, None, None, None, "ha")
    matrix = P(None, None, "ha")
    return jax.shard_map(
        per_device,
        mesh=mesh,
        in_specs=(cells,) * 4 + (kernel,) * 9 + (matrix,) * 12,
        out_specs=(cells,) * 6 + (kernel,) * 12 + (matrix,) * 16,
        check_vma=False,
    )
```

```python
import functools
import math

import jax
import jax.numpy as jnp
import numpy as np
from jax import lax
from jax.experimental import pallas as pl
from jax.experimental.pallas import tpu as pltpu
from jax.sharding import PartitionSpec as P

STEP = 6

epsilon = 1e-05
learn_rate = 3e-05
momentum = 0.5

f32 = jnp.float32
bf16 = jnp.bfloat16
MESH = pl.DeviceIdType.MESH
VMEM_LIMIT = 60 * 1024 * 1024

NN = (((1,), (0,)), ((), ()))
NT = (((1,), (1,)), ((), ()))
TN = (((0,), (0,)), ((), ()))


def dg(left, right, dims):
    return lax.dot_general(left, right, dims, preferred_element_type=f32)


def split(value):
    high = value.astype(bf16)
    return high, (value - high.astype(f32)).astype(bf16)


def dot3(left, right, dims):
    lh, ll = left
    rh, rl = right
    return dg(lh, rh, dims) + dg(ll, rh, dims) + dg(lh, rl, dims)


def sigmoid(v):
    return 1.0 / (1.0 + jnp.exp(-v))


def pad_to(n, m):
    return -(-n // m) * m


def chunks(count, step, body, carry):
    def run(i, carry):
        return body(pl.multiple_of(i * step, 8), carry)

    return lax.fori_loop(0, count // step, run, carry)


class Bucket:
    def __init__(self, rows, width, group):
        self.R, self.W, self.A = rows, width, group
        self.H = rows * group
        self.N = rows * width
        self.nb = -(-(width // 2) // group)
        self.Cp = pad_to(self.nb * rows, 8)
        self.Q = (self.nb + 1) * self.H
        self.MB = max(r * width for r in range(1, rows + 1) if rows % r == 0 and r * width <= 384)


def hi_lo(table):
    table = np.asarray(table, np.float64)
    high = table.astype(np.float32).astype(jnp.bfloat16)
    low = (table - high.astype(np.float64)).astype(np.float32).astype(jnp.bfloat16)
    return np.stack([high, low])


def tables_of(bk):
    A, nb, W, H, R = bk.A, bk.nb, bk.W, bk.H, bk.R
    row = np.zeros((2, nb, A, W))
    w = np.arange(W)
    for b in range(nb):
        for d in range(A):
            j = d * nb + b
            if j == 0:
                row[0, b, d] = 1.0
                row[1, b, d] = np.cos(math.pi * w)
            elif 2 * j < W:
                row[0, b, d] = np.cos(2 * math.pi * (j * w % W) / W)
                row[1, b, d] = -np.sin(2 * math.pi * (j * w % W) / W)
    row = row.reshape(2 * nb * A, W) / math.sqrt(W)
    k = np.arange(H)[:, None]
    h = np.array([s * R + r for r in range(R) for s in range(A)])[None, :]
    phase = 2 * math.pi * (k * h % H) / H
    cos, sin = np.cos(phase) / math.sqrt(H), np.sin(phase) / math.sqrt(H)
    none = np.zeros_like(cos)
    plain = np.block([[cos, sin], [-sin, cos]])
    packed = np.block([[cos, none], [-sin, none], [none, cos], [none, -sin]])
    other = np.concatenate([plain, np.zeros_like(plain)], 0)
    first = np.stack([hi_lo(packed), hi_lo(other)])
    return (
        hi_lo(row),
        hi_lo(row.T),
        hi_lo(plain),
        hi_lo(plain.T),
        first,
        np.swapaxes(first, 2, 3),
    )


class Names:
    def __getattr__(self, name):
        return name


n = Names()
TABLES = (n.row, n.rowT, n.col, n.colT, n.col0, n.col0T)
SPECTRA = (n.sendA, n.recvA, n.sendB, n.recvB)


def for_both(*names):
    return [name + str(q) for q in (0, 1) for name in names]


class View:
    def __init__(self, refs, q):
        self.refs, self.q = refs, q

    def __getattr__(self, name):
        return getattr(self.refs, name + str(self.q))


class Fields:
    pass


def take(names, refs):
    out = Fields()
    for name, ref in zip(names, refs):
        setattr(out, name, ref)
    return out


class Group:
    def __init__(self, ssem, rsem, landed):
        self.ssem, self.rsem, self.landed = ssem, rsem, landed

    def wait_recv(self):
        pltpu.make_async_copy(self.landed, self.landed, self.rsem).wait()

    def wait_send(self):
        pltpu.make_async_copy(self.landed, self.landed, self.ssem).wait()


class Comm:
    def __init__(self, A, B):
        self.A, self.B = A, B
        self.a = lax.axis_index("ha")
        self.z = lax.axis_index("img")
        self.pending, self.halos = [], []

    def enter(self):
        bar = pltpu.get_barrier_semaphore()
        for d in range(1, self.A):
            pl.semaphore_signal(
                bar, inc=1, device_id=(self.z, lax.rem(self.a + d, self.A)), device_id_type=MESH
            )
        for d in range(1, self.B):
            pl.semaphore_signal(
                bar, inc=1, device_id=(lax.rem(self.z + d, self.B), self.a), device_id_type=MESH
            )

    def entered(self):
        pl.semaphore_wait(pltpu.get_barrier_semaphore(), self.A + self.B - 2)

    def make(self, src, dst, ssem, rsem, ha=None, img=None):
        return pltpu.make_async_remote_copy(
            src,
            dst,
            ssem,
            rsem,
            device_id=(self.z if img is None else img, self.a if ha is None else ha),
            device_id_type=MESH,
        )

    def send(self, *args, **kwargs):
        copy = self.make(*args, **kwargs)
        copy.start()
        self.pending.append(copy)
        return copy

    def group(self, moves, ssem, rsem, landed):
        for src, dst, where in moves:
            self.make(src, dst, ssem, rsem, **where).start()
        group = Group(ssem, rsem, landed)
        self.pending.append(group)
        return group

    def finish(self):
        self.halo_sent()
        for copy in self.pending:
            copy.wait_send()

    def sum_start(self, f, k, q, sums, first=True):
        i = 2 * k + q
        for part in (0, 1):
            value = jnp.sum(sums[part], 0, keepdims=True)
            for t in range(-(-value.shape[1] // 128)):
                piece = value[:, 128 * t : 128 * (t + 1)]
                f.sum_src[i, 4 * part + t : 4 * part + t + 1, : piece.shape[1]] = piece
        return self.sum_stage(f, i, first, f.sum_src[i])

    def sum_stage(self, f, i, rows, value):
        count, me = (self.A, self.a) if rows else (self.B, self.z)
        buf, ssem, rsem = (f.sum_a, f.sum_as, f.sum_ar) if rows else (f.sum_z, f.sum_zs, f.sum_zr)
        buf[i, me] = value
        mine = buf.at[i, me]
        name = n.ha if rows else n.img
        moves = [(mine, mine, {name: lax.rem(me + d, count)}) for d in range(1, count)]
        group = None
        if moves:
            group = self.group(moves, ssem.at[i], rsem.at[i], buf.at[i, pl.ds(0, count - 1)])
        return rows, buf, count, group

    def sum_total(self, i, stage):
        rows, buf, count, group = stage
        if group is not None:
            group.wait_recv()
        total = buf[i, 0]
        for d in range(1, count):
            total = total + buf[i, d]
        return total

    def sum_cross(self, f, k, q, stage):
        i = 2 * k + q
        return self.sum_stage(f, i, not stage[0], self.sum_total(i, stage))

    def sum_end(self, f, k, q, stage):
        i = 2 * k + q
        f.sum_out[i] = self.sum_total(i, stage)

    def swap_start(self, src, dst, ssem, rsem, rows):
        def block(ref, t):
            return ref.at[:, pl.ds(pl.multiple_of(t * rows, 8), rows)]

        moves = []
        for d in range(1, self.A):
            t = lax.rem(self.a + d, self.A)
            moves.append((block(src, t), block(dst, self.a), {n.ha: t}))
        group = self.group(moves, ssem, rsem, dst.at[:, pl.ds(0, (self.A - 1) * rows)])
        mine = pl.ds(pl.multiple_of(self.a * rows, 8), rows)
        dst[:, mine, :] = src[:, mine, :]
        return group

    def swap_end(self, group):
        group.wait_recv()

    def halo_start(self, low_row, high_row, dst, ssem, rsem):
        up = jnp.maximum(self.a - 1, 0)
        down = jnp.minimum(self.a + 1, self.A - 1)
        low = self.make(low_row, dst.at[1], ssem.at[0], rsem.at[0], ha=up)
        high = self.make(high_row, dst.at[0], ssem.at[1], rsem.at[1], ha=down)

        @pl.when(self.a > 0)
        def _():
            low.start()

        @pl.when(self.a < self.A - 1)
        def _():
            high.start()

        self.halos.append((low, high))
        return [(low, high)]

    def halo_end(self, pairs):
        for low, high in pairs:

            @pl.when(self.a < self.A - 1)
            def _():
                low.wait_recv()

            @pl.when(self.a > 0)
            def _():
                high.wait_recv()

    def halo_sent(self):
        for low, high in self.halos:

            @pl.when(self.a > 0)
            def _():
                low.wait_send()

            @pl.when(self.a < self.A - 1)
            def _():
                high.wait_send()

        self.halos = []


def column_sum(value):
    rows, width = value.shape
    return jnp.sum(value.reshape(rows // 8, 8, width), 0)


def no_sums(width):
    return jnp.zeros((8, width), f32), jnp.zeros((8, width), f32)


def totals(ref, k, q, width):
    i = 2 * k + q
    return [
        jnp.concatenate([ref[i, t : t + 1, :] for t in range(first, first + 4)], 1)[:, :width]
        for first in (0, 4)
    ]


def norm_rows(ref, k, q, width, count):
    total, square = totals(ref, k, q, width)
    center = total * (1.0 / count)
    variance = square * (1.0 / count) - center * center
    return center, lax.rsqrt(variance + epsilon)


def row_transform(bk, table, source, send):
    nbA = bk.nb * bk.A
    tab = (table[0], table[1])
    for h in range(bk.R):
        out = dot3(tab, split(source(h)), NN)
        out = jnp.concatenate([out[:nbA], out[nbA:]], 1)
        for b in range(bk.nb):
            put_strided(send, b * bk.R + h, bk.A, bk.Cp, out[b * bk.A : (b + 1) * bk.A])


def row_back(bk, table, recv, h):
    parts = [get_strided(recv, b * bk.R + h, bk.A, bk.Cp) for b in range(bk.nb)]
    block = jnp.concatenate(parts, 0) if len(parts) > 1 else parts[0]
    half = block.shape[1] // 2
    block = jnp.concatenate([block[:, :half], block[:, half:]], 0)
    return dot3((table[0], table[1]), split(block), NN)


def put_strided(ref, start, count, stride, value):
    for t in range(ref.shape[0]):
        ref[t, pl.ds(start, count, stride=stride), :] = value[:, 128 * t : 128 * (t + 1)]


def get_strided(ref, start, count, stride):
    return jnp.concatenate(
        [ref[t, pl.ds(start, count, stride=stride), :] for t in range(ref.shape[0])], 1
    )


def first_table(ref, other):
    return ref[other, 0], ref[other, 1]


def col_transform(bk, f_col, f_col0, other, recv, put):
    H = bk.H
    for b in range(bk.nb):
        block = jnp.concatenate(
            [get_strided(recv, b * bk.R + h, bk.A, bk.Cp) for h in range(bk.R)], 0
        )
        half = block.shape[1] // 2
        block = split(jnp.concatenate([block[:, :half], block[:, half:]], 0))
        if b == 0:
            out = dot3(first_table(f_col0, other), block, NN)
            put(bk.nb, jnp.concatenate([out[2 * H : 3 * H], out[3 * H :]], 1))
        else:
            out = dot3((f_col[0], f_col[1]), block, NN)
        put(b, jnp.concatenate([out[:H], out[H : 2 * H]], 1))


def col_back(bk, f_colT, f_col0T, other, get, scale, send):
    H = bk.H

    def halves(value):
        half = value.shape[1] // 2
        return [value[:, :half], value[:, half:]]

    for b in range(bk.nb):
        if b == 0:
            block = jnp.concatenate(halves(get(0)) + halves(get(bk.nb)), 0)
            out = dot3(first_table(f_col0T, other), split(block), NN)
        else:
            out = dot3((f_colT[0], f_colT[1]), split(jnp.concatenate(halves(get(b)), 0)), NN)
        out = jnp.concatenate([out[:H], out[H:]], 1)
        out = scale(b, out)
        for h in range(bk.R):
            put_strided(send, b * bk.R + h, bk.A, bk.Cp, out[h * bk.A : (h + 1) * bk.A])


def conv_forward(bk, zh, zl, knh, knl, koh, kol, out):
    MB, W = bk.MB, bk.W
    col = lax.broadcasted_iota(jnp.int32, (MB, 1), 0) % W

    def combine(value, n):
        low = jnp.where(col == 0, 0.0, pltpu.roll(value[:, :n], 1, 0))
        high = jnp.where(col == W - 1, 0.0, pltpu.roll(value[:, 2 * n :], MB - 1, 0))
        return low + value[:, n : 2 * n] + high

    def body(i, carry):
        r = pl.multiple_of(i * MB, 32)
        total = None
        for a in range(3):
            left = (zh[pl.ds(r + a * W, MB), :], zl[pl.ds(r + a * W, MB), :])
            n = knh.shape[2]
            right = (knh[:, a].reshape(3 * n, -1), knl[:, a].reshape(3 * n, -1))
            part = dot3(left, right, NT)
            total = part if total is None else total + part
        CL = knh.shape[2]
        out[pl.ds(r, MB), :CL] = combine(total, CL)
        left = tuple(
            jnp.concatenate([z[pl.ds(r + a * W, MB), :CL] for a in range(3)], 1) for z in (zh, zl)
        )
        cross = dot3(left, (koh[...], kol[...]), NT)
        out[pl.ds(r, MB), CL:] = combine(cross, koh.shape[0] // 3)
        return carry

    lax.fori_loop(0, bk.N // MB, body, 0)


GATHERED = (n.sq, n.nm, n.fo)


class Loader:
    def __init__(self, sems):
        self.sems, self.copies, self.done = sems, {}, set()

    def start(self, name, src, dst):
        copy = pltpu.make_async_copy(src, dst, self.sems.at[len(self.copies)])
        copy.start()
        self.copies[name] = copy

    def wait(self, *names):
        for name in names:
            if name not in self.done:
                self.copies[name].wait()
                self.done.add(name)


KINDS = (n.near, n.inw, n.outw, n.sq, n.fo, n.ex, n.nm)


def old_of(name):
    return name + n._old


def moment_of(name):
    return name + n._moment


def whole_of(name):
    return n.g_ + name


def gather_direct(c, f, name, i):
    shard, whole = getattr(f, name), getattr(f, whole_of(name))
    whole[c.a] = shard[...]
    moves = [(shard, whole.at[c.a], {n.ha: lax.rem(c.a + d, c.A)}) for d in range(1, c.A)]
    return c.group(moves, f.g1s.at[i], f.g1r.at[i], whole.at[pl.ds(0, c.A - 1)])


class Pair:
    def __init__(self, c, f, name, i):
        self.c, self.f, self.i = c, f, i
        self.nc = c.A // 2
        self.chip, self.core = c.a // 2, c.a % 2
        self.sibling = 2 * self.chip + 1 - self.core
        self.whole = getattr(f, whole_of(name))
        shard, mine = getattr(f, name), self.whole.at[c.a]
        self.whole[c.a] = shard[...]
        moves = []
        for d in range(1, self.nc):
            moves.append((shard, mine, {n.ha: 2 * lax.rem(self.chip + d, self.nc) + self.core}))
        self.far = self.group(moves, 0)
        self.near = self.group([(shard, mine, {n.ha: self.sibling})], 1)

    def group(self, moves, k):
        f, i = self.f, self.i
        landed = self.whole.at[pl.ds(0, len(moves))]
        return self.c.group(moves, f.p1s.at[i, k], f.p1r.at[i, k], landed)

    def second(self):
        self.far.wait_recv()
        moves = []
        for d in range(1, self.nc):
            piece = self.whole.at[2 * lax.rem(self.chip + d, self.nc) + self.core]
            moves.append((piece, piece, {n.ha: self.sibling}))
        self.passed = self.group(moves, 2)

    def end(self):
        self.near.wait_recv()
        self.passed.wait_recv()


def grid_of(chips):
    across = max(x for x in range(1, chips + 1) if chips % x == 0 and x * x <= chips)
    return chips // across, across


class Spread:
    def __init__(self, c, f, names):
        self.c, self.f, self.names = c, f, names
        self.Y, self.X = grid_of(c.A // 2)
        self.chip, self.core = c.a // 2, c.a % 2
        self.y, self.x = self.chip // self.X, lax.rem(self.chip, self.X)

    def device(self, dy, dx, core=None):
        y, x = lax.rem(self.y + dy + self.Y, self.Y), lax.rem(self.x + dx + self.X, self.X)
        return 2 * (y * self.X + x) + (self.core if core is None else core)

    def part(self, ref, half, slot):
        if len(ref.shape) == 3:
            return ref.at[slot]
        cut = ref.shape[1] // 2
        return ref.at[slot, pl.ds(0, cut) if half == 0 else pl.ds(cut, ref.shape[1] - cut)]

    def lines(self, half, first):
        along_x = (half == 0) == first
        return [(0, d) for d in range(1, self.X)] if along_x else [(d, 0) for d in range(1, self.Y)]

    def members(self, half):
        for i, name in enumerate(self.names):
            if half == 0 or len(getattr(self.f, name).shape) == 3:
                yield i, name

    def pass_on(self, half, slots, lines, ssem, rsem):
        groups = []
        for i, name in self.members(half):
            ref = getattr(self.f, whole_of(name))
            moves = []
            for dy, dx in lines:
                for slot in slots:
                    piece = self.part(ref, half, slot)
                    moves.append((piece, piece, {n.ha: self.device(dy, dx)}))
            if moves:
                landed = self.part(ref, half, pl.ds(0, len(moves)))
                groups.append(self.c.group(moves, ssem.at[i, half], rsem.at[i, half], landed))
        return groups

    def start(self):
        f = self.f
        for name in self.names:
            getattr(f, whole_of(name))[self.c.a] = getattr(f, name)[...]
        self.one = []
        for half in (0, 1):
            self.one += self.pass_on(half, [self.c.a], self.lines(half, True), f.t1s, f.t1r)

    def second(self):
        f = self.f
        for group in self.one:
            group.wait_recv()
        self.two = []
        for half in (0, 1):
            slots = [self.device(-dy, -dx) for dy, dx in [(0, 0)] + self.lines(half, True)]
            self.two += self.pass_on(half, slots, self.lines(half, False), f.t2s, f.t2r)

    def third(self):
        f, c = self.f, self.c
        for group in self.two:
            group.wait_recv()
        self.three = []
        sibling = self.device(0, 0, 1 - self.core)
        for i, name in enumerate(self.names):
            ref = getattr(f, whole_of(name))
            moves = []
            for dy in range(self.Y):
                for dx in range(self.X):
                    piece = ref.at[self.device(dy, dx)]
                    moves.append((piece, piece, {n.ha: sibling}))
            landed = ref.at[pl.ds(0, len(moves))]
            self.three.append(c.group(moves, f.t3s.at[i], f.t3r.at[i], landed))

    def end(self):
        for group in self.three:
            group.wait_recv()


def far_of(name):
    return name + n._hbm


def forward_names(save):
    weights = list(KINDS)
    ins = for_both(*TABLES)
    if save:
        ins += weights[:-1] + [n.nm_old]
    else:
        ins += [n.seg1, n.flat3, n.gnorm] + [old_of(w) for w in weights]
        ins += [moment_of(w) for w in weights]
    kept = for_both(n.joined) + [n.sum_out, n.norms]
    extra = for_both(n.u, n.spec, n.mixed, n.s, n.halo)
    extra += [n.knh, n.knl, n.koh, n.kol, n.g_sq, n.g_fo, n.g_ex]
    if save:
        kept, extra = kept + extra, [n.nm]
    else:
        kept, extra = kept + [n.flat1], extra + weights + [n.zgs, n.zgr]
    scratch = [n.g_nm, n.g_near, n.g_inw, n.g_outw, n.ld]
    scratch += [n.sum_src, n.sum_a, n.sum_z, n.sum_as, n.sum_ar, n.sum_zs, n.sum_zr]
    scratch += [n.g1s, n.g1r, n.p1s, n.p1r, n.t1s, n.t1r, n.t2s, n.t2r, n.t3s, n.t3r, n.hs, n.hr, n.ws, n.wr]
    scratch += extra + for_both(n.maps, n.zh, n.zl, n.act, *SPECTRA)
    return ins, kept, scratch


def forward_far(save):
    return for_both(n.maps) if save else for_both(n.maps, n.halo)


def forward_kernel(bks, A, B, sizes, save, *refs):
    ins, kept, scratch = forward_names(save)
    far = forward_far(save)
    names = ins + [far_of(k) for k in far] + [far_of(k) for k in kept] + kept + scratch
    f = take(names, refs)
    CL, CG, CH, NPd = sizes
    CT = CL + CG
    c = Comm(A, B)
    c.enter()
    keeper = Loader(f.ld)
    for name in far:
        keeper.start(name, getattr(f, far_of(name)), getattr(f, name))
    other = jnp.minimum(c.a, 1)
    once = jnp.where(c.a == 0, 1.0, 2.0)
    cells = [B * bk.H * bk.W for bk in bks]
    freqs = [B * bk.H * (bk.W // 2 + 1) for bk in bks]
    views = [View(f, 0), View(f, 1)]
    both = (0, 1)

    def keep(*which):
        for k in which:
            if k in kept:
                keeper.start(k, getattr(f, k), getattr(f, far_of(k)))

    f.sum_src[...] = jnp.zeros_like(f.sum_src)
    c.entered()
    if not save:
        shares = spread_images(c, f)
        renew_small(f, A, sizes)
    else:
        f.nm[...] = jnp.zeros_like(f.nm)
        f.nm[0:2, :NPd] = f.nm_old[...]
    first = Pair(c, f, n.sq, 0)
    table = gather_direct(c, f, n.nm, 0)
    if save:
        middle = Pair(c, f, n.fo, 1)
        spread = Spread(c, f, (n.ex, n.near, n.inw, n.outw))
        spread.start()
    for q in both:
        bk, g = bks[q], views[q]
        keeper.wait(n.maps + str(q))

        def body(r, carry, bk=bk, g=g):
            src = pl.multiple_of(r * bk.W, bk.W)
            high, low = split(g.maps[pl.ds(src, bk.W), :])
            g.zh[pl.ds(src + bk.W, bk.W), :] = high
            g.zl[pl.ds(src + bk.W, bk.W), :] = low
            return carry

        lax.fori_loop(0, bk.R, body, 0)
    first.second()
    first.end()

    wsq = split(f.g_sq[...].reshape(CH, CG))
    keep(n.g_sq)
    adding = [None, None]
    for q in both:
        bk, g = bks[q], views[q]

        def body(r, carry, bk=bk, g=g):
            at = pl.multiple_of(r + bk.W, 32)
            value = dot3((g.zh[pl.ds(at, bk.MB), CL:], g.zl[pl.ds(at, bk.MB), CL:]), wsq, NT)
            g.s[pl.ds(r, bk.MB), :] = value
            return carry[0] + column_sum(value), carry[1] + column_sum(value * value)

        adding[q] = c.sum_start(f, 0, q, chunks(bk.N, bk.MB, body, no_sums(CH)), not save)
        keep(n.s + str(q))

    table.wait_recv()
    piece = f.g_nm.shape[2]
    span = pad_to(NPd * A, 128) + 128
    norms = None
    for d in range(A):
        part = jnp.concatenate([f.g_nm[d], jnp.zeros((8, span - piece), f32)], 1)
        if d:
            part = pltpu.roll(part, NPd * d, 1)
        norms = part if norms is None else norms + part
    f.norms[0] = norms[:, :CT]
    f.norms[1] = pltpu.roll(norms, span - CT, 1)[:, :CT]
    f.norms[2] = pltpu.roll(norms, span - CT - CH, 1)[:, :CT]

    keep(n.norms)
    for q in both:
        adding[q] = c.sum_cross(f, 0, q, adding[q])
    if not save:
        shares.wait_recv()
        keep(n.flat1)
        renew_large(f, A, B, sizes)
        middle = Pair(c, f, n.fo, 1)
        spread = Spread(c, f, (n.ex, n.near, n.inw, n.outw))
        spread.start()
    swaps = [None, None]
    for q in both:
        bk, g = bks[q], views[q]
        c.sum_end(f, 0, q, adding[q])
        center, inverse = norm_rows(f.sum_out, 0, q, CH, cells[q])

        def source(h, bk=bk, g=g, center=center, inverse=inverse):
            rows = slice(h * bk.W, (h + 1) * bk.W)
            v = (g.s[rows, :] - center) * inverse * f.norms[1, 0:1, :CH] + f.norms[1, 1:2, :CH]
            value = v * sigmoid(v)
            g.act[rows, :] = value
            return value

        row_transform(bk, g.row, source, g.sendA)
        swaps[q] = c.swap_start(g.sendA, g.recvA, f.ws.at[0, q], f.wr.at[0, q], bk.Cp)

    middle.second()
    spread.second()
    c.swap_end(swaps[0])
    middle.end()
    keep(n.g_fo)
    wfo = split(f.g_fo[...].reshape(2 * CH, 2 * CH))
    for q in both:
        bk, g = bks[q], views[q]
        if q:
            c.swap_end(swaps[q])

        def put(slot, value, g=g, bk=bk):
            g.spec[slot * bk.H : (slot + 1) * bk.H, :] = value

        col_transform(bk, g.col, g.col0, other, g.recvA, put)
        keep(n.spec + str(q))

        def body(r, carry, bk=bk, g=g):
            value = dot3(split(g.spec[pl.ds(r, bk.Q // 2), :]), wfo, NT)
            g.mixed[pl.ds(r, bk.Q // 2), :] = value
            return carry[0] + column_sum(value), carry[1] + column_sum(value * value)

        adding[q] = c.sum_start(f, 1, q, chunks(bk.Q, bk.Q // 2, body, no_sums(2 * CH)), False)
        keep(n.mixed + str(q))
    def convolve(q):
        bk, g = bks[q], views[q]
        conv_forward(bk, g.zh, g.zl, f.knh, f.knl, f.koh, f.kol, g.joined)

    def spectra_back(q):
        bk, g = bks[q], views[q]
        c.sum_end(f, 1, q, adding[q])
        center, inverse = norm_rows(f.sum_out, 1, q, 2 * CH, freqs[q])

        def get(slot, g=g, center=center, inverse=inverse, bk=bk):
            value = g.mixed[slot * bk.H : (slot + 1) * bk.H, :]
            v = (value - center) * inverse * f.norms[2, 0:1, : 2 * CH] + f.norms[2, 1:2, : 2 * CH]
            return v * sigmoid(v)

        def scale(b, value):
            return value * (once if b == 0 else 2.0)

        col_back(bk, g.colT, g.col0T, other, get, scale, g.sendB)
        swaps[q] = c.swap_start(g.sendB, g.recvB, f.ws.at[1, q], f.wr.at[1, q], bk.Cp)

    for q in both:
        adding[q] = c.sum_cross(f, 1, q, adding[q])
    halos = []
    if save:
        for q in both:
            bk, g = bks[q], views[q]
            halos += c.halo_start(
                g.maps.at[pl.ds(0, bk.W)],
                g.maps.at[pl.ds(bk.N - bk.W, bk.W)],
                g.halo,
                f.hs.at[q],
                f.hr.at[q],
            )
    spread.third()
    c.halo_end(halos)
    for q in both:
        bk, g = bks[q], views[q]
        if not save:
            keeper.wait(n.halo + str(q))
        for side, at, edge in ((0, 0, 0), (1, bk.N + bk.W, A - 1)):
            if save:
                g.halo[side] = jnp.where(c.a == edge, 0.0, g.halo[side])
            high, low = split(g.halo[side])
            g.zh[pl.ds(at, bk.W), :] = high
            g.zl[pl.ds(at, bk.W), :] = low
        keep(n.halo + str(q))
    spectra_back(0)
    spectra_back(1)
    spread.end()
    keep(n.g_ex)

    def taps(t, carry):
        a, b = t // 3, t % 3
        near = f.g_near[:, pl.ds(t, 1)].reshape(CL, CL)
        inward = f.g_inw[:, pl.ds(t, 1)].reshape(CL, CG)
        high, low = split(jnp.concatenate([near, inward], 1))
        f.knh[b, a] = high
        f.knl[b, a] = low
        return carry

    lax.fori_loop(0, 9, taps, 0)
    for a in range(3):
        for b in range(3):
            high, low = split(f.g_outw[:, 3 * a + b].reshape(CG, CL))
            f.koh[b * CG : (b + 1) * CG, a * CL : (a + 1) * CL] = high
            f.kol[b * CG : (b + 1) * CG, a * CL : (a + 1) * CL] = low
    keep(n.knh, n.knl, n.koh, n.kol)
    convolve(0)
    convolve(1)

    wex = split(f.g_ex[...].reshape(CG, CH))
    for q in both:
        bk, g = bks[q], views[q]
        c.swap_end(swaps[q])
        for h in range(bk.R):
            rows = slice(h * bk.W, (h + 1) * bk.W)
            g.u[rows, :] = g.act[rows, :] + row_back(bk, g.rowT, g.recvB, h)
        keep(n.u + str(q))

        def body(r, carry, bk=bk, g=g):
            rows = pl.ds(r, bk.MB)
            value = g.joined[rows, CL:] + dot3(split(g.u[rows, :]), wex, NT)
            g.joined[rows, CL:] = value
            value = jnp.concatenate([g.joined[rows, :CL], value], 1)
            return carry[0] + column_sum(value), carry[1] + column_sum(value * value)

        adding[q] = c.sum_start(f, 2, q, chunks(bk.N, bk.MB, body, no_sums(CT)))
        keep(n.joined + str(q))
    for q in both:
        adding[q] = c.sum_cross(f, 2, q, adding[q])
    for q in both:
        c.sum_end(f, 2, q, adding[q])
    keep(n.sum_out)
    keeper.wait(*[k for k in keeper.copies if k in kept])
    c.finish()


def renewed(weight, moment, grad):
    return weight - learn_rate * (grad + momentum * (momentum * moment + grad))


def piece_of(flat, A, B, sizes, second, at, count):
    rows = flat_rows_of(A, B, sizes)
    pieces = []
    while count:
        k, off = (2, at) if second else divmod(at, rows[0])
        part = rows[k] // B
        z, off = divmod(off, part)
        take_now = min(count, part - off)
        start = (z * sum(rows) + sum(rows[:k])) // B + off
        pieces.append(flat[start : start + take_now, :])
        at, count = at + take_now, count - take_now
    return jnp.concatenate(pieces, 0) if len(pieces) > 1 else pieces[0]


def unpack(flat, A, B, sizes, second, at, count, tiles):
    unit = pad_to(count, 8)
    return jnp.concatenate(
        [piece_of(flat, A, B, sizes, second, at + t * unit, count) for t in range(tiles)], 1
    )


def unpack_tap(flat, A, B, sizes, k):
    CL, CG, CH, NPd = sizes
    first = flat_plan(A, sizes)[0]
    o, p, tiles = CL // A, CG // A, (CL + CG) // 128
    return (
        unpack(flat, A, B, sizes, False, first[0] + k * pad_to(o, 8) * tiles, o, tiles),
        unpack(flat, A, B, sizes, False, first[1] + k * pad_to(p, 8), p, CL // 128),
    )


def unpack_squeeze(flat, A, sizes):
    CH, CG = sizes[2], sizes[1]
    o = CH // A
    unit = pad_to(o, 8)
    return jnp.concatenate([flat[t * unit : t * unit + o, :] for t in range(CG // 128)], 1)


def unpack_matrices(flat1, flat3, A, B, sizes):
    CL, CG, CH, NPd = sizes
    first = flat_plan(A, sizes)[0]
    return (
        unpack_squeeze(flat3, A, sizes) if flat3 is not None else None,
        unpack(flat1, A, B, sizes, True, 0, 2 * CH // A, 2 * CH // 128),
        unpack(flat1, A, B, sizes, False, first[2], CG // A, pad_to(CH, 128) // 128)[:, :CH],
    )


def spread_images(c, f):
    part = f.seg1.shape[0]
    mine = pl.ds(pl.multiple_of(c.z * part, 8), part)
    f.flat1[mine, :] = f.seg1[...]
    moves = [
        (f.seg1, f.flat1.at[mine], {n.img: lax.rem(c.z + d, c.B)}) for d in range(1, c.B)
    ]
    return c.group(moves, f.zgs.at[0], f.zgr.at[0], f.flat1.at[pl.ds(0, (c.B - 1) * part)])


def renew_small(f, A, sizes):
    f.sq[...] = renewed(f.sq_old[...], f.sq_moment[...], unpack_squeeze(f.flat3, A, sizes))
    P = sizes[3]
    f.nm[...] = jnp.zeros_like(f.nm)
    f.nm[0:2, :P] = renewed(f.nm_old[...], f.nm_moment[...], f.gnorm[0:2, :P])


def renew_large(f, A, B, sizes):
    CL = sizes[0]
    for k in range(9):
        both, out = unpack_tap(f.flat1, A, B, sizes, k)
        f.near[k] = renewed(f.near_old[k], f.near_moment[k], both[:, :CL])
        f.inw[k] = renewed(f.inw_old[k], f.inw_moment[k], both[:, CL:])
        f.outw[k] = renewed(f.outw_old[k], f.outw_moment[k], out)
    sq, fo, ex = unpack_matrices(f.flat1, None, A, B, sizes)
    f.fo[...] = renewed(f.fo_old[...], f.fo_moment[...], fo)
    f.ex[...] = renewed(f.ex_old[...], f.ex_moment[...], ex)


def forward_shapes(bks, A, B, sizes):
    CL, CG, CH, NPd = sizes
    CT = CL + CG
    sd = {n.sum_out: (6, 8, 128), n.norms: (3, 8, CT)}
    sd[n.knh] = sd[n.knl] = (3, 3, CL, CT)
    sd[n.koh] = sd[n.kol] = (3 * CG, 3 * CL)
    for name, shape in (
        (n.sq, (CH // A, CG)),
        (n.fo, (2 * CH // A, 2 * CH)),
        (n.ex, (CG // A, CH)),
        (n.nm, (8, pad_to(NPd, 128))),
        (n.near, (9, CL // A, CL)),
        (n.inw, (9, CL // A, CG)),
        (n.outw, (9, CG // A, CL)),
    ):
        sd[name] = shape
        sd[whole_of(name)] = (A,) + shape
    sd[n.flat1] = (sum(flat_rows_of(A, B, sizes)), 128)
    sd[n.seg1] = (sum(flat_rows_of(A, B, sizes)) // B, 128)
    for q, bk in enumerate(bks):
        here = {
            n.maps: (bk.N, CT),
            n.up: (bk.N, CT),
            n.joined: (bk.N, CT),
            n.u: (bk.N, CH),
            n.spec: (bk.Q, 2 * CH),
            n.mixed: (bk.Q, 2 * CH),
            n.s: (bk.N, CH),
            n.halo: (2, bk.W, CT),
            n.zh: ((bk.R + 2) * bk.W, CT),
            n.zl: ((bk.R + 2) * bk.W, CT),
            n.act: (bk.N, CH),
        }
        for name in SPECTRA:
            here[name] = (2 * CH // 128, A * bk.Cp, 128)
        for name, shape in here.items():
            sd[name + str(q)] = shape
    sd[n.sum_src] = (6, 8, 128)
    sd[n.sum_a] = (6, A, 8, 128)
    sd[n.sum_z] = (6, B, 8, 128)
    return sd


HALF = {n.knh, n.knl, n.koh, n.kol, n.dth, n.dtl, n.zh, n.zl} | set(for_both(n.zh, n.zl, n.dh, n.dl))


def memory(name, sd, sems):
    if name in sems:
        return pltpu.SemaphoreType.DMA(sems[name])
    return pltpu.VMEM(sd[name], bf16 if name in HALF else f32)


def result(name, sd):
    return jax.ShapeDtypeStruct(sd[name], bf16 if name in HALF else f32)


def sum_sems(A, B):
    return {
        n.sum_as: (6,),
        n.sum_ar: (6,),
        n.sum_zs: (6,),
        n.sum_zr: (6,),
        n.hs: (2, 2),
        n.hr: (2, 2),
        n.ws: (2, 2),
        n.wr: (2, 2),
    }


VM = pl.BlockSpec(memory_space=pltpu.VMEM)
FAR = pl.BlockSpec(memory_space=pl.ANY)


def forward_call(bks, A, B, sizes, save, cid, args):
    sd = forward_shapes(bks, A, B, sizes)
    ins, kept, scratch = forward_names(save)
    sems = sum_sems(A, B)
    far = forward_far(save)
    sems[n.ld] = (len(kept) + len(far),)
    sems[n.g1s] = sems[n.g1r] = (1,)
    sems[n.p1s] = sems[n.p1r] = (2, 3)
    for name in (n.t1s, n.t1r, n.t2s, n.t2r):
        sems[name] = (5, 2)
    sems[n.t3s] = sems[n.t3r] = (5,)
    sems[n.zgs] = sems[n.zgr] = (1,)
    results = kept
    macs = sum(bk.N for bk in bks) * 1400000
    res = pl.pallas_call(
        functools.partial(forward_kernel, bks, A, B, sizes, save),
        out_shape=[result(name, sd) for name in results],
        in_specs=[VM] * len(ins) + [FAR] * len(far),
        out_specs=[FAR] * len(kept),
        scratch_shapes=[memory(name, sd, sems) for name in kept + scratch],
        compiler_params=pltpu.CompilerParams(
            collective_id=cid, has_side_effects=True, vmem_limit_bytes=VMEM_LIMIT
        ),
        cost_estimate=pl.CostEstimate(flops=6 * macs, bytes_accessed=40_000_000, transcendentals=0),
        name=n.forward,
    )(*[args[name] for name in ins + far])
    return dict(zip(results, res))


def finish_kernel(counts, A, B, sizes, *refs):
    maps, joined, sums, norms = refs[0:2], refs[2:4], refs[4], refs[5]
    outs = refs[30:32]

    @pl.when(pl.program_id(0) == 0)
    def _():
        update(A, B, sizes, *refs[6:30], *refs[32:])

    for q in (0, 1):
        center, inverse = norm_rows(sums, 2, q, norms.shape[2], counts[q])
        v = (joined[q][...] - center) * inverse * norms[0, 0:1, :] + norms[0, 1:2, :]
        outs[q][...] = maps[q][...] + v * sigmoid(v)


def finish_call(bks, A, B, sizes, maps, fwd, grads, weights, moments, averages):
    N, CT = maps[0].shape
    step = N // 3 if N % 24 == 0 else N
    block = pl.BlockSpec((step, CT), lambda i: (i, 0))
    counts = [B * bk.H * bk.W for bk in bks]
    shapes = [w.shape for w in weights]
    outs = [jax.ShapeDtypeStruct(m.shape, f32) for m in maps]
    outs += [jax.ShapeDtypeStruct(s, f32) for _ in range(3) for s in shapes]
    outs += [jax.ShapeDtypeStruct(s, bf16) for s in shapes]
    res = pl.pallas_call(
        functools.partial(finish_kernel, counts, A, B, sizes),
        out_shape=outs,
        grid=(N // step,),
        in_specs=[block] * 4 + [VM] * 26,
        out_specs=[block] * 2 + [VM] * 28,
        compiler_params=pltpu.CompilerParams(vmem_limit_bytes=VMEM_LIMIT),
        cost_estimate=pl.CostEstimate(
            flops=N * CT * 20, bytes_accessed=N * CT * 24, transcendentals=N * CT * 2
        ),
        name=n.finish,
    )(
        *maps,
        *[fwd[name] for name in (n.joined0, n.joined1, n.sum_out, n.norms)],
        *grads,
        *weights,
        *moments,
        *averages,
    )
    return res[:2], (res[2:9], res[9:16], res[16:23], res[23:30])


def flat_plan(A, sizes):
    CL, CG, CH, NPd = sizes
    CT = CL + CG

    def rows(count, width):
        return pad_to(count // A, 8) * pad_to(width, 128) // 128

    near, outw = 9 * rows(CL, CT), 9 * rows(CG, CL)
    first = (0, near, near + outw)
    return first, near + outw + rows(CG, CH), rows(2 * CH, 2 * CH), rows(CH, CG)


def flat_rows_of(A, B, sizes):
    first, end1, rows2, rows3 = flat_plan(A, sizes)
    half = pad_to(end1, 16 * B) // 2
    return half, half, pad_to(rows2, 8 * B)


LATE = for_both(n.joined, n.up) + for_both(n.maps, n.halo, n.u, n.mixed, n.spec, n.s)
LATE += [n.g_fo, n.knh, n.knl, n.koh, n.kol, n.g_sq]


def backward_names():
    ins = [n.sum_out, n.norms, n.g_ex] + for_both(*TABLES)
    outs = []
    kept = [n.seg1, n.flat3, n.gnorm] + for_both(n.back, n.block)
    scratch = [n.sum_src, n.sum_a, n.sum_z, n.bsum, n.sum_as, n.sum_ar, n.sum_zs, n.sum_zr]
    scratch += [n.hs, n.hr, n.ws, n.wr, n.ld, n.rs1s, n.rs1r, n.rs2s, n.rs2r, n.rs3s, n.rs3r, n.rs5s, n.rs5r]
    scratch += [n.das, n.dar, n.dzs, n.dzr, n.cs, n.cr]
    scratch += [n.dth, n.dtl, n.zh, n.zl, n.gsq, n.gfo]
    scratch += [n.own1, n.sib1, n.far1, n.last1, n.zin1, n.own2, n.sib2, n.far2, n.zin2, n.own3, n.far3, n.zin3]
    scratch += [n.seg1, n.flat3, n.gnorm, n.tot2]
    scratch += for_both(n.dh, n.dl, n.dhalo, n.du, n.dmix, *SPECTRA)
    return ins, outs, kept, scratch


def silu_slope(v):
    sig = sigmoid(v)
    return sig * (1.0 + v * (1.0 - sig))


class Reduce:
    def __init__(self, c, f):
        self.c, self.f = c, f
        self.own, self.sib, self.far, self.last = f.own1, f.sib1, f.far1, f.last1
        self.zin = f.zin1
        self.rows = self.own.shape[1]
        self.nc = c.A // 2
        self.chip, self.core = c.a // 2, c.a % 2
        self.Y, self.X = grid_of(self.nc)
        self.y, self.x = self.chip // self.X, lax.rem(self.chip, self.X)

    def to_sibling(self):
        f, c = self.f, self.c
        other = 1 - self.core
        moves = [
            (self.own.at[2 * cc + other], self.sib.at[cc], {n.ha: 2 * self.chip + other})
            for cc in range(self.nc)
        ]
        self.copies = [c.group(moves, f.rs1s.at[0], f.rs1r.at[0], self.sib.at[pl.ds(0, self.nc)])]

    def device(self, dy, dx):
        y, x = lax.rem(self.y + dy + self.Y, self.Y), lax.rem(self.x + dx + self.X, self.X)
        return 2 * (y * self.X + x) + self.core

    def lines(self, half, first):
        along_x = (half == 0) == first
        return [(0, d) for d in range(1, self.X)] if along_x else [(d, 0) for d in range(1, self.Y)]

    def part(self, half):
        h = self.rows // 2
        return pl.ds(half * h, h)

    def to_lines(self):
        f, c = self.f, self.c
        for copy in self.copies:
            copy.wait_recv()
        for dy in range(self.Y):
            for dx in range(self.X):
                t = self.device(dy, dx)
                self.own[t] = self.own[t] + self.sib[t // 2]
        self.copies = []
        for half in (0, 1):
            rest = [(0, 0)] + self.lines(half, False)
            moves = []
            for k, (dy, dx) in enumerate(self.lines(half, True)):
                for j, (ry, rx) in enumerate(rest):
                    t = self.device(dy + ry, dx + rx)
                    moves.append(
                        (
                            self.own.at[t, self.part(half)],
                            self.far.at[half, k * len(rest) + j],
                            {n.ha: self.device(dy, dx)},
                        )
                    )
            if moves:
                landed = self.far.at[half, pl.ds(0, len(moves))]
                self.copies.append(c.group(moves, f.rs2s.at[half], f.rs2r.at[half], landed))

    def to_owners(self):
        f, c = self.f, self.c
        for copy in self.copies:
            copy.wait_recv()
        self.copies = []
        for half in (1, 0):
            rows = self.part(half)
            rest = [(0, 0)] + self.lines(half, False)
            lines = self.lines(half, True)
            moves = []
            for j, (ry, rx) in enumerate(rest):
                t = self.device(ry, rx)
                total = self.own[t, rows, :]
                for k in range(len(lines)):
                    total = total + self.far[half, k * len(rest) + j]
                self.own[t, rows, :] = total
                if j:
                    moves.append((self.own.at[t, rows], self.last.at[half, j], {n.ha: t}))
            if moves:
                landed = self.last.at[half, pl.ds(1, len(moves))]
                self.copies.append(c.group(moves, f.rs5s.at[half], f.rs5r.at[half], landed))

    def collect(self):
        f, c = self.f, self.c
        for copy in self.copies:
            copy.wait_recv()
        for half in (0, 1):
            rows = self.part(half)
            total = self.own[c.a, rows, :]
            for j in range(1, 1 + len(self.lines(half, False))):
                total = total + self.last[half, j]
            self.own[c.a, rows, :] = total

    def to_images(self, k):
        f, c = self.f, self.c
        return to_images(
            c, self.own.at[c.a, self.part(k)], self.zin.at[k], f.rs3s.at[k], f.rs3r.at[k]
        )


def to_images(c, total, zin, ssem, rsem):
    part = total.shape[0] // c.B
    moves = []
    for d in range(1, c.B):
        zz = lax.rem(c.z + d, c.B)
        piece = total.at[pl.ds(pl.multiple_of(zz * part, 8), part)]
        moves.append((piece, zin.at[d], {n.img: zz}))
    return [c.group(moves, ssem, rsem, zin.at[pl.ds(1, c.B - 1)])] if moves else []


def from_images(c, copies, total, zin, out):
    for copy in copies:
        copy.wait_recv()
    part = total.shape[0] // c.B
    value = total[pl.ds(pl.multiple_of(c.z * part, 8), part), :]
    for d in range(1, c.B):
        value = value + zin[d]
    out[...] = value


class Direct:
    def __init__(self, c, f, own, far):
        self.c, self.f = c, f
        self.own, self.far = own, far

    def start(self):
        c, f = self.c, self.f
        moves = []
        for d in range(1, c.A):
            t = lax.rem(c.a + d, c.A)
            moves.append((self.own.at[t], self.far.at[d], {n.ha: t}))
        landed = self.far.at[pl.ds(1, c.A - 1)]
        self.copies = c.group(moves, f.das.at[0], f.dar.at[0], landed)

    def cross(self, zin):
        c, f = self.c, self.f
        self.copies.wait_recv()
        total = self.own[c.a]
        for d in range(1, c.A):
            total = total + self.far[d]
        zin[c.z] = total
        mine = zin.at[c.z]
        moves = [(mine, mine, {n.img: lax.rem(c.z + d, c.B)}) for d in range(1, c.B)]
        self.copies = []
        if moves:
            landed = zin.at[pl.ds(0, c.B - 1)]
            self.copies = [c.group(moves, f.dzs.at[0], f.dzr.at[0], landed)]

    def end(self, zin, out):
        for copy in self.copies:
            copy.wait_recv()
        total = zin[0]
        for d in range(1, self.c.B):
            total = total + zin[d]
        out[...] = total


class Chips:
    def __init__(self, c, f, own, sib, far):
        self.c, self.f = c, f
        self.own, self.sib, self.far = own, sib, far
        self.nc = c.A // 2
        self.chip, self.core = c.a // 2, c.a % 2

    def to_sibling(self):
        f, c = self.f, self.c
        other = 1 - self.core
        moves = [
            (self.own.at[2 * cc + other], self.sib.at[cc], {n.ha: 2 * self.chip + other})
            for cc in range(self.nc)
        ]
        self.copies = c.group(moves, f.cs.at[0], f.cr.at[0], self.sib.at[pl.ds(0, self.nc)])

    def start(self):
        f, c = self.f, self.c
        self.copies.wait_recv()
        moves = []
        for d in range(self.nc):
            cc = lax.rem(self.chip + d, self.nc)
            t = 2 * cc + self.core
            self.own[t] = self.own[t] + self.sib[cc]
            if d:
                moves.append((self.own.at[t], self.far.at[d], {n.ha: t}))
        self.copies = c.group(moves, f.cs.at[1], f.cr.at[1], self.far.at[pl.ds(1, self.nc - 1)])

    def owned(self):
        self.copies.wait_recv()
        total = self.own[self.c.a]
        for d in range(1, self.nc):
            total = total + self.far[d]
        return total


def backward_kernel(bks, A, B, sizes, *refs):
    ins, outs, kept, scratch = backward_names()
    near = ins + [far_of(name) for name in LATE] + [far_of(name) for name in kept]
    f = take(near + LATE + scratch, refs)
    CL, CG, CH, NPd = sizes
    CT = CL + CG
    c = Comm(A, B)
    c.enter()
    loader = Loader(f.ld)

    def load(names):
        for name in names:
            loader.start(name, getattr(f, far_of(name)), getattr(f, name))

    load(LATE[:4])
    other = jnp.minimum(c.a, 1)
    once = jnp.where(c.a == 0, 1.0, 2.0)
    cells = [B * bk.H * bk.W for bk in bks]
    freqs = [B * bk.H * (bk.W // 2 + 1) for bk in bks]
    views = [View(f, 0), View(f, 1)]
    both = (0, 1)
    sums = take(
        (n.sum_src, n.sum_a, n.sum_z, n.sum_as, n.sum_ar, n.sum_zs, n.sum_zr, n.sum_out),
        (f.sum_src, f.sum_a, f.sum_z, f.sum_as, f.sum_ar, f.sum_zs, f.sum_zr, f.bsum),
    )
    f.sum_src[...] = jnp.zeros_like(f.sum_src)
    adding, swaps = [None, None], [None, None]

    for q in both:
        bk, g = bks[q], views[q]
        center, inverse = norm_rows(f.sum_out, 2, q, CT, cells[q])
        loader.wait(n.joined + str(q), n.up + str(q))

        def body(r, carry, g=g, center=center, inverse=inverse):
            rows = pl.ds(r, 32)
            x = (g.joined[rows, :] - center) * inverse
            dy = g.up[rows, :] * silu_slope(x * f.norms[0, 0:1, :] + f.norms[0, 1:2, :])
            g.up[rows, :] = dy
            return carry[0] + column_sum(dy), carry[1] + column_sum(dy * x)

        total = chunks(bk.N, 32, body, no_sums(CT))
        if q == 0:
            load(LATE[4:])
            c.entered()
        adding[q] = c.sum_start(sums, 0, q, total)
    for q in both:
        adding[q] = c.sum_cross(sums, 0, q, adding[q])

    wex = split(f.g_ex[...].reshape(CG, CH))
    halos = []
    for q in both:
        bk, g = bks[q], views[q]
        c.sum_end(sums, 0, q, adding[q])
        center, inverse = norm_rows(f.sum_out, 2, q, CT, cells[q])
        gain = f.norms[0, 0:1, :] * inverse
        m1, m2 = (value * (1.0 / cells[q]) for value in totals(f.bsum, 0, q, CT))
        loader.wait(n.maps + str(q))

        def body(r, carry, bk=bk, g=g, center=center, inverse=inverse, gain=gain, m1=m1, m2=m2):
            rows = pl.ds(r, 32)
            x = (g.joined[rows, :] - center) * inverse
            dz = gain * (g.up[rows, :] - m1 - x * m2)
            g.up[rows, :] = dz
            high, low = split(dz)
            at = pl.ds(pl.multiple_of(r + bk.W, 32), 32)
            g.dh[at, :] = high
            g.dl[at, :] = low
            v = x * f.norms[0, 0:1, :] + f.norms[0, 1:2, :]
            g.joined[rows, :] = g.maps[rows, :] + v * sigmoid(v)
            return carry

        chunks(bk.N, 32, body, 0)
        name = n.block + str(q)
        loader.start(name, g.joined, getattr(f, far_of(name)))
        halos += c.halo_start(
            g.up.at[pl.ds(0, bk.W)],
            g.up.at[pl.ds(bk.N - bk.W, bk.W)],
            g.dhalo,
            f.hs.at[q],
            f.hr.at[q],
        )

        def body2(r, carry, bk=bk, g=g):
            at = pl.ds(pl.multiple_of(r + bk.W, 32), bk.MB)
            g.du[pl.ds(r, bk.MB), :] = dot3((g.dh[at, CL:], g.dl[at, CL:]), wex, NN)
            return carry

        chunks(bk.N, bk.MB, body2, 0)
        row_transform(bk, g.row, lambda h, g=g, bk=bk: g.du[h * bk.W : (h + 1) * bk.W, :], g.sendA)
        swaps[q] = c.swap_start(g.sendA, g.recvA, f.ws.at[0, q], f.wr.at[0, q], bk.Cp)

    first, end1, rows2, rows3 = flat_plan(A, sizes)
    units = (pad_to(CL // A, 8) * (CT // 128), pad_to(CG // A, 8))

    def pack(own, at, value, more):
        rows = value.shape[0] // A
        for t in range(A):
            for k in range(value.shape[1] // 128):
                piece = value[t * rows : (t + 1) * rows, 128 * k : 128 * (k + 1)]
                to = pl.ds(at + k * pad_to(rows, 8), rows)
                own[t, to, :] = own[t, to, :] + piece if more else piece

    def kernel_gradients(q):
        bk, g = bks[q], views[q]
        step = min(bk.N, 384)
        col = lax.broadcasted_iota(jnp.int32, (step, 1), 0) % bk.W
        for i in range(bk.N // step):
            for t in range(CT // 128):
                value = g.up[i * step : (i + 1) * step, 128 * t : 128 * (t + 1)]
                moved = (
                    jnp.where(col == bk.W - 1, 0.0, pltpu.roll(value, step - 1, 0)),
                    value,
                    jnp.where(col == 0, 0.0, pltpu.roll(value, 1, 0)),
                )
                for b in range(3):
                    high, low = split(jnp.transpose(moved[b]))
                    at = b * CL if t == 0 else 3 * CL + b * CG + 128 * (t - 1)
                    f.dth[at : at + 128, i * step : (i + 1) * step] = high
                    f.dtl[at : at + 128, i * step : (i + 1) * step] = low
        loader.wait(n.maps + str(q), n.halo + str(q), n.u + str(q))

        def body(r, carry):
            src = pl.multiple_of(r * bk.W, bk.W)
            high, low = split(g.maps[pl.ds(src, bk.W), :])
            f.zh[pl.ds(src + bk.W, bk.W), :] = high
            f.zl[pl.ds(src + bk.W, bk.W), :] = low
            return carry

        lax.fori_loop(0, bk.R, body, 0)
        for side, at in ((0, 0), (1, bk.N + bk.W)):
            high, low = split(g.halo[side])
            f.zh[pl.ds(at, bk.W), :] = high
            f.zl[pl.ds(at, bk.W), :] = low

        def taps(a, carry):
            rows = pl.ds(pl.multiple_of(a * bk.W, 32), bk.N)
            right = (f.zh[rows, :], f.zl[rows, :])
            out = dot3((f.dth[: 3 * CL, :], f.dtl[: 3 * CL, :]), right, NN)
            for b in range(3):
                at = pl.multiple_of(first[0] + (3 * a + b) * units[0], 8)
                pack(f.own1, at, out[b * CL : (b + 1) * CL], q)
            return carry

        lax.fori_loop(0, 3, taps, 0)
        right = tuple(
            jnp.concatenate([z[a * bk.W : a * bk.W + bk.N, :CL] for a in range(3)], 1)
            for z in (f.zh, f.zl)
        )
        for b in range(3):
            at = 3 * CL + b * CG
            value = dot3((f.dth[at : at + CG, :], f.dtl[at : at + CG, :]), right, NN)
            for a in range(3):
                piece = value[:, a * CL : (a + 1) * CL]
                pack(f.own1, first[1] + (3 * a + b) * units[1], piece, q)
        at = 3 * CL + CG
        value = dot3((f.dth[at : at + CG, :], f.dtl[at : at + CG, :]), split(g.u[...]), NN)
        value = jnp.concatenate([value, jnp.zeros((CG, pad_to(CH, 128) - CH), f32)], 1)
        pack(f.own1, first[2], value, q)

    def spectra_slopes(q):
        bk, g = bks[q], views[q]
        loader.wait(n.mixed + str(q))
        c.swap_end(swaps[q])
        center, inverse = norm_rows(f.sum_out, 1, q, 2 * CH, freqs[q])
        carry = [no_sums(2 * CH)]

        def put(slot, value):
            rows = slice(slot * bk.H, (slot + 1) * bk.H)
            x = (g.mixed[rows, :] - center) * inverse
            value = value * (once if slot in (0, bk.nb) else 2.0)
            dy = value * silu_slope(x * f.norms[2, 0:1, : 2 * CH] + f.norms[2, 1:2, : 2 * CH])
            g.dmix[rows, :] = dy
            carry[0] = (carry[0][0] + column_sum(dy), carry[0][1] + column_sum(dy * x))

        col_transform(bk, g.col, g.col0, other, g.recvA, put)
        adding[q] = c.sum_start(sums, 1, q, carry[0])

    def spectra_back(q, wfo):
        bk, g = bks[q], views[q]
        c.sum_end(sums, 1, q, adding[q])
        center, inverse = norm_rows(f.sum_out, 1, q, 2 * CH, freqs[q])
        gain = f.norms[2, 0:1, : 2 * CH] * inverse
        m1, m2 = (value * (1.0 / freqs[q]) for value in totals(f.bsum, 1, q, 2 * CH))

        def get(slot):
            rows = slice(slot * bk.H, (slot + 1) * bk.H)
            x = (g.mixed[rows, :] - center) * inverse
            dz = gain * (g.dmix[rows, :] - m1 - x * m2)
            g.dmix[rows, :] = dz
            return dot3(split(dz), wfo, NN)

        col_back(bk, g.colT, g.col0T, other, get, lambda b, v: v, g.sendB)
        swaps[q] = c.swap_start(g.sendB, g.recvB, f.ws.at[1, q], f.wr.at[1, q], bk.Cp)

    kernel_gradients(0)
    spectra_slopes(0)
    kernel_gradients(1)
    adding[0] = c.sum_cross(sums, 1, 0, adding[0])
    if f.own1.shape[1] > end1:
        f.own1[:, end1:, :] = jnp.zeros((A, f.own1.shape[1] - end1, 128), f32)
    red1 = Reduce(c, f)
    red1.to_sibling()
    spectra_slopes(1)
    loader.wait(n.g_fo)
    wfo = split(f.g_fo[...].reshape(2 * CH, 2 * CH))
    adding[1] = c.sum_cross(sums, 1, 1, adding[1])
    red1.to_lines()
    spectra_back(0, wfo)
    spectra_back(1, wfo)
    for q in both:
        bk, g = bks[q], views[q]
        loader.wait(n.spec + str(q))
        value = dot3(split(jnp.transpose(g.dmix[...])), split(g.spec[...]), NN)
        f.gfo[...] = value if q == 0 else f.gfo[...] + value
    pack(f.own2, 0, f.gfo, 0)
    red2 = Chips(c, f, f.own2, f.sib2, f.far2)
    red2.to_sibling()

    c.halo_end(halos)
    c.halo_sent()
    loader.wait(n.knh, n.knl, n.koh, n.kol)

    def input_gradients(q):
        bk, g = bks[q], views[q]
        for side, at, edge in ((0, 0, 0), (1, bk.N + bk.W, A - 1)):
            high, low = split(jnp.where(c.a == edge, 0.0, g.dhalo[side]))
            g.dh[pl.ds(at, bk.W), :] = high
            g.dl[pl.ds(at, bk.W), :] = low
        conv_backward(bk, g.dh, g.dl, f.knh, f.knl, f.koh, f.kol, g.up)

    def active_slopes(q):
        bk, g = bks[q], views[q]
        loader.wait(n.s + str(q))
        c.swap_end(swaps[q])
        center, inverse = norm_rows(f.sum_out, 0, q, CH, cells[q])
        total = no_sums(CH)
        for h in range(bk.R):
            rows = slice(h * bk.W, (h + 1) * bk.W)
            x = (g.s[rows, :] - center) * inverse
            value = g.du[rows, :] + row_back(bk, g.rowT, g.recvB, h)
            dy = value * silu_slope(x * f.norms[1, 0:1, :CH] + f.norms[1, 1:2, :CH])
            g.du[rows, :] = dy
            total = (total[0] + column_sum(dy), total[1] + column_sum(dy * x))
        adding[q] = c.sum_start(sums, 2, q, total, False)

    def squeeze_back(q, wsq):
        bk, g = bks[q], views[q]
        c.sum_end(sums, 2, q, adding[q])
        center, inverse = norm_rows(f.sum_out, 0, q, CH, cells[q])
        gain = f.norms[1, 0:1, :CH] * inverse
        m1, m2 = (value * (1.0 / cells[q]) for value in totals(f.bsum, 2, q, CH))

        def body(r, carry):
            rows = pl.ds(r, bk.MB)
            x = (g.s[rows, :] - center) * inverse
            dz = gain * (g.du[rows, :] - m1 - x * m2)
            g.du[rows, :] = dz
            g.up[rows, CL:] += dot3(split(dz), wsq, NN)
            return carry

        chunks(bk.N, bk.MB, body, 0)
        value = dot3(split(jnp.transpose(g.du[...])), split(g.maps[:, CL:]), NN)
        f.gsq[...] = value if q == 0 else f.gsq[...] + value

    input_gradients(0)
    red1.to_owners()
    input_gradients(1)
    active_slopes(0)
    active_slopes(1)
    red1.collect()
    images = [red1.to_images(0), red1.to_images(1)]
    loader.wait(n.g_sq)
    wsq = split(f.g_sq[...].reshape(CH, CG))
    for q in both:
        adding[q] = c.sum_cross(sums, 2, q, adding[q])
    red2.start()
    squeeze_back(0, wsq)
    squeeze_back(1, wsq)
    for q in both:
        name = n.back + str(q)
        loader.start(name, views[q].up, getattr(f, far_of(name)))
    pack(f.own3, 0, f.gsq, 0)
    red3 = Direct(c, f, f.own3, f.far3)
    red3.start()
    f.tot2[: f.own2.shape[1], :] = red2.owned()
    if f.tot2.shape[0] > f.own2.shape[1]:
        f.tot2[f.own2.shape[1] :, :] = jnp.zeros((f.tot2.shape[0] - f.own2.shape[1], 128), f32)
    images.append(to_images(c, f.tot2, f.zin2, f.rs3s.at[2], f.rs3r.at[2]))

    span = pad_to(NPd * A, 128) + 128
    lane = lax.broadcasted_iota(jnp.int32, (8, span), 1)
    out = []
    for i in (1, 0):
        rows = []
        for k, width in ((0, CT), (1, 2 * CH), (2, CH)):
            pair = [totals(f.bsum, k, q, CT)[i] for q in both]
            row = jnp.concatenate([pair[0] + pair[1], jnp.zeros((1, span - CT), f32)], 1)
            rows.append(jnp.where(lane < width, jnp.broadcast_to(row, (8, span)), 0.0))
        out.append(rows[0] + pltpu.roll(rows[2], CT, 1) + pltpu.roll(rows[1], CT + CH, 1))
    sub = lax.broadcasted_iota(jnp.int32, (8, span), 0)
    value = pltpu.roll(jnp.where(sub == 0, out[0], out[1]), lax.rem(span - NPd * c.a, span), 1)
    f.gnorm[...] = value[:, : f.gnorm.shape[1]]

    def keep(name):
        loader.start(name, getattr(f, name), getattr(f, far_of(name)))

    keep(n.gnorm)
    red3.cross(f.zin3)
    at = 0
    for k, (total, zin) in enumerate(
        (
            (f.own1.at[c.a, red1.part(0)], f.zin1.at[0]),
            (f.own1.at[c.a, red1.part(1)], f.zin1.at[1]),
            (f.tot2, f.zin2),
        )
    ):
        from_images(c, images[k], total, zin, f.seg1.at[pl.ds(at, zin.shape[1])])
        at += zin.shape[1]
    keep(n.seg1)
    red3.end(f.zin3, f.flat3)
    keep(n.flat3)
    loader.wait(*kept)
    c.finish()


def conv_backward(bk, dh, dl, knh, knl, koh, kol, out):
    MB, W = bk.MB, bk.W
    CL = knh.shape[2]
    CG = koh.shape[0] // 3
    CT = knh.shape[3]
    col = lax.broadcasted_iota(jnp.int32, (MB, 1), 0) % W

    def moved(value, b):
        if b == 0:
            return jnp.where(col == W - 1, 0.0, pltpu.roll(value, MB - 1, 0))
        if b == 2:
            return jnp.where(col == 0, 0.0, pltpu.roll(value, 1, 0))
        return value

    def body(i, carry):
        r = pl.multiple_of(i * MB, 32)
        rows = [pl.ds(pl.multiple_of(r + (2 - a) * W, 32), MB) for a in range(3)]
        left = tuple(jnp.concatenate([d[rows[a], :CL] for a in range(3)], 1) for d in (dh, dl))
        total = None
        for b in (1, 0, 2):
            right = (knh[b].reshape(3 * CL, CT), knl[b].reshape(3 * CL, CT))
            value = moved(dot3(left, right, NN), b)
            total = value if total is None else total + value
        out[pl.ds(r, MB), :] = total
        cross = None
        for a in range(3):
            left2 = (dh[rows[a], CL:], dl[rows[a], CL:])
            right = tuple(
                jnp.concatenate(
                    [k[b * CG : (b + 1) * CG, a * CL : (a + 1) * CL] for b in range(3)], 1
                )
                for k in (koh, kol)
            )
            value = dot3(left2, right, NN)
            cross = value if cross is None else cross + value
        total = None
        for b in range(3):
            value = moved(cross[:, b * CL : (b + 1) * CL], b)
            total = value if total is None else total + value
        out[pl.ds(r, MB), :CL] += total
        return carry

    lax.fori_loop(0, bk.N // MB, body, 0)


def backward_call(bks, A, B, sizes, cid, args):
    CL, CG, CH, NPd = sizes
    CT = CL + CG
    nc = A // 2
    first, end1, rows2, rows3 = flat_plan(A, sizes)
    half1, _, padded2 = flat_rows_of(A, B, sizes)
    rows1 = 2 * half1
    N = max(bk.N for bk in bks)
    big = max((bk.R + 2) * bk.W for bk in bks)
    sd = forward_shapes(bks, A, B, sizes)
    sd[n.bsum] = sd[n.sum_src]
    sd[n.gnorm] = (8, pad_to(NPd, 128))
    sd[n.dth] = sd[n.dtl] = (3 * CT, N)
    sd[n.zh] = sd[n.zl] = (big, CT)
    sd[n.gsq], sd[n.gfo] = (CH, CG), (2 * CH, 2 * CH)
    sd[n.own1], sd[n.zin1] = (A, rows1, 128), (2, B, half1 // B, 128)
    sd[n.sib1] = (nc, rows1, 128)
    sd[n.far1] = (2, nc, rows1 // 2, 128)
    sd[n.last1] = (2, max(grid_of(nc)), rows1 // 2, 128)
    sd[n.tot2], sd[n.zin2] = (padded2, 128), (B, padded2 // B, 128)
    sd[n.own2] = (A, rows2, 128)
    sd[n.sib2] = sd[n.far2] = (nc, rows2, 128)
    sd[n.flat3], sd[n.zin3] = (rows3, 128), (B, rows3, 128)
    sd[n.own3] = sd[n.far3] = (A, rows3, 128)
    for q, bk in enumerate(bks):
        here = {
            n.back: (bk.N, CT),
            n.block: (bk.N, CT),
            n.dh: ((bk.R + 2) * bk.W, CT),
            n.dl: ((bk.R + 2) * bk.W, CT),
            n.dhalo: (2, bk.W, CT),
            n.du: (bk.N, CH),
            n.dmix: (bk.Q, 2 * CH),
        }
        for name, shape in here.items():
            sd[name + str(q)] = shape
    ins, outs, kept, scratch = backward_names()
    results = outs + kept
    sems = sum_sems(A, B)
    sems[n.ld] = (len(LATE) + len(kept),)
    for name in (n.rs1s, n.rs1r, n.das, n.dar, n.dzs, n.dzr):
        sems[name] = (1,)
    sems[n.rs3s] = sems[n.rs3r] = (3,)
    for name in (n.rs2s, n.rs2r, n.rs5s, n.rs5r, n.cs, n.cr):
        sems[name] = (2,)
    macs = sum(bk.N for bk in bks) * 2800000
    res = pl.pallas_call(
        functools.partial(backward_kernel, bks, A, B, sizes),
        out_shape=[result(name, sd) for name in results],
        in_specs=[VM] * len(ins) + [FAR] * len(LATE),
        out_specs=[VM] * len(outs) + [FAR] * len(kept),
        scratch_shapes=[memory(name, sd, sems) for name in LATE + scratch],
        compiler_params=pltpu.CompilerParams(
            collective_id=cid, has_side_effects=True, vmem_limit_bytes=VMEM_LIMIT
        ),
        cost_estimate=pl.CostEstimate(flops=6 * macs, bytes_accessed=40_000_000, transcendentals=0),
        name=n.backward,
    )(*[args[name] for name in ins + LATE])
    return dict(zip(results, res))


def update(A, B, sizes, *refs):
    CL, CG, CH, NPd = sizes
    flat1, flat3, gnorm = refs[:3]
    weights, moments, averages = refs[3:10], refs[10:17], refs[17:24]
    updated, velocity, smoothed, half = refs[24:31], refs[31:38], refs[38:45], refs[45:52]
    decay = min(0.5, (1.0 + STEP) / (10.0 + STEP))

    def step(i, at, grad):
        new = renewed(weights[i][at], moments[i][at], grad)
        velocity[i][at] = momentum * moments[i][at] + grad
        updated[i][at] = new
        smoothed[i][at] = decay * averages[i][at] + (1.0 - decay) * new
        half[i][at] = new.astype(bf16)

    for k in range(9):
        both, out = unpack_tap(flat1, A, B, sizes, k)
        step(0, k, both[:, :CL])
        step(1, k, both[:, CL:])
        step(2, k, out)
    every = slice(None)
    for i, grad in zip((3, 4, 5), unpack_matrices(flat1, flat3, A, B, sizes)):
        step(i, every, grad)
    step(6, every, gnorm[0:2, :NPd])


def as_rows(weight):
    return jnp.transpose(weight[0], (0, 1, 3, 2)).reshape(9, weight.shape[4], weight.shape[3])


def from_rows(value):
    return jnp.transpose(value.reshape(1, 3, 3, value.shape[1], value.shape[2]), (0, 1, 2, 4, 3))


def flat_rows(weight):
    return jnp.transpose(weight[0])


def from_flat(value):
    return jnp.transpose(value)[None]


def per_device(*arrays):
    A, B = lax.axis_size("ha"), lax.axis_size("img")
    maps, ups = arrays[0:2], arrays[2:4]
    groups = [arrays[4 + i :: 3] for i in range(3)]
    to_local = (as_rows,) * 3 + (flat_rows,) * 3 + (lambda w: w[0],)
    weights, moments, averages = (
        [change(w) for change, w in zip(to_local, group)] for group in groups
    )
    bks = [Bucket(m.shape[1], m.shape[2], A) for m in maps]
    CL, CG, CH, NPd = weights[0].shape[2], weights[1].shape[2], weights[5].shape[1], weights[6].shape[1]
    sizes = (CL, CG, CH, NPd)
    CT = CL + CG
    args = {}
    for q in (0, 1):
        args[n.maps + str(q)] = maps[q].reshape(-1, CT)
        args[n.up + str(q)] = ups[q].reshape(-1, CT)
        for name, table in zip(TABLES, tables_of(bks[q])):
            args[name + str(q)] = jnp.asarray(table)
    flat_maps = [args[n.maps0], args[n.maps1]]
    args.update(zip(KINDS, weights))
    args[old_of(n.nm)] = weights[6]
    fwd = forward_call(bks, A, B, sizes, True, 1, args)
    bwd = backward_call(bks, A, B, sizes, 2, {**args, **fwd})
    block = [bwd[n.block0], bwd[n.block1]]
    back = [args[n.up + str(q)] + bwd[n.back + str(q)] for q in (0, 1)]
    again = {**args, **bwd, n.halo0: fwd[n.halo0], n.halo1: fwd[n.halo1]}
    for name, weight, moment in zip(KINDS, weights, moments):
        again[old_of(name)] = weight
        again[moment_of(name)] = moment
    fresh = forward_call(bks, A, B, sizes, False, 3, again)
    grads = (fresh[n.flat1], bwd[n.flat3], bwd[n.gnorm])
    rerun, groups = finish_call(
        bks, A, B, sizes, flat_maps, fresh, grads, weights, moments, averages
    )
    out = []
    for pair in (block, back, rerun):
        out += [value.reshape(m.shape) for value, m in zip(pair, maps)]
    to_outer = (from_rows,) * 3 + (from_flat,) * 3 + (lambda w: w[None],)
    for i in range(7):
        out += [to_outer[i](group[i]) for group in groups]
    return tuple(out)


def solution(mesh):
    cells = P("img", "ha", None, None)
    kernel = P(None, None, None, None, "ha")
    matrix = P(None, None, "ha")
    return jax.shard_map(
        per_device,
        mesh=mesh,
        in_specs=(cells,) * 4 + (kernel,) * 9 + (matrix,) * 12,
        out_specs=(cells,) * 6 + (kernel,) * 12 + (matrix,) * 16,
        check_vma=False,
    )
```

```python
import functools
import math

import jax
import jax.numpy as jnp
import numpy as np
from jax import lax
from jax.experimental import pallas as pl
from jax.experimental.pallas import tpu as pltpu
from jax.sharding import PartitionSpec as P

STEP = 6

epsilon = 1e-05
learn_rate = 3e-05
momentum = 0.5

f32 = jnp.float32
bf16 = jnp.bfloat16
MESH = pl.DeviceIdType.MESH
VMEM_LIMIT = 60 * 1024 * 1024

NN = (((1,), (0,)), ((), ()))
NT = (((1,), (1,)), ((), ()))
TN = (((0,), (0,)), ((), ()))


def dg(left, right, dims):
    return lax.dot_general(left, right, dims, preferred_element_type=f32)


def split(value):
    high = value.astype(bf16)
    return high, (value - high.astype(f32)).astype(bf16)


def dot3(left, right, dims):
    lh, ll = left
    rh, rl = right
    return dg(lh, rh, dims) + dg(ll, rh, dims) + dg(lh, rl, dims)


def sigmoid(v):
    return 1.0 / (1.0 + jnp.exp(-v))


def pad_to(n, m):
    return -(-n // m) * m


def chunks(count, step, body, carry):
    def run(i, carry):
        return body(pl.multiple_of(i * step, 8), carry)

    return lax.fori_loop(0, count // step, run, carry)


class Bucket:
    def __init__(self, rows, width, group):
        self.R, self.W, self.A = rows, width, group
        self.H = rows * group
        self.N = rows * width
        self.nb = -(-(width // 2) // group)
        self.Cp = pad_to(self.nb * rows, 8)
        self.Q = (self.nb + 1) * self.H
        self.MB = max(r * width for r in range(1, rows + 1) if rows % r == 0 and r * width <= 384)


def hi_lo(table):
    table = np.asarray(table, np.float64)
    high = table.astype(np.float32).astype(jnp.bfloat16)
    low = (table - high.astype(np.float64)).astype(np.float32).astype(jnp.bfloat16)
    return np.stack([high, low])


def tables_of(bk):
    A, nb, W, H, R = bk.A, bk.nb, bk.W, bk.H, bk.R
    row = np.zeros((2, nb, A, W))
    w = np.arange(W)
    for b in range(nb):
        for d in range(A):
            j = d * nb + b
            if j == 0:
                row[0, b, d] = 1.0
                row[1, b, d] = np.cos(math.pi * w)
            elif 2 * j < W:
                row[0, b, d] = np.cos(2 * math.pi * (j * w % W) / W)
                row[1, b, d] = -np.sin(2 * math.pi * (j * w % W) / W)
    row = row.reshape(2 * nb * A, W) / math.sqrt(W)
    k = np.arange(H)[:, None]
    h = np.array([s * R + r for r in range(R) for s in range(A)])[None, :]
    phase = 2 * math.pi * (k * h % H) / H
    cos, sin = np.cos(phase) / math.sqrt(H), np.sin(phase) / math.sqrt(H)
    none = np.zeros_like(cos)
    plain = np.block([[cos, sin], [-sin, cos]])
    packed = np.block([[cos, none], [-sin, none], [none, cos], [none, -sin]])
    other = np.concatenate([plain, np.zeros_like(plain)], 0)
    first = np.stack([hi_lo(packed), hi_lo(other)])
    return (
        hi_lo(row),
        hi_lo(row.T),
        hi_lo(plain),
        hi_lo(plain.T),
        first,
        np.swapaxes(first, 2, 3),
    )


class Names:
    def __getattr__(self, name):
        return name


n = Names()
TABLES = (n.row, n.rowT, n.col, n.colT, n.col0, n.col0T)
SPECTRA = (n.sendA, n.recvA, n.sendB, n.recvB)


def for_both(*names):
    return [name + str(q) for q in (0, 1) for name in names]


class View:
    def __init__(self, refs, q):
        self.refs, self.q = refs, q

    def __getattr__(self, name):
        return getattr(self.refs, name + str(self.q))


class Fields:
    pass


def take(names, refs):
    out = Fields()
    for name, ref in zip(names, refs):
        setattr(out, name, ref)
    return out


class Group:
    def __init__(self, ssem, rsem, landed):
        self.ssem, self.rsem, self.landed = ssem, rsem, landed

    def wait_recv(self):
        pltpu.make_async_copy(self.landed, self.landed, self.rsem).wait()

    def wait_send(self):
        pltpu.make_async_copy(self.landed, self.landed, self.ssem).wait()


class Comm:
    def __init__(self, A, B):
        self.A, self.B = A, B
        self.a = lax.axis_index("ha")
        self.z = lax.axis_index("img")
        self.pending, self.halos = [], []

    def enter(self):
        bar = pltpu.get_barrier_semaphore()
        for d in range(1, self.A):
            pl.semaphore_signal(
                bar, inc=1, device_id=(self.z, lax.rem(self.a + d, self.A)), device_id_type=MESH
            )
        for d in range(1, self.B):
            pl.semaphore_signal(
                bar, inc=1, device_id=(lax.rem(self.z + d, self.B), self.a), device_id_type=MESH
            )

    def entered(self):
        pl.semaphore_wait(pltpu.get_barrier_semaphore(), self.A + self.B - 2)

    def make(self, src, dst, ssem, rsem, ha=None, img=None):
        return pltpu.make_async_remote_copy(
            src,
            dst,
            ssem,
            rsem,
            device_id=(self.z if img is None else img, self.a if ha is None else ha),
            device_id_type=MESH,
        )

    def send(self, *args, **kwargs):
        copy = self.make(*args, **kwargs)
        copy.start()
        self.pending.append(copy)
        return copy

    def group(self, moves, ssem, rsem, landed):
        for src, dst, where in moves:
            self.make(src, dst, ssem, rsem, **where).start()
        group = Group(ssem, rsem, landed)
        self.pending.append(group)
        return group

    def finish(self):
        self.halo_sent()
        for copy in self.pending:
            copy.wait_send()

    def sum_start(self, f, k, q, sums, first=True):
        i = 2 * k + q
        for part in (0, 1):
            value = jnp.sum(sums[part], 0, keepdims=True)
            for t in range(-(-value.shape[1] // 128)):
                piece = value[:, 128 * t : 128 * (t + 1)]
                f.sum_src[i, 4 * part + t : 4 * part + t + 1, : piece.shape[1]] = piece
        return self.sum_stage(f, i, first, f.sum_src[i])

    def sum_stage(self, f, i, rows, value):
        count, me = (self.A, self.a) if rows else (self.B, self.z)
        buf, ssem, rsem = (f.sum_a, f.sum_as, f.sum_ar) if rows else (f.sum_z, f.sum_zs, f.sum_zr)
        buf[i, me] = value
        mine = buf.at[i, me]
        name = n.ha if rows else n.img
        moves = [(mine, mine, {name: lax.rem(me + d, count)}) for d in range(1, count)]
        group = None
        if moves:
            group = self.group(moves, ssem.at[i], rsem.at[i], buf.at[i, pl.ds(0, count - 1)])
        return rows, buf, count, group

    def sum_total(self, i, stage):
        rows, buf, count, group = stage
        if group is not None:
            group.wait_recv()
        total = buf[i, 0]
        for d in range(1, count):
            total = total + buf[i, d]
        return total

    def sum_cross(self, f, k, q, stage):
        i = 2 * k + q
        return self.sum_stage(f, i, not stage[0], self.sum_total(i, stage))

    def sum_end(self, f, k, q, stage):
        i = 2 * k + q
        f.sum_out[i] = self.sum_total(i, stage)

    def swap_start(self, src, dst, ssem, rsem, rows):
        def block(ref, t):
            return ref.at[:, pl.ds(pl.multiple_of(t * rows, 8), rows)]

        moves = []
        for d in range(1, self.A):
            t = lax.rem(self.a + d, self.A)
            moves.append((block(src, t), block(dst, self.a), {n.ha: t}))
        group = self.group(moves, ssem, rsem, dst.at[:, pl.ds(0, (self.A - 1) * rows)])
        mine = pl.ds(pl.multiple_of(self.a * rows, 8), rows)
        dst[:, mine, :] = src[:, mine, :]
        return group

    def swap_end(self, group):
        group.wait_recv()

    def halo_start(self, low_row, high_row, dst, ssem, rsem):
        up = jnp.maximum(self.a - 1, 0)
        down = jnp.minimum(self.a + 1, self.A - 1)
        low = self.make(low_row, dst.at[1], ssem.at[0], rsem.at[0], ha=up)
        high = self.make(high_row, dst.at[0], ssem.at[1], rsem.at[1], ha=down)

        @pl.when(self.a > 0)
        def _():
            low.start()

        @pl.when(self.a < self.A - 1)
        def _():
            high.start()

        self.halos.append((low, high))
        return [(low, high)]

    def halo_end(self, pairs):
        for low, high in pairs:

            @pl.when(self.a < self.A - 1)
            def _():
                low.wait_recv()

            @pl.when(self.a > 0)
            def _():
                high.wait_recv()

    def halo_sent(self):
        for low, high in self.halos:

            @pl.when(self.a > 0)
            def _():
                low.wait_send()

            @pl.when(self.a < self.A - 1)
            def _():
                high.wait_send()

        self.halos = []


def column_sum(value):
    rows, width = value.shape
    return jnp.sum(value.reshape(rows // 8, 8, width), 0)


def no_sums(width):
    return jnp.zeros((8, width), f32), jnp.zeros((8, width), f32)


def totals(ref, k, q, width):
    i = 2 * k + q
    return [
        jnp.concatenate([ref[i, t : t + 1, :] for t in range(first, first + 4)], 1)[:, :width]
        for first in (0, 4)
    ]


def norm_rows(ref, k, q, width, count):
    total, square = totals(ref, k, q, width)
    center = total * (1.0 / count)
    variance = square * (1.0 / count) - center * center
    return center, lax.rsqrt(variance + epsilon)


def row_transform(bk, table, source, send):
    nbA = bk.nb * bk.A
    tab = (table[0], table[1])
    for h in range(bk.R):
        out = dot3(tab, split(source(h)), NN)
        out = jnp.concatenate([out[:nbA], out[nbA:]], 1)
        for b in range(bk.nb):
            put_strided(send, b * bk.R + h, bk.A, bk.Cp, out[b * bk.A : (b + 1) * bk.A])


def row_back(bk, table, recv, h):
    parts = [get_strided(recv, b * bk.R + h, bk.A, bk.Cp) for b in range(bk.nb)]
    block = jnp.concatenate(parts, 0) if len(parts) > 1 else parts[0]
    half = block.shape[1] // 2
    block = jnp.concatenate([block[:, :half], block[:, half:]], 0)
    return dot3((table[0], table[1]), split(block), NN)


def put_strided(ref, start, count, stride, value):
    for t in range(ref.shape[0]):
        ref[t, pl.ds(start, count, stride=stride), :] = value[:, 128 * t : 128 * (t + 1)]


def get_strided(ref, start, count, stride):
    return jnp.concatenate(
        [ref[t, pl.ds(start, count, stride=stride), :] for t in range(ref.shape[0])], 1
    )


def first_table(ref, other):
    return ref[other, 0], ref[other, 1]


def col_transform(bk, f_col, f_col0, other, recv, put):
    H = bk.H
    for b in range(bk.nb):
        block = jnp.concatenate(
            [get_strided(recv, b * bk.R + h, bk.A, bk.Cp) for h in range(bk.R)], 0
        )
        half = block.shape[1] // 2
        block = split(jnp.concatenate([block[:, :half], block[:, half:]], 0))
        if b == 0:
            out = dot3(first_table(f_col0, other), block, NN)
            put(bk.nb, jnp.concatenate([out[2 * H : 3 * H], out[3 * H :]], 1))
        else:
            out = dot3((f_col[0], f_col[1]), block, NN)
        put(b, jnp.concatenate([out[:H], out[H : 2 * H]], 1))


def col_back(bk, f_colT, f_col0T, other, get, scale, send):
    H = bk.H

    def halves(value):
        half = value.shape[1] // 2
        return [value[:, :half], value[:, half:]]

    for b in range(bk.nb):
        if b == 0:
            block = jnp.concatenate(halves(get(0)) + halves(get(bk.nb)), 0)
            out = dot3(first_table(f_col0T, other), split(block), NN)
        else:
            out = dot3((f_colT[0], f_colT[1]), split(jnp.concatenate(halves(get(b)), 0)), NN)
        out = jnp.concatenate([out[:H], out[H:]], 1)
        out = scale(b, out)
        for h in range(bk.R):
            put_strided(send, b * bk.R + h, bk.A, bk.Cp, out[h * bk.A : (h + 1) * bk.A])


def conv_forward(bk, zh, zl, knh, knl, koh, kol, out):
    MB, W = bk.MB, bk.W
    col = lax.broadcasted_iota(jnp.int32, (MB, 1), 0) % W

    def combine(value, n):
        low = jnp.where(col == 0, 0.0, pltpu.roll(value[:, :n], 1, 0))
        high = jnp.where(col == W - 1, 0.0, pltpu.roll(value[:, 2 * n :], MB - 1, 0))
        return low + value[:, n : 2 * n] + high

    def body(i, carry):
        r = pl.multiple_of(i * MB, 32)
        total = None
        for a in range(3):
            left = (zh[pl.ds(r + a * W, MB), :], zl[pl.ds(r + a * W, MB), :])
            n = knh.shape[2]
            right = (knh[:, a].reshape(3 * n, -1), knl[:, a].reshape(3 * n, -1))
            part = dot3(left, right, NT)
            total = part if total is None else total + part
        CL = knh.shape[2]
        out[pl.ds(r, MB), :CL] = combine(total, CL)
        left = tuple(
            jnp.concatenate([z[pl.ds(r + a * W, MB), :CL] for a in range(3)], 1) for z in (zh, zl)
        )
        cross = dot3(left, (koh[...], kol[...]), NT)
        out[pl.ds(r, MB), CL:] = combine(cross, koh.shape[0] // 3)
        return carry

    lax.fori_loop(0, bk.N // MB, body, 0)


GATHERED = (n.sq, n.nm, n.fo)


class Loader:
    def __init__(self, sems):
        self.sems, self.copies, self.done = sems, {}, set()

    def start(self, name, src, dst):
        copy = pltpu.make_async_copy(src, dst, self.sems.at[len(self.copies)])
        copy.start()
        self.copies[name] = copy

    def wait(self, *names):
        for name in names:
            if name not in self.done:
                self.copies[name].wait()
                self.done.add(name)


KINDS = (n.near, n.inw, n.outw, n.sq, n.fo, n.ex, n.nm)


def old_of(name):
    return name + n._old


def moment_of(name):
    return name + n._moment


def whole_of(name):
    return n.g_ + name


def gather_direct(c, f, name, i):
    shard, whole = getattr(f, name), getattr(f, whole_of(name))
    whole[c.a] = shard[...]
    moves = [(shard, whole.at[c.a], {n.ha: lax.rem(c.a + d, c.A)}) for d in range(1, c.A)]
    return c.group(moves, f.g1s.at[i], f.g1r.at[i], whole.at[pl.ds(0, c.A - 1)])


class Pair:
    def __init__(self, c, f, name, i):
        self.c, self.f, self.i = c, f, i
        self.nc = c.A // 2
        self.chip, self.core = c.a // 2, c.a % 2
        self.sibling = 2 * self.chip + 1 - self.core
        self.whole = getattr(f, whole_of(name))
        shard, mine = getattr(f, name), self.whole.at[c.a]
        self.whole[c.a] = shard[...]
        moves = []
        for d in range(1, self.nc):
            moves.append((shard, mine, {n.ha: 2 * lax.rem(self.chip + d, self.nc) + self.core}))
        self.far = self.group(moves, 0)
        self.near = self.group([(shard, mine, {n.ha: self.sibling})], 1)

    def group(self, moves, k):
        f, i = self.f, self.i
        landed = self.whole.at[pl.ds(0, len(moves))]
        return self.c.group(moves, f.p1s.at[i, k], f.p1r.at[i, k], landed)

    def second(self):
        self.far.wait_recv()
        moves = []
        for d in range(1, self.nc):
            piece = self.whole.at[2 * lax.rem(self.chip + d, self.nc) + self.core]
            moves.append((piece, piece, {n.ha: self.sibling}))
        self.passed = self.group(moves, 2)

    def end(self):
        self.near.wait_recv()
        self.passed.wait_recv()


def grid_of(chips):
    across = max(x for x in range(1, chips + 1) if chips % x == 0 and x * x <= chips)
    return chips // across, across


class Spread:
    def __init__(self, c, f, names):
        self.c, self.f, self.names = c, f, names
        self.Y, self.X = grid_of(c.A // 2)
        self.chip, self.core = c.a // 2, c.a % 2
        self.y, self.x = self.chip // self.X, lax.rem(self.chip, self.X)

    def device(self, dy, dx, core=None):
        y, x = lax.rem(self.y + dy + self.Y, self.Y), lax.rem(self.x + dx + self.X, self.X)
        return 2 * (y * self.X + x) + (self.core if core is None else core)

    def part(self, ref, half, slot):
        if len(ref.shape) == 3:
            return ref.at[slot]
        cut = ref.shape[1] // 2
        return ref.at[slot, pl.ds(0, cut) if half == 0 else pl.ds(cut, ref.shape[1] - cut)]

    def lines(self, half, first):
        along_x = (half == 0) == first
        return [(0, d) for d in range(1, self.X)] if along_x else [(d, 0) for d in range(1, self.Y)]

    def members(self, half):
        for i, name in enumerate(self.names):
            if half == 0 or len(getattr(self.f, name).shape) == 3:
                yield i, name

    def pass_on(self, half, slots, lines, ssem, rsem):
        groups = []
        for i, name in self.members(half):
            ref = getattr(self.f, whole_of(name))
            moves = []
            for dy, dx in lines:
                for slot in slots:
                    piece = self.part(ref, half, slot)
                    moves.append((piece, piece, {n.ha: self.device(dy, dx)}))
            if moves:
                landed = self.part(ref, half, pl.ds(0, len(moves)))
                groups.append(self.c.group(moves, ssem.at[i, half], rsem.at[i, half], landed))
        return groups

    def start(self):
        f = self.f
        for name in self.names:
            getattr(f, whole_of(name))[self.c.a] = getattr(f, name)[...]
        self.one = []
        for half in (0, 1):
            self.one += self.pass_on(half, [self.c.a], self.lines(half, True), f.t1s, f.t1r)

    def second(self):
        f = self.f
        for group in self.one:
            group.wait_recv()
        self.two = []
        for half in (0, 1):
            slots = [self.device(-dy, -dx) for dy, dx in [(0, 0)] + self.lines(half, True)]
            self.two += self.pass_on(half, slots, self.lines(half, False), f.t2s, f.t2r)

    def third(self):
        f, c = self.f, self.c
        for group in self.two:
            group.wait_recv()
        self.three = []
        sibling = self.device(0, 0, 1 - self.core)
        for i, name in enumerate(self.names):
            ref = getattr(f, whole_of(name))
            moves = []
            for dy in range(self.Y):
                for dx in range(self.X):
                    piece = ref.at[self.device(dy, dx)]
                    moves.append((piece, piece, {n.ha: sibling}))
            landed = ref.at[pl.ds(0, len(moves))]
            self.three.append(c.group(moves, f.t3s.at[i], f.t3r.at[i], landed))

    def end(self):
        for group in self.three:
            group.wait_recv()


def far_of(name):
    return name + n._hbm


def forward_names(save):
    weights = list(KINDS)
    ins = for_both(*TABLES)
    if save:
        ins += weights[:-1] + [n.nm_old]
    else:
        ins += [n.seg1, n.flat3, n.gnorm] + [old_of(w) for w in weights]
        ins += [moment_of(w) for w in weights]
    kept = for_both(n.joined) + [n.sum_out, n.norms]
    extra = for_both(n.u, n.spec, n.mixed, n.s, n.halo)
    extra += [n.knh, n.knl, n.koh, n.kol, n.g_sq, n.g_fo, n.g_ex]
    if save:
        kept, extra = kept + extra, [n.nm]
    else:
        kept, extra = kept + [n.flat1], extra + weights + [n.zgs, n.zgr]
    scratch = [n.g_nm, n.g_near, n.g_inw, n.g_outw, n.ld]
    scratch += [n.sum_src, n.sum_a, n.sum_z, n.sum_as, n.sum_ar, n.sum_zs, n.sum_zr]
    scratch += [n.g1s, n.g1r, n.p1s, n.p1r, n.t1s, n.t1r, n.t2s, n.t2r, n.t3s, n.t3r, n.hs, n.hr, n.ws, n.wr]
    scratch += extra + for_both(n.maps, n.zh, n.zl, n.act, *SPECTRA)
    return ins, kept, scratch


def forward_far(save):
    return for_both(n.maps) if save else for_both(n.maps, n.halo)


def forward_kernel(bks, A, B, sizes, save, *refs):
    ins, kept, scratch = forward_names(save)
    far = forward_far(save)
    names = ins + [far_of(k) for k in far] + [far_of(k) for k in kept] + kept + scratch
    f = take(names, refs)
    CL, CG, CH, NPd = sizes
    CT = CL + CG
    c = Comm(A, B)
    c.enter()
    keeper = Loader(f.ld)
    for name in far:
        keeper.start(name, getattr(f, far_of(name)), getattr(f, name))
    other = jnp.minimum(c.a, 1)
    once = jnp.where(c.a == 0, 1.0, 2.0)
    cells = [B * bk.H * bk.W for bk in bks]
    freqs = [B * bk.H * (bk.W // 2 + 1) for bk in bks]
    views = [View(f, 0), View(f, 1)]
    both = (0, 1)

    def keep(*which):
        for k in which:
            if k in kept:
                keeper.start(k, getattr(f, k), getattr(f, far_of(k)))

    f.sum_src[...] = jnp.zeros_like(f.sum_src)
    c.entered()
    if not save:
        shares = spread_images(c, f)
        renew_small(f, A, sizes)
    else:
        f.nm[...] = jnp.zeros_like(f.nm)
        f.nm[0:2, :NPd] = f.nm_old[...]
    first = Pair(c, f, n.sq, 0)
    table = gather_direct(c, f, n.nm, 0)
    if save:
        middle = Pair(c, f, n.fo, 1)
        spread = Spread(c, f, (n.ex, n.near, n.inw, n.outw))
        spread.start()
    for q in both:
        bk, g = bks[q], views[q]
        keeper.wait(n.maps + str(q))

        def body(r, carry, bk=bk, g=g):
            src = pl.multiple_of(r * bk.W, bk.W)
            high, low = split(g.maps[pl.ds(src, bk.W), :])
            g.zh[pl.ds(src + bk.W, bk.W), :] = high
            g.zl[pl.ds(src + bk.W, bk.W), :] = low
            return carry

        lax.fori_loop(0, bk.R, body, 0)
    first.second()
    first.end()

    wsq = split(f.g_sq[...].reshape(CH, CG))
    keep(n.g_sq)
    adding = [None, None]
    for q in both:
        bk, g = bks[q], views[q]

        def body(r, carry, bk=bk, g=g):
            at = pl.multiple_of(r + bk.W, 32)
            value = dot3((g.zh[pl.ds(at, bk.MB), CL:], g.zl[pl.ds(at, bk.MB), CL:]), wsq, NT)
            g.s[pl.ds(r, bk.MB), :] = value
            return carry[0] + column_sum(value), carry[1] + column_sum(value * value)

        adding[q] = c.sum_start(f, 0, q, chunks(bk.N, bk.MB, body, no_sums(CH)), not save)
        keep(n.s + str(q))

    table.wait_recv()
    piece = f.g_nm.shape[2]
    span = pad_to(NPd * A, 128) + 128
    norms = None
    for d in range(A):
        part = jnp.concatenate([f.g_nm[d], jnp.zeros((8, span - piece), f32)], 1)
        if d:
            part = pltpu.roll(part, NPd * d, 1)
        norms = part if norms is None else norms + part
    f.norms[0] = norms[:, :CT]
    f.norms[1] = pltpu.roll(norms, span - CT, 1)[:, :CT]
    f.norms[2] = pltpu.roll(norms, span - CT - CH, 1)[:, :CT]

    keep(n.norms)
    for q in both:
        adding[q] = c.sum_cross(f, 0, q, adding[q])
    if not save:
        shares.wait_recv()
        keep(n.flat1)
        renew_large(f, A, B, sizes)
        middle = Pair(c, f, n.fo, 1)
        spread = Spread(c, f, (n.ex, n.near, n.inw, n.outw))
        spread.start()
    swaps = [None, None]
    for q in both:
        bk, g = bks[q], views[q]
        c.sum_end(f, 0, q, adding[q])
        center, inverse = norm_rows(f.sum_out, 0, q, CH, cells[q])

        def source(h, bk=bk, g=g, center=center, inverse=inverse):
            rows = slice(h * bk.W, (h + 1) * bk.W)
            v = (g.s[rows, :] - center) * inverse * f.norms[1, 0:1, :CH] + f.norms[1, 1:2, :CH]
            value = v * sigmoid(v)
            g.act[rows, :] = value
            return value

        row_transform(bk, g.row, source, g.sendA)
        swaps[q] = c.swap_start(g.sendA, g.recvA, f.ws.at[0, q], f.wr.at[0, q], bk.Cp)

    middle.second()
    spread.second()
    c.swap_end(swaps[0])
    middle.end()
    keep(n.g_fo)
    wfo = split(f.g_fo[...].reshape(2 * CH, 2 * CH))
    for q in both:
        bk, g = bks[q], views[q]
        if q:
            c.swap_end(swaps[q])

        def put(slot, value, g=g, bk=bk):
            g.spec[slot * bk.H : (slot + 1) * bk.H, :] = value

        col_transform(bk, g.col, g.col0, other, g.recvA, put)
        keep(n.spec + str(q))

        def body(r, carry, bk=bk, g=g):
            value = dot3(split(g.spec[pl.ds(r, bk.Q // 2), :]), wfo, NT)
            g.mixed[pl.ds(r, bk.Q // 2), :] = value
            return carry[0] + column_sum(value), carry[1] + column_sum(value * value)

        adding[q] = c.sum_start(f, 1, q, chunks(bk.Q, bk.Q // 2, body, no_sums(2 * CH)), False)
        keep(n.mixed + str(q))
    def convolve(q):
        bk, g = bks[q], views[q]
        conv_forward(bk, g.zh, g.zl, f.knh, f.knl, f.koh, f.kol, g.joined)

    def spectra_back(q):
        bk, g = bks[q], views[q]
        c.sum_end(f, 1, q, adding[q])
        center, inverse = norm_rows(f.sum_out, 1, q, 2 * CH, freqs[q])

        def get(slot, g=g, center=center, inverse=inverse, bk=bk):
            value = g.mixed[slot * bk.H : (slot + 1) * bk.H, :]
            v = (value - center) * inverse * f.norms[2, 0:1, : 2 * CH] + f.norms[2, 1:2, : 2 * CH]
            return v * sigmoid(v)

        def scale(b, value):
            return value * (once if b == 0 else 2.0)

        col_back(bk, g.colT, g.col0T, other, get, scale, g.sendB)
        swaps[q] = c.swap_start(g.sendB, g.recvB, f.ws.at[1, q], f.wr.at[1, q], bk.Cp)

    for q in both:
        adding[q] = c.sum_cross(f, 1, q, adding[q])
    halos = []
    if save:
        for q in both:
            bk, g = bks[q], views[q]
            halos += c.halo_start(
                g.maps.at[pl.ds(0, bk.W)],
                g.maps.at[pl.ds(bk.N - bk.W, bk.W)],
                g.halo,
                f.hs.at[q],
                f.hr.at[q],
            )
    spread.third()
    c.halo_end(halos)
    for q in both:
        bk, g = bks[q], views[q]
        if not save:
            keeper.wait(n.halo + str(q))
        for side, at, edge in ((0, 0, 0), (1, bk.N + bk.W, A - 1)):
            if save:
                g.halo[side] = jnp.where(c.a == edge, 0.0, g.halo[side])
            high, low = split(g.halo[side])
            g.zh[pl.ds(at, bk.W), :] = high
            g.zl[pl.ds(at, bk.W), :] = low
        keep(n.halo + str(q))
    spectra_back(0)
    spectra_back(1)
    spread.end()
    keep(n.g_ex)

    def taps(t, carry):
        a, b = t // 3, t % 3
        near = f.g_near[:, pl.ds(t, 1)].reshape(CL, CL)
        inward = f.g_inw[:, pl.ds(t, 1)].reshape(CL, CG)
        high, low = split(jnp.concatenate([near, inward], 1))
        f.knh[b, a] = high
        f.knl[b, a] = low
        return carry

    lax.fori_loop(0, 9, taps, 0)
    for a in range(3):
        for b in range(3):
            high, low = split(f.g_outw[:, 3 * a + b].reshape(CG, CL))
            f.koh[b * CG : (b + 1) * CG, a * CL : (a + 1) * CL] = high
            f.kol[b * CG : (b + 1) * CG, a * CL : (a + 1) * CL] = low
    keep(n.knh, n.knl, n.koh, n.kol)
    convolve(0)
    convolve(1)

    wex = split(f.g_ex[...].reshape(CG, CH))
    for q in both:
        bk, g = bks[q], views[q]
        c.swap_end(swaps[q])
        for h in range(bk.R):
            rows = slice(h * bk.W, (h + 1) * bk.W)
            g.u[rows, :] = g.act[rows, :] + row_back(bk, g.rowT, g.recvB, h)
        keep(n.u + str(q))

        def body(r, carry, bk=bk, g=g):
            rows = pl.ds(r, bk.MB)
            value = g.joined[rows, CL:] + dot3(split(g.u[rows, :]), wex, NT)
            g.joined[rows, CL:] = value
            value = jnp.concatenate([g.joined[rows, :CL], value], 1)
            return carry[0] + column_sum(value), carry[1] + column_sum(value * value)

        adding[q] = c.sum_start(f, 2, q, chunks(bk.N, bk.MB, body, no_sums(CT)))
        keep(n.joined + str(q))
    for q in both:
        adding[q] = c.sum_cross(f, 2, q, adding[q])
    for q in both:
        c.sum_end(f, 2, q, adding[q])
    keep(n.sum_out)
    keeper.wait(*[k for k in keeper.copies if k in kept])
    c.finish()


def renewed(weight, moment, grad):
    return weight - learn_rate * (grad + momentum * (momentum * moment + grad))


def piece_of(flat, A, B, sizes, second, at, count):
    rows = flat_rows_of(A, B, sizes)
    pieces = []
    while count:
        k, off = (2, at) if second else divmod(at, rows[0])
        part = rows[k] // B
        z, off = divmod(off, part)
        take_now = min(count, part - off)
        start = (z * sum(rows) + sum(rows[:k])) // B + off
        pieces.append(flat[start : start + take_now, :])
        at, count = at + take_now, count - take_now
    return jnp.concatenate(pieces, 0) if len(pieces) > 1 else pieces[0]


def unpack(flat, A, B, sizes, second, at, count, tiles):
    unit = pad_to(count, 8)
    return jnp.concatenate(
        [piece_of(flat, A, B, sizes, second, at + t * unit, count) for t in range(tiles)], 1
    )


def unpack_tap(flat, A, B, sizes, k):
    CL, CG, CH, NPd = sizes
    first = flat_plan(A, sizes)[0]
    o, p, tiles = CL // A, CG // A, (CL + CG) // 128
    return (
        unpack(flat, A, B, sizes, False, first[0] + k * pad_to(o, 8) * tiles, o, tiles),
        unpack(flat, A, B, sizes, False, first[1] + k * pad_to(p, 8), p, CL // 128),
    )


def unpack_squeeze(flat, A, sizes):
    CH, CG = sizes[2], sizes[1]
    o = CH // A
    unit = pad_to(o, 8)
    return jnp.concatenate([flat[t * unit : t * unit + o, :] for t in range(CG // 128)], 1)


def unpack_matrices(flat1, flat3, A, B, sizes):
    CL, CG, CH, NPd = sizes
    first = flat_plan(A, sizes)[0]
    return (
        unpack_squeeze(flat3, A, sizes) if flat3 is not None else None,
        unpack(flat1, A, B, sizes, True, 0, 2 * CH // A, 2 * CH // 128),
        unpack(flat1, A, B, sizes, False, first[2], CG // A, pad_to(CH, 128) // 128)[:, :CH],
    )


def spread_images(c, f):
    part = f.seg1.shape[0]
    mine = pl.ds(pl.multiple_of(c.z * part, 8), part)
    f.flat1[mine, :] = f.seg1[...]
    moves = [
        (f.seg1, f.flat1.at[mine], {n.img: lax.rem(c.z + d, c.B)}) for d in range(1, c.B)
    ]
    return c.group(moves, f.zgs.at[0], f.zgr.at[0], f.flat1.at[pl.ds(0, (c.B - 1) * part)])


def renew_small(f, A, sizes):
    f.sq[...] = renewed(f.sq_old[...], f.sq_moment[...], unpack_squeeze(f.flat3, A, sizes))
    P = sizes[3]
    f.nm[...] = jnp.zeros_like(f.nm)
    f.nm[0:2, :P] = renewed(f.nm_old[...], f.nm_moment[...], f.gnorm[0:2, :P])


def renew_large(f, A, B, sizes):
    CL = sizes[0]
    for k in range(9):
        both, out = unpack_tap(f.flat1, A, B, sizes, k)
        f.near[k] = renewed(f.near_old[k], f.near_moment[k], both[:, :CL])
        f.inw[k] = renewed(f.inw_old[k], f.inw_moment[k], both[:, CL:])
        f.outw[k] = renewed(f.outw_old[k], f.outw_moment[k], out)
    sq, fo, ex = unpack_matrices(f.flat1, None, A, B, sizes)
    f.fo[...] = renewed(f.fo_old[...], f.fo_moment[...], fo)
    f.ex[...] = renewed(f.ex_old[...], f.ex_moment[...], ex)


def forward_shapes(bks, A, B, sizes):
    CL, CG, CH, NPd = sizes
    CT = CL + CG
    sd = {n.sum_out: (6, 8, 128), n.norms: (3, 8, CT)}
    sd[n.knh] = sd[n.knl] = (3, 3, CL, CT)
    sd[n.koh] = sd[n.kol] = (3 * CG, 3 * CL)
    for name, shape in (
        (n.sq, (CH // A, CG)),
        (n.fo, (2 * CH // A, 2 * CH)),
        (n.ex, (CG // A, CH)),
        (n.nm, (8, pad_to(NPd, 128))),
        (n.near, (9, CL // A, CL)),
        (n.inw, (9, CL // A, CG)),
        (n.outw, (9, CG // A, CL)),
    ):
        sd[name] = shape
        sd[whole_of(name)] = (A,) + shape
    sd[n.flat1] = (sum(flat_rows_of(A, B, sizes)), 128)
    sd[n.seg1] = (sum(flat_rows_of(A, B, sizes)) // B, 128)
    for q, bk in enumerate(bks):
        here = {
            n.maps: (bk.N, CT),
            n.up: (bk.N, CT),
            n.joined: (bk.N, CT),
            n.u: (bk.N, CH),
            n.spec: (bk.Q, 2 * CH),
            n.mixed: (bk.Q, 2 * CH),
            n.s: (bk.N, CH),
            n.halo: (2, bk.W, CT),
            n.zh: ((bk.R + 2) * bk.W, CT),
            n.zl: ((bk.R + 2) * bk.W, CT),
            n.act: (bk.N, CH),
        }
        for name in SPECTRA:
            here[name] = (2 * CH // 128, A * bk.Cp, 128)
        for name, shape in here.items():
            sd[name + str(q)] = shape
    sd[n.sum_src] = (6, 8, 128)
    sd[n.sum_a] = (6, A, 8, 128)
    sd[n.sum_z] = (6, B, 8, 128)
    return sd


HALF = {n.knh, n.knl, n.koh, n.kol, n.dth, n.dtl, n.zh, n.zl} | set(for_both(n.zh, n.zl, n.dh, n.dl))


def memory(name, sd, sems):
    if name in sems:
        return pltpu.SemaphoreType.DMA(sems[name])
    return pltpu.VMEM(sd[name], bf16 if name in HALF else f32)


def result(name, sd):
    return jax.ShapeDtypeStruct(sd[name], bf16 if name in HALF else f32)


def sum_sems(A, B):
    return {
        n.sum_as: (6,),
        n.sum_ar: (6,),
        n.sum_zs: (6,),
        n.sum_zr: (6,),
        n.hs: (2, 2),
        n.hr: (2, 2),
        n.ws: (2, 2),
        n.wr: (2, 2),
    }


VM = pl.BlockSpec(memory_space=pltpu.VMEM)
FAR = pl.BlockSpec(memory_space=pl.ANY)


def forward_call(bks, A, B, sizes, save, cid, args):
    sd = forward_shapes(bks, A, B, sizes)
    ins, kept, scratch = forward_names(save)
    sems = sum_sems(A, B)
    far = forward_far(save)
    sems[n.ld] = (len(kept) + len(far),)
    sems[n.g1s] = sems[n.g1r] = (1,)
    sems[n.p1s] = sems[n.p1r] = (2, 3)
    for name in (n.t1s, n.t1r, n.t2s, n.t2r):
        sems[name] = (5, 2)
    sems[n.t3s] = sems[n.t3r] = (5,)
    sems[n.zgs] = sems[n.zgr] = (1,)
    results = kept
    macs = sum(bk.N for bk in bks) * 1400000
    res = pl.pallas_call(
        functools.partial(forward_kernel, bks, A, B, sizes, save),
        out_shape=[result(name, sd) for name in results],
        in_specs=[VM] * len(ins) + [FAR] * len(far),
        out_specs=[FAR] * len(kept),
        scratch_shapes=[memory(name, sd, sems) for name in kept + scratch],
        compiler_params=pltpu.CompilerParams(
            collective_id=cid, has_side_effects=True, vmem_limit_bytes=VMEM_LIMIT
        ),
        cost_estimate=pl.CostEstimate(flops=6 * macs, bytes_accessed=40_000_000, transcendentals=0),
        name=n.forward,
    )(*[args[name] for name in ins + far])
    return dict(zip(results, res))


def finish_kernel(counts, A, B, sizes, *refs):
    maps, joined, sums, norms = refs[0:2], refs[2:4], refs[4], refs[5]
    outs = refs[30:32]

    @pl.when(pl.program_id(0) == 0)
    def _():
        update(A, B, sizes, *refs[6:30], *refs[32:])

    for q in (0, 1):
        center, inverse = norm_rows(sums, 2, q, norms.shape[2], counts[q])
        v = (joined[q][...] - center) * inverse * norms[0, 0:1, :] + norms[0, 1:2, :]
        outs[q][...] = maps[q][...] + v * sigmoid(v)


def finish_call(bks, A, B, sizes, maps, fwd, grads, weights, moments, averages):
    N, CT = maps[0].shape
    step = N // 3 if N % 24 == 0 else N
    block = pl.BlockSpec((step, CT), lambda i: (i, 0))
    counts = [B * bk.H * bk.W for bk in bks]
    shapes = [w.shape for w in weights]
    outs = [jax.ShapeDtypeStruct(m.shape, f32) for m in maps]
    outs += [jax.ShapeDtypeStruct(s, f32) for _ in range(3) for s in shapes]
    outs += [jax.ShapeDtypeStruct(s, bf16) for s in shapes]
    res = pl.pallas_call(
        functools.partial(finish_kernel, counts, A, B, sizes),
        out_shape=outs,
        grid=(N // step,),
        in_specs=[block] * 4 + [VM] * 26,
        out_specs=[block] * 2 + [VM] * 28,
        compiler_params=pltpu.CompilerParams(vmem_limit_bytes=VMEM_LIMIT),
        cost_estimate=pl.CostEstimate(
            flops=N * CT * 20, bytes_accessed=N * CT * 24, transcendentals=N * CT * 2
        ),
        name=n.finish,
    )(
        *maps,
        *[fwd[name] for name in (n.joined0, n.joined1, n.sum_out, n.norms)],
        *grads,
        *weights,
        *moments,
        *averages,
    )
    return res[:2], (res[2:9], res[9:16], res[16:23], res[23:30])


def flat_plan(A, sizes):
    CL, CG, CH, NPd = sizes
    CT = CL + CG

    def rows(count, width):
        return pad_to(count // A, 8) * pad_to(width, 128) // 128

    near, outw = 9 * rows(CL, CT), 9 * rows(CG, CL)
    first = (0, near, near + outw)
    return first, near + outw + rows(CG, CH), rows(2 * CH, 2 * CH), rows(CH, CG)


def flat_rows_of(A, B, sizes):
    first, end1, rows2, rows3 = flat_plan(A, sizes)
    half = pad_to(end1, 16 * B) // 2
    return half, half, pad_to(rows2, 8 * B)


LATE = for_both(n.joined, n.up) + for_both(n.maps, n.halo, n.u, n.mixed, n.spec, n.s)
LATE += [n.g_fo, n.knh, n.knl, n.koh, n.kol, n.g_sq]


def backward_names():
    ins = [n.sum_out, n.norms, n.g_ex] + for_both(*TABLES)
    outs = []
    kept = [n.seg1, n.flat3, n.gnorm] + for_both(n.back, n.block)
    scratch = [n.sum_src, n.sum_a, n.sum_z, n.bsum, n.sum_as, n.sum_ar, n.sum_zs, n.sum_zr]
    scratch += [n.hs, n.hr, n.ws, n.wr, n.ld, n.rs1s, n.rs1r, n.rs2s, n.rs2r, n.rs3s, n.rs3r, n.rs5s, n.rs5r]
    scratch += [n.das, n.dar, n.dzs, n.dzr, n.cs, n.cr]
    scratch += [n.dth, n.dtl, n.zh, n.zl, n.gsq, n.gfo]
    scratch += [n.own1, n.sib1, n.far1, n.last1, n.zin1, n.own2, n.sib2, n.far2, n.zin2, n.own3, n.far3, n.zin3]
    scratch += [n.seg1, n.flat3, n.gnorm, n.tot2]
    scratch += for_both(n.dh, n.dl, n.dhalo, n.du, n.dmix, *SPECTRA)
    return ins, outs, kept, scratch


def silu_slope(v):
    sig = sigmoid(v)
    return sig * (1.0 + v * (1.0 - sig))


class Reduce:
    def __init__(self, c, f):
        self.c, self.f = c, f
        self.own, self.sib, self.far, self.last = f.own1, f.sib1, f.far1, f.last1
        self.zin = f.zin1
        self.rows = self.own.shape[1]
        self.nc = c.A // 2
        self.chip, self.core = c.a // 2, c.a % 2
        self.Y, self.X = grid_of(self.nc)
        self.y, self.x = self.chip // self.X, lax.rem(self.chip, self.X)

    def to_sibling(self):
        f, c = self.f, self.c
        other = 1 - self.core
        moves = [
            (self.own.at[2 * cc + other], self.sib.at[cc], {n.ha: 2 * self.chip + other})
            for cc in range(self.nc)
        ]
        self.copies = [c.group(moves, f.rs1s.at[0], f.rs1r.at[0], self.sib.at[pl.ds(0, self.nc)])]

    def device(self, dy, dx):
        y, x = lax.rem(self.y + dy + self.Y, self.Y), lax.rem(self.x + dx + self.X, self.X)
        return 2 * (y * self.X + x) + self.core

    def lines(self, half, first):
        along_x = (half == 0) == first
        return [(0, d) for d in range(1, self.X)] if along_x else [(d, 0) for d in range(1, self.Y)]

    def part(self, half):
        h = self.rows // 2
        return pl.ds(half * h, h)

    def to_lines(self):
        f, c = self.f, self.c
        for copy in self.copies:
            copy.wait_recv()
        for dy in range(self.Y):
            for dx in range(self.X):
                t = self.device(dy, dx)
                self.own[t] = self.own[t] + self.sib[t // 2]
        self.copies = []
        for half in (0, 1):
            rest = [(0, 0)] + self.lines(half, False)
            moves = []
            for k, (dy, dx) in enumerate(self.lines(half, True)):
                for j, (ry, rx) in enumerate(rest):
                    t = self.device(dy + ry, dx + rx)
                    moves.append(
                        (
                            self.own.at[t, self.part(half)],
                            self.far.at[half, k * len(rest) + j],
                            {n.ha: self.device(dy, dx)},
                        )
                    )
            if moves:
                landed = self.far.at[half, pl.ds(0, len(moves))]
                self.copies.append(c.group(moves, f.rs2s.at[half], f.rs2r.at[half], landed))

    def to_owners(self):
        f, c = self.f, self.c
        for copy in self.copies:
            copy.wait_recv()
        self.copies = []
        for half in (1, 0):
            rows = self.part(half)
            rest = [(0, 0)] + self.lines(half, False)
            lines = self.lines(half, True)
            moves = []
            for j, (ry, rx) in enumerate(rest):
                t = self.device(ry, rx)
                total = self.own[t, rows, :]
                for k in range(len(lines)):
                    total = total + self.far[half, k * len(rest) + j]
                self.own[t, rows, :] = total
                if j:
                    moves.append((self.own.at[t, rows], self.last.at[half, j], {n.ha: t}))
            if moves:
                landed = self.last.at[half, pl.ds(1, len(moves))]
                self.copies.append(c.group(moves, f.rs5s.at[half], f.rs5r.at[half], landed))

    def collect(self):
        f, c = self.f, self.c
        for copy in self.copies:
            copy.wait_recv()
        for half in (0, 1):
            rows = self.part(half)
            total = self.own[c.a, rows, :]
            for j in range(1, 1 + len(self.lines(half, False))):
                total = total + self.last[half, j]
            self.own[c.a, rows, :] = total

    def to_images(self, k):
        f, c = self.f, self.c
        return to_images(
            c, self.own.at[c.a, self.part(k)], self.zin.at[k], f.rs3s.at[k], f.rs3r.at[k]
        )


def to_images(c, total, zin, ssem, rsem):
    part = total.shape[0] // c.B
    moves = []
    for d in range(1, c.B):
        zz = lax.rem(c.z + d, c.B)
        piece = total.at[pl.ds(pl.multiple_of(zz * part, 8), part)]
        moves.append((piece, zin.at[d], {n.img: zz}))
    return [c.group(moves, ssem, rsem, zin.at[pl.ds(1, c.B - 1)])] if moves else []


def from_images(c, copies, total, zin, out):
    for copy in copies:
        copy.wait_recv()
    part = total.shape[0] // c.B
    value = total[pl.ds(pl.multiple_of(c.z * part, 8), part), :]
    for d in range(1, c.B):
        value = value + zin[d]
    out[...] = value


class Direct:
    def __init__(self, c, f, own, far):
        self.c, self.f = c, f
        self.own, self.far = own, far

    def start(self):
        c, f = self.c, self.f
        moves = []
        for d in range(1, c.A):
            t = lax.rem(c.a + d, c.A)
            moves.append((self.own.at[t], self.far.at[d], {n.ha: t}))
        landed = self.far.at[pl.ds(1, c.A - 1)]
        self.copies = c.group(moves, f.das.at[0], f.dar.at[0], landed)

    def cross(self, zin):
        c, f = self.c, self.f
        self.copies.wait_recv()
        total = self.own[c.a]
        for d in range(1, c.A):
            total = total + self.far[d]
        zin[c.z] = total
        mine = zin.at[c.z]
        moves = [(mine, mine, {n.img: lax.rem(c.z + d, c.B)}) for d in range(1, c.B)]
        self.copies = []
        if moves:
            landed = zin.at[pl.ds(0, c.B - 1)]
            self.copies = [c.group(moves, f.dzs.at[0], f.dzr.at[0], landed)]

    def end(self, zin, out):
        for copy in self.copies:
            copy.wait_recv()
        total = zin[0]
        for d in range(1, self.c.B):
            total = total + zin[d]
        out[...] = total


class Chips:
    def __init__(self, c, f, own, sib, far):
        self.c, self.f = c, f
        self.own, self.sib, self.far = own, sib, far
        self.nc = c.A // 2
        self.chip, self.core = c.a // 2, c.a % 2

    def to_sibling(self):
        f, c = self.f, self.c
        other = 1 - self.core
        moves = [
            (self.own.at[2 * cc + other], self.sib.at[cc], {n.ha: 2 * self.chip + other})
            for cc in range(self.nc)
        ]
        self.copies = c.group(moves, f.cs.at[0], f.cr.at[0], self.sib.at[pl.ds(0, self.nc)])

    def start(self):
        f, c = self.f, self.c
        self.copies.wait_recv()
        moves = []
        for d in range(self.nc):
            cc = lax.rem(self.chip + d, self.nc)
            t = 2 * cc + self.core
            self.own[t] = self.own[t] + self.sib[cc]
            if d:
                moves.append((self.own.at[t], self.far.at[d], {n.ha: t}))
        self.copies = c.group(moves, f.cs.at[1], f.cr.at[1], self.far.at[pl.ds(1, self.nc - 1)])

    def owned(self):
        self.copies.wait_recv()
        total = self.own[self.c.a]
        for d in range(1, self.nc):
            total = total + self.far[d]
        return total


def backward_kernel(bks, A, B, sizes, *refs):
    ins, outs, kept, scratch = backward_names()
    near = ins + [far_of(name) for name in LATE] + [far_of(name) for name in kept]
    f = take(near + LATE + scratch, refs)
    CL, CG, CH, NPd = sizes
    CT = CL + CG
    c = Comm(A, B)
    c.enter()
    loader = Loader(f.ld)

    def load(names):
        for name in names:
            loader.start(name, getattr(f, far_of(name)), getattr(f, name))

    load(LATE[:4])
    other = jnp.minimum(c.a, 1)
    once = jnp.where(c.a == 0, 1.0, 2.0)
    cells = [B * bk.H * bk.W for bk in bks]
    freqs = [B * bk.H * (bk.W // 2 + 1) for bk in bks]
    views = [View(f, 0), View(f, 1)]
    both = (0, 1)
    sums = take(
        (n.sum_src, n.sum_a, n.sum_z, n.sum_as, n.sum_ar, n.sum_zs, n.sum_zr, n.sum_out),
        (f.sum_src, f.sum_a, f.sum_z, f.sum_as, f.sum_ar, f.sum_zs, f.sum_zr, f.bsum),
    )
    f.sum_src[...] = jnp.zeros_like(f.sum_src)
    adding, swaps = [None, None], [None, None]

    for q in both:
        bk, g = bks[q], views[q]
        center, inverse = norm_rows(f.sum_out, 2, q, CT, cells[q])
        loader.wait(n.joined + str(q), n.up + str(q))

        def body(r, carry, g=g, center=center, inverse=inverse):
            rows = pl.ds(r, 32)
            x = (g.joined[rows, :] - center) * inverse
            dy = g.up[rows, :] * silu_slope(x * f.norms[0, 0:1, :] + f.norms[0, 1:2, :])
            g.up[rows, :] = dy
            return carry[0] + column_sum(dy), carry[1] + column_sum(dy * x)

        total = chunks(bk.N, 32, body, no_sums(CT))
        if q == 0:
            load(LATE[4:])
            c.entered()
        adding[q] = c.sum_start(sums, 0, q, total)
    for q in both:
        adding[q] = c.sum_cross(sums, 0, q, adding[q])

    wex = split(f.g_ex[...].reshape(CG, CH))
    halos = []
    for q in both:
        bk, g = bks[q], views[q]
        c.sum_end(sums, 0, q, adding[q])
        center, inverse = norm_rows(f.sum_out, 2, q, CT, cells[q])
        gain = f.norms[0, 0:1, :] * inverse
        m1, m2 = (value * (1.0 / cells[q]) for value in totals(f.bsum, 0, q, CT))
        loader.wait(n.maps + str(q))

        def body(r, carry, bk=bk, g=g, center=center, inverse=inverse, gain=gain, m1=m1, m2=m2):
            rows = pl.ds(r, 32)
            x = (g.joined[rows, :] - center) * inverse
            dz = gain * (g.up[rows, :] - m1 - x * m2)
            g.up[rows, :] = dz
            high, low = split(dz)
            at = pl.ds(pl.multiple_of(r + bk.W, 32), 32)
            g.dh[at, :] = high
            g.dl[at, :] = low
            v = x * f.norms[0, 0:1, :] + f.norms[0, 1:2, :]
            g.joined[rows, :] = g.maps[rows, :] + v * sigmoid(v)
            return carry

        chunks(bk.N, 32, body, 0)
        name = n.block + str(q)
        loader.start(name, g.joined, getattr(f, far_of(name)))
        halos += c.halo_start(
            g.up.at[pl.ds(0, bk.W)],
            g.up.at[pl.ds(bk.N - bk.W, bk.W)],
            g.dhalo,
            f.hs.at[q],
            f.hr.at[q],
        )

        def body2(r, carry, bk=bk, g=g):
            at = pl.ds(pl.multiple_of(r + bk.W, 32), bk.MB)
            g.du[pl.ds(r, bk.MB), :] = dot3((g.dh[at, CL:], g.dl[at, CL:]), wex, NN)
            return carry

        chunks(bk.N, bk.MB, body2, 0)
        row_transform(bk, g.row, lambda h, g=g, bk=bk: g.du[h * bk.W : (h + 1) * bk.W, :], g.sendA)
        swaps[q] = c.swap_start(g.sendA, g.recvA, f.ws.at[0, q], f.wr.at[0, q], bk.Cp)

    first, end1, rows2, rows3 = flat_plan(A, sizes)
    units = (pad_to(CL // A, 8) * (CT // 128), pad_to(CG // A, 8))

    def pack(own, at, value, more):
        rows = value.shape[0] // A
        for t in range(A):
            for k in range(value.shape[1] // 128):
                piece = value[t * rows : (t + 1) * rows, 128 * k : 128 * (k + 1)]
                to = pl.ds(at + k * pad_to(rows, 8), rows)
                own[t, to, :] = own[t, to, :] + piece if more else piece

    def kernel_gradients(q):
        bk, g = bks[q], views[q]
        step = min(bk.N, 384)
        col = lax.broadcasted_iota(jnp.int32, (step, 1), 0) % bk.W
        for i in range(bk.N // step):
            for t in range(CT // 128):
                value = g.up[i * step : (i + 1) * step, 128 * t : 128 * (t + 1)]
                moved = (
                    jnp.where(col == bk.W - 1, 0.0, pltpu.roll(value, step - 1, 0)),
                    value,
                    jnp.where(col == 0, 0.0, pltpu.roll(value, 1, 0)),
                )
                for b in range(3):
                    high, low = split(jnp.transpose(moved[b]))
                    at = b * CL if t == 0 else 3 * CL + b * CG + 128 * (t - 1)
                    f.dth[at : at + 128, i * step : (i + 1) * step] = high
                    f.dtl[at : at + 128, i * step : (i + 1) * step] = low
        loader.wait(n.maps + str(q), n.halo + str(q), n.u + str(q))

        def body(r, carry):
            src = pl.multiple_of(r * bk.W, bk.W)
            high, low = split(g.maps[pl.ds(src, bk.W), :])
            f.zh[pl.ds(src + bk.W, bk.W), :] = high
            f.zl[pl.ds(src + bk.W, bk.W), :] = low
            return carry

        lax.fori_loop(0, bk.R, body, 0)
        for side, at in ((0, 0), (1, bk.N + bk.W)):
            high, low = split(g.halo[side])
            f.zh[pl.ds(at, bk.W), :] = high
            f.zl[pl.ds(at, bk.W), :] = low

        def taps(a, carry):
            rows = pl.ds(pl.multiple_of(a * bk.W, 32), bk.N)
            right = (f.zh[rows, :], f.zl[rows, :])
            out = dot3((f.dth[: 3 * CL, :], f.dtl[: 3 * CL, :]), right, NN)
            for b in range(3):
                at = pl.multiple_of(first[0] + (3 * a + b) * units[0], 8)
                pack(f.own1, at, out[b * CL : (b + 1) * CL], q)
            return carry

        lax.fori_loop(0, 3, taps, 0)
        right = tuple(
            jnp.concatenate([z[a * bk.W : a * bk.W + bk.N, :CL] for a in range(3)], 1)
            for z in (f.zh, f.zl)
        )
        for b in range(3):
            at = 3 * CL + b * CG
            value = dot3((f.dth[at : at + CG, :], f.dtl[at : at + CG, :]), right, NN)
            for a in range(3):
                piece = value[:, a * CL : (a + 1) * CL]
                pack(f.own1, first[1] + (3 * a + b) * units[1], piece, q)
        at = 3 * CL + CG
        value = dot3((f.dth[at : at + CG, :], f.dtl[at : at + CG, :]), split(g.u[...]), NN)
        value = jnp.concatenate([value, jnp.zeros((CG, pad_to(CH, 128) - CH), f32)], 1)
        pack(f.own1, first[2], value, q)

    def spectra_slopes(q):
        bk, g = bks[q], views[q]
        loader.wait(n.mixed + str(q))
        c.swap_end(swaps[q])
        center, inverse = norm_rows(f.sum_out, 1, q, 2 * CH, freqs[q])
        carry = [no_sums(2 * CH)]

        def put(slot, value):
            rows = slice(slot * bk.H, (slot + 1) * bk.H)
            x = (g.mixed[rows, :] - center) * inverse
            value = value * (once if slot in (0, bk.nb) else 2.0)
            dy = value * silu_slope(x * f.norms[2, 0:1, : 2 * CH] + f.norms[2, 1:2, : 2 * CH])
            g.dmix[rows, :] = dy
            carry[0] = (carry[0][0] + column_sum(dy), carry[0][1] + column_sum(dy * x))

        col_transform(bk, g.col, g.col0, other, g.recvA, put)
        adding[q] = c.sum_start(sums, 1, q, carry[0])

    def spectra_back(q, wfo):
        bk, g = bks[q], views[q]
        c.sum_end(sums, 1, q, adding[q])
        center, inverse = norm_rows(f.sum_out, 1, q, 2 * CH, freqs[q])
        gain = f.norms[2, 0:1, : 2 * CH] * inverse
        m1, m2 = (value * (1.0 / freqs[q]) for value in totals(f.bsum, 1, q, 2 * CH))

        def get(slot):
            rows = slice(slot * bk.H, (slot + 1) * bk.H)
            x = (g.mixed[rows, :] - center) * inverse
            dz = gain * (g.dmix[rows, :] - m1 - x * m2)
            g.dmix[rows, :] = dz
            return dot3(split(dz), wfo, NN)

        col_back(bk, g.colT, g.col0T, other, get, lambda b, v: v, g.sendB)
        swaps[q] = c.swap_start(g.sendB, g.recvB, f.ws.at[1, q], f.wr.at[1, q], bk.Cp)

    kernel_gradients(0)
    spectra_slopes(0)
    kernel_gradients(1)
    adding[0] = c.sum_cross(sums, 1, 0, adding[0])
    if f.own1.shape[1] > end1:
        f.own1[:, end1:, :] = jnp.zeros((A, f.own1.shape[1] - end1, 128), f32)
    red1 = Reduce(c, f)
    red1.to_sibling()
    spectra_slopes(1)
    loader.wait(n.g_fo)
    wfo = split(f.g_fo[...].reshape(2 * CH, 2 * CH))
    adding[1] = c.sum_cross(sums, 1, 1, adding[1])
    red1.to_lines()
    spectra_back(0, wfo)
    spectra_back(1, wfo)
    for q in both:
        bk, g = bks[q], views[q]
        loader.wait(n.spec + str(q))
        value = dot3(split(jnp.transpose(g.dmix[...])), split(g.spec[...]), NN)
        f.gfo[...] = value if q == 0 else f.gfo[...] + value
    pack(f.own2, 0, f.gfo, 0)
    red2 = Chips(c, f, f.own2, f.sib2, f.far2)
    red2.to_sibling()

    c.halo_end(halos)
    c.halo_sent()
    loader.wait(n.knh, n.knl, n.koh, n.kol)

    def input_gradients(q):
        bk, g = bks[q], views[q]
        for side, at, edge in ((0, 0, 0), (1, bk.N + bk.W, A - 1)):
            high, low = split(jnp.where(c.a == edge, 0.0, g.dhalo[side]))
            g.dh[pl.ds(at, bk.W), :] = high
            g.dl[pl.ds(at, bk.W), :] = low
        conv_backward(bk, g.dh, g.dl, f.knh, f.knl, f.koh, f.kol, g.up)

    def active_slopes(q):
        bk, g = bks[q], views[q]
        loader.wait(n.s + str(q))
        c.swap_end(swaps[q])
        center, inverse = norm_rows(f.sum_out, 0, q, CH, cells[q])
        total = no_sums(CH)
        for h in range(bk.R):
            rows = slice(h * bk.W, (h + 1) * bk.W)
            x = (g.s[rows, :] - center) * inverse
            value = g.du[rows, :] + row_back(bk, g.rowT, g.recvB, h)
            dy = value * silu_slope(x * f.norms[1, 0:1, :CH] + f.norms[1, 1:2, :CH])
            g.du[rows, :] = dy
            total = (total[0] + column_sum(dy), total[1] + column_sum(dy * x))
        adding[q] = c.sum_start(sums, 2, q, total, False)

    def squeeze_back(q, wsq):
        bk, g = bks[q], views[q]
        c.sum_end(sums, 2, q, adding[q])
        center, inverse = norm_rows(f.sum_out, 0, q, CH, cells[q])
        gain = f.norms[1, 0:1, :CH] * inverse
        m1, m2 = (value * (1.0 / cells[q]) for value in totals(f.bsum, 2, q, CH))
        loader.wait(n.again + str(q))

        def body(r, carry):
            rows = pl.ds(r, bk.MB)
            x = (g.s[rows, :] - center) * inverse
            dz = gain * (g.du[rows, :] - m1 - x * m2)
            g.du[rows, :] = dz
            g.up[rows, :CL] += g.joined[rows, :CL]
            g.up[rows, CL:] += g.joined[rows, CL:] + dot3(split(dz), wsq, NN)
            return carry

        chunks(bk.N, bk.MB, body, 0)
        value = dot3(split(jnp.transpose(g.du[...])), split(g.maps[:, CL:]), NN)
        f.gsq[...] = value if q == 0 else f.gsq[...] + value

    for q in both:
        loader.wait(n.block + str(q))
        loader.start(n.again + str(q), getattr(f, far_of(n.up + str(q))), views[q].joined)
    input_gradients(0)
    red1.to_owners()
    input_gradients(1)
    active_slopes(0)
    active_slopes(1)
    red1.collect()
    images = [red1.to_images(0), red1.to_images(1)]
    loader.wait(n.g_sq)
    wsq = split(f.g_sq[...].reshape(CH, CG))
    for q in both:
        adding[q] = c.sum_cross(sums, 2, q, adding[q])
    red2.start()
    squeeze_back(0, wsq)
    squeeze_back(1, wsq)
    for q in both:
        name = n.back + str(q)
        loader.start(name, views[q].up, getattr(f, far_of(name)))
    pack(f.own3, 0, f.gsq, 0)
    red3 = Direct(c, f, f.own3, f.far3)
    red3.start()
    f.tot2[: f.own2.shape[1], :] = red2.owned()
    if f.tot2.shape[0] > f.own2.shape[1]:
        f.tot2[f.own2.shape[1] :, :] = jnp.zeros((f.tot2.shape[0] - f.own2.shape[1], 128), f32)
    images.append(to_images(c, f.tot2, f.zin2, f.rs3s.at[2], f.rs3r.at[2]))

    span = pad_to(NPd * A, 128) + 128
    lane = lax.broadcasted_iota(jnp.int32, (8, span), 1)
    out = []
    for i in (1, 0):
        rows = []
        for k, width in ((0, CT), (1, 2 * CH), (2, CH)):
            pair = [totals(f.bsum, k, q, CT)[i] for q in both]
            row = jnp.concatenate([pair[0] + pair[1], jnp.zeros((1, span - CT), f32)], 1)
            rows.append(jnp.where(lane < width, jnp.broadcast_to(row, (8, span)), 0.0))
        out.append(rows[0] + pltpu.roll(rows[2], CT, 1) + pltpu.roll(rows[1], CT + CH, 1))
    sub = lax.broadcasted_iota(jnp.int32, (8, span), 0)
    value = pltpu.roll(jnp.where(sub == 0, out[0], out[1]), lax.rem(span - NPd * c.a, span), 1)
    f.gnorm[...] = value[:, : f.gnorm.shape[1]]

    def keep(name):
        loader.start(name, getattr(f, name), getattr(f, far_of(name)))

    keep(n.gnorm)
    red3.cross(f.zin3)
    at = 0
    for k, (total, zin) in enumerate(
        (
            (f.own1.at[c.a, red1.part(0)], f.zin1.at[0]),
            (f.own1.at[c.a, red1.part(1)], f.zin1.at[1]),
            (f.tot2, f.zin2),
        )
    ):
        from_images(c, images[k], total, zin, f.seg1.at[pl.ds(at, zin.shape[1])])
        at += zin.shape[1]
    keep(n.seg1)
    red3.end(f.zin3, f.flat3)
    keep(n.flat3)
    loader.wait(*kept)
    c.finish()


def conv_backward(bk, dh, dl, knh, knl, koh, kol, out):
    MB, W = bk.MB, bk.W
    CL = knh.shape[2]
    CG = koh.shape[0] // 3
    CT = knh.shape[3]
    col = lax.broadcasted_iota(jnp.int32, (MB, 1), 0) % W

    def moved(value, b):
        if b == 0:
            return jnp.where(col == W - 1, 0.0, pltpu.roll(value, MB - 1, 0))
        if b == 2:
            return jnp.where(col == 0, 0.0, pltpu.roll(value, 1, 0))
        return value

    def body(i, carry):
        r = pl.multiple_of(i * MB, 32)
        rows = [pl.ds(pl.multiple_of(r + (2 - a) * W, 32), MB) for a in range(3)]
        left = tuple(jnp.concatenate([d[rows[a], :CL] for a in range(3)], 1) for d in (dh, dl))
        total = None
        for b in (1, 0, 2):
            right = (knh[b].reshape(3 * CL, CT), knl[b].reshape(3 * CL, CT))
            value = moved(dot3(left, right, NN), b)
            total = value if total is None else total + value
        out[pl.ds(r, MB), :] = total
        cross = None
        for a in range(3):
            left2 = (dh[rows[a], CL:], dl[rows[a], CL:])
            right = tuple(
                jnp.concatenate(
                    [k[b * CG : (b + 1) * CG, a * CL : (a + 1) * CL] for b in range(3)], 1
                )
                for k in (koh, kol)
            )
            value = dot3(left2, right, NN)
            cross = value if cross is None else cross + value
        total = None
        for b in range(3):
            value = moved(cross[:, b * CL : (b + 1) * CL], b)
            total = value if total is None else total + value
        out[pl.ds(r, MB), :CL] += total
        return carry

    lax.fori_loop(0, bk.N // MB, body, 0)


def backward_call(bks, A, B, sizes, cid, args):
    CL, CG, CH, NPd = sizes
    CT = CL + CG
    nc = A // 2
    first, end1, rows2, rows3 = flat_plan(A, sizes)
    half1, _, padded2 = flat_rows_of(A, B, sizes)
    rows1 = 2 * half1
    N = max(bk.N for bk in bks)
    big = max((bk.R + 2) * bk.W for bk in bks)
    sd = forward_shapes(bks, A, B, sizes)
    sd[n.bsum] = sd[n.sum_src]
    sd[n.gnorm] = (8, pad_to(NPd, 128))
    sd[n.dth] = sd[n.dtl] = (3 * CT, N)
    sd[n.zh] = sd[n.zl] = (big, CT)
    sd[n.gsq], sd[n.gfo] = (CH, CG), (2 * CH, 2 * CH)
    sd[n.own1], sd[n.zin1] = (A, rows1, 128), (2, B, half1 // B, 128)
    sd[n.sib1] = (nc, rows1, 128)
    sd[n.far1] = (2, nc, rows1 // 2, 128)
    sd[n.last1] = (2, max(grid_of(nc)), rows1 // 2, 128)
    sd[n.tot2], sd[n.zin2] = (padded2, 128), (B, padded2 // B, 128)
    sd[n.own2] = (A, rows2, 128)
    sd[n.sib2] = sd[n.far2] = (nc, rows2, 128)
    sd[n.flat3], sd[n.zin3] = (rows3, 128), (B, rows3, 128)
    sd[n.own3] = sd[n.far3] = (A, rows3, 128)
    for q, bk in enumerate(bks):
        here = {
            n.back: (bk.N, CT),
            n.block: (bk.N, CT),
            n.dh: ((bk.R + 2) * bk.W, CT),
            n.dl: ((bk.R + 2) * bk.W, CT),
            n.dhalo: (2, bk.W, CT),
            n.du: (bk.N, CH),
            n.dmix: (bk.Q, 2 * CH),
        }
        for name, shape in here.items():
            sd[name + str(q)] = shape
    ins, outs, kept, scratch = backward_names()
    results = outs + kept
    sems = sum_sems(A, B)
    sems[n.ld] = (len(LATE) + len(kept) + 2,)
    for name in (n.rs1s, n.rs1r, n.das, n.dar, n.dzs, n.dzr):
        sems[name] = (1,)
    sems[n.rs3s] = sems[n.rs3r] = (3,)
    for name in (n.rs2s, n.rs2r, n.rs5s, n.rs5r, n.cs, n.cr):
        sems[name] = (2,)
    macs = sum(bk.N for bk in bks) * 2800000
    res = pl.pallas_call(
        functools.partial(backward_kernel, bks, A, B, sizes),
        out_shape=[result(name, sd) for name in results],
        in_specs=[VM] * len(ins) + [FAR] * len(LATE),
        out_specs=[VM] * len(outs) + [FAR] * len(kept),
        scratch_shapes=[memory(name, sd, sems) for name in LATE + scratch],
        compiler_params=pltpu.CompilerParams(
            collective_id=cid, has_side_effects=True, vmem_limit_bytes=VMEM_LIMIT
        ),
        cost_estimate=pl.CostEstimate(flops=6 * macs, bytes_accessed=40_000_000, transcendentals=0),
        name=n.backward,
    )(*[args[name] for name in ins + LATE])
    return dict(zip(results, res))


def update(A, B, sizes, *refs):
    CL, CG, CH, NPd = sizes
    flat1, flat3, gnorm = refs[:3]
    weights, moments, averages = refs[3:10], refs[10:17], refs[17:24]
    updated, velocity, smoothed, half = refs[24:31], refs[31:38], refs[38:45], refs[45:52]
    decay = min(0.5, (1.0 + STEP) / (10.0 + STEP))

    def step(i, at, grad):
        new = renewed(weights[i][at], moments[i][at], grad)
        velocity[i][at] = momentum * moments[i][at] + grad
        updated[i][at] = new
        smoothed[i][at] = decay * averages[i][at] + (1.0 - decay) * new
        half[i][at] = new.astype(bf16)

    for k in range(9):
        both, out = unpack_tap(flat1, A, B, sizes, k)
        step(0, k, both[:, :CL])
        step(1, k, both[:, CL:])
        step(2, k, out)
    every = slice(None)
    for i, grad in zip((3, 4, 5), unpack_matrices(flat1, flat3, A, B, sizes)):
        step(i, every, grad)
    step(6, every, gnorm[0:2, :NPd])


def as_rows(weight):
    return jnp.transpose(weight[0], (0, 1, 3, 2)).reshape(9, weight.shape[4], weight.shape[3])


def from_rows(value):
    return jnp.transpose(value.reshape(1, 3, 3, value.shape[1], value.shape[2]), (0, 1, 2, 4, 3))


def flat_rows(weight):
    return jnp.transpose(weight[0])


def from_flat(value):
    return jnp.transpose(value)[None]


def per_device(*arrays):
    A, B = lax.axis_size("ha"), lax.axis_size("img")
    maps, ups = arrays[0:2], arrays[2:4]
    groups = [arrays[4 + i :: 3] for i in range(3)]
    to_local = (as_rows,) * 3 + (flat_rows,) * 3 + (lambda w: w[0],)
    weights, moments, averages = (
        [change(w) for change, w in zip(to_local, group)] for group in groups
    )
    bks = [Bucket(m.shape[1], m.shape[2], A) for m in maps]
    CL, CG, CH, NPd = weights[0].shape[2], weights[1].shape[2], weights[5].shape[1], weights[6].shape[1]
    sizes = (CL, CG, CH, NPd)
    CT = CL + CG
    args = {}
    for q in (0, 1):
        args[n.maps + str(q)] = maps[q].reshape(-1, CT)
        args[n.up + str(q)] = ups[q].reshape(-1, CT)
        for name, table in zip(TABLES, tables_of(bks[q])):
            args[name + str(q)] = jnp.asarray(table)
    flat_maps = [args[n.maps0], args[n.maps1]]
    args.update(zip(KINDS, weights))
    args[old_of(n.nm)] = weights[6]
    fwd = forward_call(bks, A, B, sizes, True, 1, args)
    bwd = backward_call(bks, A, B, sizes, 2, {**args, **fwd})
    block = [bwd[n.block0], bwd[n.block1]]
    back = [bwd[n.back0], bwd[n.back1]]
    again = {**args, **bwd, n.halo0: fwd[n.halo0], n.halo1: fwd[n.halo1]}
    for name, weight, moment in zip(KINDS, weights, moments):
        again[old_of(name)] = weight
        again[moment_of(name)] = moment
    fresh = forward_call(bks, A, B, sizes, False, 3, again)
    grads = (fresh[n.flat1], bwd[n.flat3], bwd[n.gnorm])
    rerun, groups = finish_call(
        bks, A, B, sizes, flat_maps, fresh, grads, weights, moments, averages
    )
    out = []
    for pair in (block, back, rerun):
        out += [value.reshape(m.shape) for value, m in zip(pair, maps)]
    to_outer = (from_rows,) * 3 + (from_flat,) * 3 + (lambda w: w[None],)
    for i in range(7):
        out += [to_outer[i](group[i]) for group in groups]
    return tuple(out)


def solution(mesh):
    cells = P("img", "ha", None, None)
    kernel = P(None, None, None, None, "ha")
    matrix = P(None, None, "ha")
    return jax.shard_map(
        per_device,
        mesh=mesh,
        in_specs=(cells,) * 4 + (kernel,) * 9 + (matrix,) * 12,
        out_specs=(cells,) * 6 + (kernel,) * 12 + (matrix,) * 16,
        check_vma=False,
    )
```
